32 devices in a mesh: mem: 16 (over z, x, core), lat: 2 (over y).
Axes of the slice: x: 2, y: 2, z: 4, core: 2. Of those that a mesh axis runs over, the one named last changes fastest.
Arguments:
- background: float32 [128, 128, 2, 256], P('lat', 'mem'), may hold values from -16 to 16, as said below
- wind_east: bfloat16 [128, 256], P('lat'), may hold values from -0.8984375 to 0.8984375
- wind_north: bfloat16 [128, 256], P('lat'), may hold values from -0.8984375 to 0.8984375
- obs_index: int32 [2, 64, 1, 128], P('lat', 'mem'), may hold values from 0 to 511
- obs_value: float32 [2, 64, 1, 128], P('lat', 'mem'), may hold values from -4 to 4
- obs_scale: float32 [2, 64, 1, 128], P('lat', 'mem'), may hold values from 1 to 8
Outputs:
- analysis: float32 [128, 128, 2, 256], P('lat', 'mem')
The draws below stay inside these ranges and needn't reach their ends.
Inputs may be any that keep to these rules, and one draw needn't show every extreme that they name: `background`: Members' states.
All inputs are finite; a program needn't handle non-finite values.
Results may differ from the reference program's by a relative error of at most 0.0043.
Values may be sent and summed in bfloat16 or wider, within the bound.
No kernel may reach another device: no remote copies, remote signals or barrier semaphores. Data moves between devices by JAX's collectives and lax.ppermute only.
A program may use at most 64 MiB of HBM per device.

```python
import math
import jax
import jax.numpy as jnp
from jax import lax

REALIZATION_TOTAL = 128
QUANTITY_TOTAL = 2
MERIDIAN_POINTS = 256
PW = 256
NOBS = 128
ROWS_DEV = 64
STEPS = 4
ITERS = 12
PARALLEL_LINES = 128
BANDS = 2
NPR = 1


def draw_background(key, part):
    key_base = jax.random.fold_in(key, 11)
    key_scale = jax.random.fold_in(key, 12)
    key_noise = jax.random.fold_in(key, 13)
    base = jnp.clip(jax.random.normal(key_base, (PARALLEL_LINES, 1, QUANTITY_TOTAL, MERIDIAN_POINTS), jnp.float32), -4.0, 4.0)
    spread = jnp.exp(jax.random.uniform(key_scale, (1, REALIZATION_TOTAL, 1, 1), jnp.float32, math.log(0.1), math.log(3.0)))
    noise = jnp.clip(jax.random.normal(key_noise, (PARALLEL_LINES, REALIZATION_TOTAL, QUANTITY_TOTAL, MERIDIAN_POINTS), jnp.float32), -4.0, 4.0)
    return base + spread * noise


def plant(entries, own_key, low, high):
    shape = entries.shape
    spot = [jax.random.randint(jax.random.fold_in(own_key, axis), (), 0, shape[axis]) for axis in range(len(shape))]
    entries = entries.at[tuple(spot)].set(low)
    longest = shape.index(max(shape))
    spot[longest] = (spot[longest] + 1) % shape[longest]
    return entries.at[tuple(spot)].set(high)


def shard_levels(own_key, shape, cuts, smallest, top_value):
    def one(position, shards_of):
        steps = jax.random.uniform(jax.random.fold_in(jax.random.fold_in(own_key, 6), position), (shards_of,), jnp.float32, smallest / len(cuts), top_value / len(cuts))
        return jnp.repeat(jnp.exp(steps), shape[position] // shards_of).reshape((-1,) + (1,) * (len(shape) - position - 1))

    loudness = one(*cuts[0])
    for cut in cuts[1:]:
        loudness = loudness * one(*cut)
    return loudness


def gaussian(key, shape, deviation, limit, split=(), held_as=jnp.bfloat16):
    factor_of = shard_levels(key, shape, split, -0.22, 0.18) if split else 1.0
    drawn = jax.random.normal(key, shape, jnp.float32) * deviation * factor_of
    return jnp.minimum(jnp.maximum(drawn, -limit), limit).astype(held_as)


def setup_inputs(seed: int = 0) -> dict:
    keys = jax.random.split(jax.random.key(seed), 7)
    background = draw_background(jax.random.fold_in(keys[6], 71), 0)
    wind_east = jnp.clip(jax.random.uniform(keys[1], (PARALLEL_LINES, MERIDIAN_POINTS), jnp.float32, -0.8984375, 0.8984375) * shard_levels(keys[1], (PARALLEL_LINES, MERIDIAN_POINTS), ((0, 2),), -0.4, 0.0), -0.8984375, 0.8984375).astype(jnp.bfloat16)
    wind_north = jnp.clip(jax.random.uniform(keys[2], (PARALLEL_LINES, MERIDIAN_POINTS), jnp.float32, -0.8984375, 0.8984375) * shard_levels(keys[2], (PARALLEL_LINES, MERIDIAN_POINTS), ((0, 2),), -0.4, 0.0), -0.8984375, 0.8984375).astype(jnp.bfloat16)
    obs_index = plant(jax.random.randint(keys[3], (BANDS, ROWS_DEV, NPR, NOBS), 0, QUANTITY_TOTAL * PW), jax.random.fold_in(keys[3], 1), 0, (QUANTITY_TOTAL * PW) - 1).astype(jnp.int32)
    obs_value = gaussian(keys[4], (BANDS, ROWS_DEV, NPR, NOBS), 1.0, 4.0, ((0, 2), (1, 16)), jnp.float32)
    obs_scale = jnp.clip(jnp.exp(math.log(8.0) - 2.0794415 * jax.random.uniform(keys[5], (BANDS, ROWS_DEV, NPR, NOBS), jnp.float32) ** shard_levels(keys[5], (BANDS, ROWS_DEV, NPR, NOBS), ((0, 2), (1, 16)), -0.2, 0.2)), 1.0, 8.0)
    return {"background": background, "wind_east": wind_east, "wind_north": wind_north, "obs_index": obs_index, "obs_value": obs_value, "obs_scale": obs_scale}


HIGHEST = lax.Precision.HIGHEST

def tendency(padded, circumpolar_wind_speed, poleward_wind_speed):
    center_rows = padded[1:-1]
    along_diff = jnp.roll(center_rows, -1, axis=-1) - jnp.roll(center_rows, 1, axis=-1)
    across_diff = padded[2:] - padded[:-2]
    return -0.5 * (circumpolar_wind_speed * along_diff + poleward_wind_speed * across_diff)

def predicted_realization(sample_realization, circumpolar_wind_speed, poleward_wind_speed):

    def slope(values):
        padded = jnp.pad(values, ((1, 1), (0, 0), (0, 0)))
        return tendency(padded, circumpolar_wind_speed, poleward_wind_speed)
    current = sample_realization
    for step_index in range(STEPS):
        slope_one = slope(current)
        slope_two = slope(current + 0.5 * slope_one)
        slope_three = slope(current + 0.5 * slope_two)
        slope_four = slope(current + slope_three)
        current = current + (slope_one + 2.0 * slope_two + 2.0 * slope_three + slope_four) / 6.0
    return current

def make_blocks(row_state, index_row, value_row, scale_row):
    offsets = jnp.arange(NPR, dtype=jnp.int32)[:, None] * PW
    columns = index_row // PW * MERIDIAN_POINTS + offsets + index_row % PW
    picked = jnp.take(row_state, columns.reshape(-1).astype(jnp.int32), axis=1).reshape(REALIZATION_TOTAL, NPR, NOBS)
    average = lax.optimization_barrier(jnp.mean(picked, axis=0))
    spread = (picked - average) * scale_row / math.sqrt(REALIZATION_TOTAL - 1)
    innovation = (value_row - average) * scale_row
    return jnp.concatenate([spread, innovation[None]], axis=0).astype(jnp.bfloat16)

def transform(patch_values, gram_sum):
    identity = jnp.eye(REALIZATION_TOTAL, dtype=jnp.float32)
    system = identity + gram_sum[:, :REALIZATION_TOTAL, :REALIZATION_TOTAL]
    coupling = gram_sum[:, :REALIZATION_TOTAL, REALIZATION_TOTAL]
    trace_sum = jnp.trace(system, axis1=1, axis2=2)
    scaled = system / trace_sum[:, None, None]

    def newton(turn_index, carry):
        upper_iter, lower_iter = carry
        factor = 1.5 * identity - 0.5 * jnp.einsum('pij,pjk->pik', lower_iter, upper_iter, precision=HIGHEST)
        return (jnp.einsum('pij,pjk->pik', upper_iter, factor, precision=HIGHEST), jnp.einsum('pij,pjk->pik', factor, lower_iter, precision=HIGHEST))
    start_lower = jnp.broadcast_to(identity, scaled.shape)
    upper_iter, lower_iter = lax.fori_loop(0, ITERS, newton, (scaled, start_lower))
    inv_root = lower_iter / jnp.sqrt(trace_sum)[:, None, None]
    half_step = jnp.einsum('pkl,pl->pk', inv_root, coupling, precision=HIGHEST)
    mean_weight = jnp.einsum('pkl,pl->pk', inv_root, half_step, precision=HIGHEST) / math.sqrt(REALIZATION_TOTAL - 1)
    weights = mean_weight[:, :, None] + inv_root
    center = lax.optimization_barrier(jnp.mean(patch_values, axis=0))
    return center + jnp.einsum('kfpt,pki->ifpt', patch_values - center, weights, precision=HIGHEST)

def update_with_observations(row_items):
    row_state, own_block, right_adjacent, leftward_adjacent, upper_adjacent, bottom_adjacent = row_items
    gram_sum = jnp.zeros((NPR, REALIZATION_TOTAL + 1, REALIZATION_TOTAL + 1), jnp.float32)
    for neighbor_block in (own_block, right_adjacent, leftward_adjacent, upper_adjacent, bottom_adjacent):
        widened = neighbor_block.astype(jnp.float32)
        gram_sum = gram_sum + jnp.einsum('kpj,lpj->pkl', widened, widened, precision=HIGHEST)
    result = transform(row_state.reshape(REALIZATION_TOTAL, QUANTITY_TOTAL, NPR, PW), gram_sum)
    return result.reshape(REALIZATION_TOTAL, QUANTITY_TOTAL, MERIDIAN_POINTS)

def reference(background, wind_east, wind_north, obs_index, obs_value, obs_scale):
    circumpolar_wind_speed = wind_east.astype(jnp.float32)[:, None, :]
    poleward_wind_speed = wind_north.astype(jnp.float32)[:, None, :]

    def advance(sample_realization):
        return predicted_realization(sample_realization, circumpolar_wind_speed, poleward_wind_speed)
    advanced_in_time = lax.map(advance, jnp.moveaxis(background, 1, 0))
    integrate_model = jnp.moveaxis(advanced_in_time, 0, 1)
    model_variables = integrate_model.reshape(PARALLEL_LINES, REALIZATION_TOTAL, QUANTITY_TOTAL * MERIDIAN_POINTS)
    index_rows = obs_index.reshape(PARALLEL_LINES, NPR, NOBS)
    value_rows = obs_value.reshape(PARALLEL_LINES, NPR, NOBS)
    scale_rows = obs_scale.reshape(PARALLEL_LINES, NPR, NOBS)

    def block_row(row_items):
        return make_blocks(row_items[0], row_items[1], row_items[2], row_items[3])
    mesh_tiles = lax.map(block_row, (model_variables, index_rows, value_rows, scale_rows))
    zero_row = jnp.zeros((1,) + mesh_tiles.shape[1:], jnp.bfloat16)
    upper_adjacent = jnp.concatenate([zero_row, mesh_tiles[:-1]], axis=0)
    bottom_adjacent = jnp.concatenate([mesh_tiles[1:], zero_row], axis=0)
    right_adjacent = jnp.roll(mesh_tiles, -1, axis=2)
    leftward_adjacent = jnp.roll(mesh_tiles, 1, axis=2)
    return lax.map(update_with_observations, (integrate_model, mesh_tiles, right_adjacent, leftward_adjacent, upper_adjacent, bottom_adjacent))
```

```python
import functools
import math

import jax
import jax.numpy as jnp
from jax import lax
from jax.experimental import pallas as pl
from jax.experimental.pallas import tpu as pltpu
from jax.sharding import PartitionSpec as P

PW = 256
NOBS = 128
STEPS = 4
ITERS = 12
LANES = 128
HALO = 4 * STEPS + 1
CHUNK = 8

HIGHEST = lax.Precision.HIGHEST
F32 = jnp.float32
BF16 = jnp.bfloat16


def padded_2(block, sides, width, periodic):
    for axis, dim in sides:
        count = lax.axis_size(axis)
        forward = [(i, i + 1) for i in range(count - 1)]
        if periodic:
            forward.append((count - 1, 0))
        backward = [(target, source) for source, target in forward]
        low = lax.ppermute(
            lax.slice_in_dim(block, block.shape[dim] - width, None, axis=dim), axis, forward
        )
        high = lax.ppermute(lax.slice_in_dim(block, 0, width, axis=dim), axis, backward)
        block = jnp.concatenate([low, block, high], axis=dim)
    return block


def tendency(padded, circumpolar_wind_speed, poleward_wind_speed):
    center_rows = padded[1:-1]
    along_diff = jnp.roll(center_rows, -1, axis=-1) - jnp.roll(center_rows, 1, axis=-1)
    across_diff = padded[2:] - padded[:-2]
    return -0.5 * (circumpolar_wind_speed * along_diff + poleward_wind_speed * across_diff)


def make_blocks(model_variables, index_rows, value_rows, scale_rows):
    row_count, members, flat_width = model_variables.shape
    patch_count = index_rows.shape[1]
    obs_count = index_rows.shape[2]
    fields = flat_width // (patch_count * PW)
    patch_values = model_variables.reshape(row_count, members, fields, patch_count, PW)
    value_ids = lax.broadcasted_iota(jnp.int32, (fields * PW, 1), 0)
    selector = (value_ids[None, None] == index_rows[:, :, None, :]).astype(jnp.float32)
    selector = selector.reshape(row_count, patch_count, fields, PW, obs_count)
    picked = jnp.einsum("akfpt,apftj->akpj", patch_values, selector, precision=HIGHEST)
    average = jnp.mean(picked, axis=1)
    spread = (picked - average[:, None]) * scale_rows[:, None] / math.sqrt(members - 1)
    innovation = (value_rows - average) * scale_rows
    return jnp.concatenate([spread, innovation[:, None]], axis=1).astype(jnp.bfloat16)


def edge_pair(extended):
    return jnp.stack([extended[-1], extended[0]])


def rows_beside(local_rows, extended, banded):
    position = lax.axis_index("mem")
    last_index = lax.axis_size("mem") - 1
    upper_rim = jnp.where(position == 0, banded[0], extended[0])
    lower_rim = jnp.where(position == last_index, banded[3], extended[-1])
    upper_adjacent = jnp.concatenate([upper_rim[None], local_rows[:-1]], axis=0)
    bottom_adjacent = jnp.concatenate([local_rows[1:], lower_rim[None]], axis=0)
    return (upper_adjacent, bottom_adjacent)


def per_device_any(background, wind_east, wind_north, obs_index, obs_value, obs_scale):
    current = background
    stacked_winds = jnp.stack([wind_east, wind_north])
    wide_winds = padded_2(stacked_winds, (("lat", 1),), 3, False).astype(jnp.float32)
    east_wide = wide_winds[0][:, None, None, :]
    north_wide = wide_winds[1][:, None, None, :]
    span = east_wide.shape[0]
    for step_index in range(STEPS):
        extended = padded_2(current, (("lat", 0),), 4, False)
        slope_one = tendency(extended, east_wide, north_wide)
        slope_two = tendency(
            extended[1:-1] + 0.5 * slope_one, east_wide[1 : span - 1], north_wide[1 : span - 1]
        )
        slope_three = tendency(
            extended[2:-2] + 0.5 * slope_two, east_wide[2 : span - 2], north_wide[2 : span - 2]
        )
        slope_four = tendency(
            extended[3:-3] + slope_three, east_wide[3 : span - 3], north_wide[3 : span - 3]
        )
        current = (
            extended[4:-4]
            + (slope_one[3:-3] + 2.0 * slope_two[2:-2] + 2.0 * slope_three[1:-1] + slope_four) / 6.0
        )
    points = lax.all_to_all(current, "mem", split_axis=0, concat_axis=1, tiled=True)
    row_count, members, fields, width = points.shape
    patch_count = obs_index.shape[2]
    model_variables = points.reshape(row_count, members, fields * width)
    index_rows = obs_index.reshape(row_count, patch_count, NOBS)
    value_rows = obs_value.reshape(row_count, patch_count, NOBS)
    scale_rows = obs_scale.reshape(row_count, patch_count, NOBS)
    own_block = make_blocks(model_variables, index_rows, value_rows, scale_rows)
    extended = padded_2(own_block, (("mem", 0),), 1, True)
    banded = padded_2(edge_pair(extended), (("lat", 0),), 1, False)
    upper_adjacent, bottom_adjacent = rows_beside(own_block, extended, banded)
    gram_sum = jnp.zeros((row_count, patch_count, members + 1, members + 1), jnp.float32)
    for neighbor_block in (
        own_block,
        jnp.roll(own_block, -1, axis=2),
        jnp.roll(own_block, 1, axis=2),
        upper_adjacent,
        bottom_adjacent,
    ):
        gram_sum = gram_sum + jnp.einsum(
            "akpj,alpj->apkl", neighbor_block, neighbor_block, preferred_element_type=jnp.float32
        )
    identity = jnp.eye(members, dtype=jnp.float32)
    system = identity + gram_sum[:, :, :members, :members]
    coupling = gram_sum[:, :, :members, members]
    trace_sum = jnp.trace(system, axis1=2, axis2=3)
    scaled = system / trace_sum[:, :, None, None]

    def newton(turn_index, carry):
        upper_iter, lower_iter = carry
        factor = 1.5 * identity - 0.5 * jnp.einsum(
            "apij,apjk->apik", lower_iter, upper_iter, precision=HIGHEST
        )
        return (
            jnp.einsum("apij,apjk->apik", upper_iter, factor, precision=HIGHEST),
            jnp.einsum("apij,apjk->apik", factor, lower_iter, precision=HIGHEST),
        )

    start_lower = jnp.broadcast_to(identity, scaled.shape)
    upper_iter, lower_iter = lax.fori_loop(0, ITERS, newton, (scaled, start_lower))
    inv_root = lower_iter / jnp.sqrt(trace_sum)[:, :, None, None]
    half_step = jnp.einsum("apkl,apl->apk", inv_root, coupling, precision=HIGHEST)
    mean_weight = jnp.einsum("apkl,apl->apk", inv_root, half_step, precision=HIGHEST) / math.sqrt(
        members - 1
    )
    weights = mean_weight[:, :, :, None] + inv_root
    patch_values = points.reshape(row_count, members, fields, patch_count, PW)
    center = jnp.mean(patch_values, axis=1)
    result = center[:, None] + jnp.einsum(
        "akfpt,apki->aifpt", patch_values - center[:, None], weights, precision=HIGHEST
    )
    analysis = result.reshape(row_count, members, fields, width)
    return lax.all_to_all(analysis, "mem", split_axis=1, concat_axis=0, tiled=True)


PAD = 8
INNER_BLOCK = 32
OUTER_BLOCK = 25
LEVELS = 32766.0
LOG_STEP = math.log(2.0) / 512.0


def take_lanes(values, lanes):
    return jnp.take_along_axis(values, lanes, axis=1, mode="promise_in_bounds")


def parity_matrix():
    source = lax.broadcasted_iota(jnp.int32, (2 * LANES, 2 * LANES), 0)
    target = lax.broadcasted_iota(jnp.int32, (2 * LANES, 2 * LANES), 1)
    wanted = jnp.where(target < LANES, 2 * target, 2 * (target - LANES) + 1)
    return jnp.where(source == wanted, F32(1.0), F32(0.0)).astype(BF16)


def stage_states(source_ref, rows_of, count, members, matrix, store):
    for field in range(2):
        low = [source_ref[rows_of(k), pl.ds(field, members, stride=4), :] for k in range(count)]
        high = [
            source_ref[rows_of(k), pl.ds(2 + field, members, stride=4), :] for k in range(count)
        ]
        left = jnp.concatenate(
            [jnp.concatenate(low, axis=0), jnp.concatenate(high, axis=0)], axis=1
        )
        first = left.astype(BF16)
        left = left - first.astype(F32)
        second = left.astype(BF16)
        third = (left - second.astype(F32)).astype(BF16)
        split = jnp.dot(first, matrix, preferred_element_type=F32) + (
            jnp.dot(second, matrix, preferred_element_type=F32)
            + jnp.dot(third, matrix, preferred_element_type=F32)
        )
        store(field, split[:, :LANES].reshape(count, members, LANES))
        store(2 + field, split[:, LANES:].reshape(count, members, LANES))


def stage_winds(east, north, north_sign, matrix, w_ref, start):
    count = east.shape[0]
    for side, (wind, sign) in enumerate(((east, F32(-0.25)), (north, north_sign))):
        split = jnp.dot(wind, matrix, preferred_element_type=F32) * sign
        for parity in range(2):
            lanes = split[:, parity * LANES : (parity + 1) * LANES]
            wide = jnp.broadcast_to(lanes[:, None, :], (count, w_ref.shape[2], LANES))
            w_ref[2 * side + parity, pl.ds(start, count)] = wide


def rk_passes(q_ref, stage_refs, offset, w_ref, wind_row, first, count, block):
    a_ref, b_ref, c_ref = stage_refs

    def finish_one(part, at, half):
        a_ref[part, at] = q_ref[part, at] + half

    def finish_two(part, at, half):
        b_ref[part, at] = q_ref[part, at] + half

    def finish_three(part, at, half):
        c_ref[part, at] = q_ref[part, at] + (half + half)

    def finish_four(part, at, half):
        doubled = b_ref[part, at]
        gathered = (a_ref[part, at] + c_ref[part, at] - q_ref[part, at]) + (doubled + doubled)
        q_ref[part, at] = (gathered + half) * F32(1.0 / 3.0)

    for stage, finish in (
        (q_ref, finish_one),
        (a_ref, finish_two),
        (b_ref, finish_three),
        (c_ref, finish_four),
    ):

        def turn(index, _):
            base = first + index * block + offset
            states = [[stage[part, base + k - 1] for k in range(block + 2)] for part in range(4)]
            for k in range(1, block + 1):
                place = wind_row(base - offset + k - 1)
                winds = [w_ref[part, place] for part in range(4)]
                for field in range(2):
                    even, odd = states[field], states[2 + field]
                    along_even = odd[k] - pltpu.roll(odd[k], 1, 1)
                    along_odd = pltpu.roll(even[k], LANES - 1, 1) - even[k]
                    finish(
                        field,
                        base + k - 1,
                        winds[0] * along_even + winds[2] * (even[k + 1] - even[k - 1]),
                    )
                    finish(
                        2 + field,
                        base + k - 1,
                        winds[1] * along_odd + winds[3] * (odd[k + 1] - odd[k - 1]),
                    )
            return 0

        turns = -(-count // block)
        if turns == 1:
            turn(0, 0)
        else:
            lax.fori_loop(0, turns, turn, 0)


def encode_rows(states, row_count, members, store):
    lane = lax.broadcasted_iota(jnp.int32, (members, LANES), 1)
    scales = jnp.zeros((members, LANES), jnp.int32)
    coded = []
    for j in range(row_count):
        top = jnp.abs(states[j][0])
        for part in range(1, 4):
            top = jnp.maximum(top, jnp.abs(states[j][part]))
        top = jnp.maximum(jnp.max(top, axis=1, keepdims=True), F32(1e-9))
        level = jnp.floor(jnp.log(top) * F32(1.0 / LOG_STEP)) + 2.0
        factor = F32(LEVELS) / jnp.exp(level * F32(LOG_STEP))
        scales = jnp.where(lane == j, level.astype(jnp.int32), scales)
        coded.append([jnp.round(states[j][part] * factor).astype(jnp.int32) for part in range(4)])
    for part in range(4):
        for j in range(0, row_count, 2):
            store(
                (part * row_count + j) * members,
                jnp.concatenate([coded[j][part], coded[j + 1][part]], axis=0).astype(jnp.int16),
            )
    store(
        4 * row_count * members,
        jnp.concatenate([scales, jnp.zeros_like(scales)], axis=0).astype(jnp.int16),
    )


def inner_kernel(sizes, flags_ref, own_ref, east_ref, north_ref, q_ref, out_ref, w_ref, *stage_refs):
    rows, members, devices = sizes
    own_rows = rows // devices
    band = flags_ref[0]
    matrix = parity_matrix()
    north_sign = jnp.where(band == 0, F32(-0.25), F32(0.25))
    for ref in (q_ref, *stage_refs):
        ref[:, :PAD] = jnp.zeros((4, PAD, members, LANES), F32)
        ref[:, PAD + rows :] = jnp.zeros((4, PAD, members, LANES), F32)
    w_ref[...] = jnp.zeros(w_ref.shape, F32)
    stage_winds(east_ref[...], north_ref[...], north_sign, matrix, w_ref, PAD)

    def stage(index, _):
        base = index * CHUNK

        def store(part, values):
            q_ref[part, pl.ds(PAD + base, CHUNK)] = values

        def row_of(k):
            return jnp.where(band == 0, base + k, rows - 1 - base - k)

        stage_states(own_ref, row_of, CHUNK, members, matrix, store)
        return 0

    lax.fori_loop(0, rows // CHUNK, stage, 0)

    def wind_row(row):
        return PAD + jnp.where(band == 0, row, rows - 1 - row)

    def step(_, carry):
        rk_passes(q_ref, stage_refs, PAD, w_ref, wind_row, 0, rows, INNER_BLOCK)
        return carry

    lax.fori_loop(0, STEPS, step, 0)

    def emit(device, _):
        def store(place, values):
            out_ref[device, pl.ds(place, values.shape[0]), :] = values

        base = PAD + device * own_rows
        states = [[q_ref[part, base + j] for part in range(4)] for j in range(own_rows)]
        encode_rows(states, own_rows, members, store)
        return 0

    lax.fori_loop(0, (rows - 4 * STEPS) // own_rows, emit, 0)


def outer_kernel(
    sizes,
    flags_ref,
    own_ref,
    halo_ref,
    halo_winds_ref,
    east_ref,
    north_ref,
    inner_ref,
    table_ref,
    coded_ref,
    out_ref,
    observed_ref,
    q_ref,
    w_ref,
    *stage_refs,
):
    rows, members, devices = sizes
    own_rows = rows // devices
    band = flags_ref[0]
    matrix = parity_matrix()
    north_sign = jnp.where(band == 0, F32(-0.25), F32(0.25))
    wind_halo = halo_winds_ref.shape[0] // 4
    inner_rows = rows - 4 * STEPS
    first = inner_rows - 4 * STEPS
    count = rows + HALO - first
    shift = 4 - first

    w_ref[...] = jnp.zeros(w_ref.shape, F32)
    stage_winds(
        east_ref[...],
        north_ref[...],
        north_sign,
        matrix,
        w_ref,
        PAD + jnp.where(band == 0, 0, wind_halo),
    )
    halo_winds = [
        halo_winds_ref[part * wind_halo : (part + 1) * wind_halo].astype(BF16) for part in range(4)
    ]
    stage_winds(
        jnp.concatenate(halo_winds[:2], axis=1),
        jnp.concatenate(halo_winds[2:], axis=1),
        north_sign,
        matrix,
        w_ref,
        PAD + jnp.where(band == 0, rows, 0),
    )

    def stage_own(index, _):
        base = first + index * CHUNK

        def store(part, values):
            q_ref[part, pl.ds(shift + base, CHUNK)] = values

        def row_of(k):
            return jnp.where(band == 0, base + k, rows - 1 - base - k)

        stage_states(own_ref, row_of, CHUNK, members, matrix, store)
        return 0

    lax.fori_loop(0, (rows - first) // CHUNK, stage_own, 0)

    def stage_halo(index, _):
        base = index * CHUNK

        def store(part, values):
            q_ref[part, pl.ds(shift + rows + base, CHUNK)] = values

        def row_of(k):
            row = jnp.minimum(base + k, HALO - 1)
            return jnp.where(band == 0, row, HALO - 1 - row)

        stage_states(halo_ref, row_of, CHUNK, members, matrix, store)
        return 0

    lax.fori_loop(0, -(-HALO // CHUNK), stage_halo, 0)

    def wind_row(row):
        return PAD + jnp.where(band == 0, row, rows + wind_halo - 1 - row)

    def step(_, carry):
        rk_passes(q_ref, stage_refs, shift, w_ref, wind_row, first, count, OUTER_BLOCK)
        return carry

    lax.fori_loop(0, STEPS, step, 0)

    def observed(states, table_row):
        index = jnp.broadcast_to(table_ref[pl.ds(table_row * 3, 1), :], (members, LANES))
        index = index.astype(jnp.int32)
        lanes = jnp.bitwise_and(jnp.right_shift(index, 1), LANES - 1)
        is_odd = jnp.bitwise_and(index, 1) == 1
        second = index >= 2 * LANES
        picks = [take_lanes(state, lanes) for state in states]
        return jnp.where(
            second,
            jnp.where(is_odd, picks[3], picks[1]),
            jnp.where(is_odd, picks[2], picks[0]),
        )

    def table_row_of(row):
        return band * rows + jnp.where(band == 0, row, rows - 1 - row)

    def place(device, slot, values):
        observed_ref[device, pl.ds(slot * members, members), :] = values

    def emit(device, state_of):
        values = []
        for j in range(own_rows):
            row = device * own_rows + j
            values.append(observed(state_of(row), table_row_of(row)))
            place(device, j + 1, values[j])

        @pl.when(device + 1 < devices)
        def _():
            place(device + 1, 0, values[own_rows - 1])

        @pl.when(device > 0)
        def _():
            place(device - 1, own_rows + 1, values[0])

    def emit_inner(device, _):
        emit(device, lambda row: [inner_ref[part, PAD + row] for part in range(4)])
        return 0

    def outer_state(row):
        return [q_ref[part, shift + row] for part in range(4)]

    def emit_outer(device, _):
        emit(device, outer_state)

        def store(place_at, values):
            out_ref[device, pl.ds(place_at, values.shape[0]), :] = values

        states = [outer_state(device * own_rows + j) for j in range(own_rows)]
        encode_rows(states, own_rows, members, store)
        return 0

    lax.fori_loop(0, inner_rows // own_rows, emit_inner, 0)
    out_ref[...] = coded_ref[...]
    lax.fori_loop(inner_rows // own_rows, devices, emit_outer, 0)
    place(0, 0, jnp.zeros((members, LANES), F32))
    edge = (1 - band) * rows + jnp.where(band == 0, 0, rows - 1)
    place(devices - 1, own_rows + 1, observed(outer_state(rows), edge))


def split_value(value):
    high = value.astype(BF16)
    return high, (value - high.astype(F32)).astype(BF16)


def product(left, right):
    (left_high, left_low), (right_high, right_low) = left, right
    size = right_high.shape[1]
    both = jnp.dot(
        jnp.concatenate([left_high, left_low], axis=1),
        jnp.concatenate(
            [
                jnp.concatenate([right_high, right_low], axis=1),
                jnp.concatenate([right_high, jnp.zeros_like(right_low)], axis=1),
            ],
            axis=0,
        ),
        preferred_element_type=F32,
    )
    return both[:, :size] + both[:, size:]


def weights_kernel(
    sizes, flags_ref, got_ref, table_ref, out_ref, upper_ref, upper_low_ref, lower_ref, lower_low_ref
):
    rows, members, devices = sizes
    own_rows = rows // devices
    total = members * devices
    band = flags_ref[0]
    first = flags_ref[1] * own_rows
    nobs = LANES

    def info(row):
        inside = jnp.logical_and(row >= 0, row < rows)
        here = band * rows + jnp.where(band == 0, row, rows - 1 - row)
        edge = (1 - band) * rows + jnp.where(band == 0, 0, rows - 1)
        at = 3 * jnp.where(inside, here, edge)
        keep = jnp.where(row >= 0, F32(1.0), F32(0.0))
        return table_ref[pl.ds(at + 1, 1), :], table_ref[pl.ds(at + 2, 1), :] * keep

    grams = []
    couplings = []
    for j in range(-1, own_rows + 1):
        value, scale = info(first + j)
        picked = got_ref[:, (j + 1) * members : (j + 2) * members, :].reshape(total, nobs)
        average = jnp.mean(picked, axis=0, keepdims=True)
        spread = ((picked - average) * scale / math.sqrt(total - 1)).astype(BF16)
        innovation = jnp.broadcast_to((value - average) * scale, (16, nobs)).astype(BF16)
        contract = (((1,), (1,)), ((), ()))
        grams.append(lax.dot_general(spread, spread, contract, preferred_element_type=F32))
        couplings.append(
            lax.dot_general(innovation, spread, contract, preferred_element_type=F32)
        )

    row_ids = lax.broadcasted_iota(jnp.int32, (total, total), 0)
    column_ids = lax.broadcasted_iota(jnp.int32, (total, total), 1)
    diagonal = row_ids == column_ids
    identity = jnp.where(diagonal, F32(1.0), F32(0.0))

    def put(high_ref, low_ref, j, value):
        high_ref[j], low_ref[j] = split_value(value)

    traces = []
    for j in range(own_rows):
        system = identity + 3.0 * grams[j + 1] + grams[j] + grams[j + 2]
        trace = jnp.sum(
            jnp.sum(jnp.where(diagonal, system, 0.0), axis=0, keepdims=True),
            axis=1,
            keepdims=True,
        )
        traces.append(trace)
        scaled = system / trace
        factor = split_value(1.5 * identity - 0.5 * scaled)
        put(upper_ref, upper_low_ref, j, product(split_value(scaled), factor))
        lower_ref[j], lower_low_ref[j] = factor

    def factor_of(j):
        lower = lower_ref[j], lower_low_ref[j]
        upper = upper_ref[j], upper_low_ref[j]
        return lower, upper, split_value(1.5 * identity - 0.5 * product(lower, upper))

    def newton(turn, _):
        parts = [factor_of(j) for j in range(own_rows)]
        for j in range(own_rows):
            lower, upper, factor = parts[j]
            put(upper_ref, upper_low_ref, j, product(upper, factor))
            put(lower_ref, lower_low_ref, j, product(factor, lower))
        return 0

    lax.fori_loop(0, ITERS - 2, newton, 0)

    parts = [factor_of(j) for j in range(own_rows)]
    for j in range(own_rows):
        lower, upper, factor = parts[j]
        inv_root = product(factor, lower) / jnp.sqrt(traces[j])
        coupling = 3.0 * couplings[j + 1] + couplings[j] + couplings[j + 2]
        root_parts = split_value(inv_root)
        half_step = product(split_value(coupling), root_parts)
        mean_weight = product(split_value(half_step), root_parts)[:1] / math.sqrt(total - 1)
        out_ref[j] = inv_root + mean_weight


def apply_kernel(sizes, got_ref, weights_ref, out_ref):
    rows, members, devices = sizes
    own_rows = rows // devices
    total = members * devices
    pair = 2 * members
    levels = got_ref[:, pl.ds(4 * own_rows * members, pair), :].astype(jnp.int32).astype(F32)
    levels = levels[:, :members].reshape(total, LANES)
    scales = jnp.exp(levels * F32(LOG_STEP)) * F32(1.0 / LEVELS)
    weights = [split_value(weights_ref[j]) for j in range(own_rows)]
    for j in range(0, own_rows, 2):
        for part in range(4):
            place = (part * own_rows + j) * members
            both = got_ref[:, pl.ds(place, pair), :].astype(jnp.int32).astype(F32)
            both = both.reshape(devices, 2, members, LANES)
            moved = []
            for k in range(2):
                state = both[:, k].reshape(total, LANES) * scales[:, j + k : j + k + 1]
                center = jnp.mean(state, axis=0, keepdims=True)
                high, low = split_value(state - center)
                weights_high, weights_low = weights[j + k]
                result = center + (
                    jnp.dot(weights_high, high, preferred_element_type=F32)
                    + jnp.dot(weights_high, low, preferred_element_type=F32)
                    + jnp.dot(weights_low, high, preferred_element_type=F32)
                )
                moved.append(result.reshape(devices, members, LANES))
            out_ref[:, pl.ds(place, pair), :] = jnp.concatenate(moved, axis=1).astype(BF16)


def unpack_kernel(sizes, flags_ref, got_ref, out_ref):
    rows, members, devices = sizes
    own_rows = rows // devices
    band = flags_ref[0]
    pair = 2 * members
    source = lax.broadcasted_iota(jnp.int32, (2 * LANES, 2 * LANES), 0)
    target = lax.broadcasted_iota(jnp.int32, (2 * LANES, 2 * LANES), 1)
    wanted = jnp.where(source < LANES, 2 * source, 2 * (source - LANES) + 1)
    matrix = jnp.where(target == wanted, F32(1.0), F32(0.0)).astype(BF16)

    def place(index, _):
        device = index * 2
        for field in range(2):
            even, odd = [
                jnp.concatenate(
                    [
                        got_ref[
                            device + d, pl.ds((part * own_rows) * members, own_rows * members), :
                        ]
                        for d in range(2)
                    ],
                    axis=0,
                )
                for part in (field, 2 + field)
            ]
            joined = jnp.dot(
                jnp.concatenate([even, odd], axis=1), matrix, preferred_element_type=F32
            )
            for k in range(2 * own_rows):
                row = device * own_rows + k
                row = jnp.where(band == 0, row, rows - 1 - row)
                values = joined[k * members : (k + 1) * members]
                for half in range(2):
                    out_ref[row, pl.ds(2 * half + field, members, stride=4), :] = values[
                        :, half * LANES : (half + 1) * LANES
                    ]
        return 0

    lax.fori_loop(0, devices // 2, place, 0)


def per_device_pair(background, wind_east, wind_north, obs_index, obs_value, obs_scale):
    rows, members, fields, width = background.shape
    devices = lax.axis_size("mem")
    bands = lax.axis_size("lat")
    own_rows = rows // devices
    total = members * devices
    sizes = (rows, members, devices)
    band = lax.axis_index("lat")
    flags = jnp.stack([band, lax.axis_index("mem")]).astype(jnp.int32)
    smem = pl.BlockSpec(memory_space=pltpu.SMEM)
    vmem = pl.BlockSpec(memory_space=pltpu.VMEM)
    params = pltpu.CompilerParams(vmem_limit_bytes=40 * 1024 * 1024)

    def cost(microseconds):
        return pl.CostEstimate(
            flops=0, bytes_accessed=int(microseconds * 3_000_000), transcendentals=0
        )

    grouped = members * fields * 2
    own = background.reshape(rows, members, fields, 2, LANES)
    own = own.transpose(0, 1, 3, 2, 4).reshape(rows, grouped, LANES)

    wind_halo = -(-HALO // CHUNK) * CHUNK

    def edge_rows(array, count):
        return lax.dynamic_slice_in_dim(
            array, jnp.where(band == 0, rows - count, 0), count, 0
        )

    edge_winds = [edge_rows(wind, wind_halo).astype(F32) for wind in (wind_east, wind_north)]
    sent = jnp.concatenate(
        [edge_rows(own, HALO).reshape(HALO * grouped, LANES)]
        + [wind[:, half * LANES : (half + 1) * LANES] for wind in edge_winds for half in range(2)],
        axis=0,
    )
    halo = lax.ppermute(sent, "lat", [(0, 1), (1, 0)])
    info = jnp.stack(
        [
            obs_index.reshape(own_rows, NOBS).astype(F32),
            obs_value.reshape(own_rows, NOBS),
            obs_scale.reshape(own_rows, NOBS),
        ],
        axis=1,
    ).reshape(1, own_rows * 3, NOBS)
    table = lax.all_to_all(
        jnp.broadcast_to(info, (bands * devices, own_rows * 3, NOBS)),
        ("lat", "mem"),
        split_axis=0,
        concat_axis=0,
        tiled=True,
    ).reshape(bands * rows * 3, NOBS)

    coded_shape = jax.ShapeDtypeStruct(
        (devices, (4 * own_rows + 2) * members, LANES), jnp.int16
    )
    inner, coded = pl.pallas_call(
        functools.partial(inner_kernel, sizes),
        out_shape=(
            jax.ShapeDtypeStruct((4, rows + 2 * PAD, members, LANES), F32),
            coded_shape,
        ),
        in_specs=[smem, vmem, vmem, vmem],
        out_specs=(vmem, vmem),
        scratch_shapes=[pltpu.VMEM((4, rows + 2 * PAD, members, LANES), F32)] * 4,
        compiler_params=params,
        cost_estimate=cost(6),
        name="forecast_inner",
    )(flags, own, wind_east, wind_north)

    outer_rows = 4 * STEPS * 2 + wind_halo + CHUNK
    coded, observed = pl.pallas_call(
        functools.partial(outer_kernel, sizes),
        out_shape=(
            coded_shape,
            jax.ShapeDtypeStruct((devices, (own_rows + 2) * members, LANES), F32),
        ),
        in_specs=[smem] + [vmem] * 8,
        out_specs=(vmem, vmem),
        scratch_shapes=[
            pltpu.VMEM((4, outer_rows, members, LANES), F32),
            pltpu.VMEM((4, rows + wind_halo + 2 * PAD, members, LANES), F32),
        ]
        + [pltpu.VMEM((4, outer_rows, members, LANES), F32)] * 3,
        compiler_params=params,
        cost_estimate=cost(6),
        name="forecast_outer",
    )(
        flags,
        own,
        halo[: HALO * grouped].reshape(HALO, grouped, LANES),
        halo[HALO * grouped :],
        wind_east,
        wind_north,
        inner,
        table,
        coded,
    )
    got_observed = lax.all_to_all(observed, "mem", split_axis=0, concat_axis=0, tiled=True)
    got_states = lax.all_to_all(coded, "mem", split_axis=0, concat_axis=0, tiled=True)
    half_matrix = pltpu.VMEM((own_rows, total, total), BF16)
    weights = pl.pallas_call(
        functools.partial(weights_kernel, sizes),
        out_shape=jax.ShapeDtypeStruct((own_rows, total, total), F32),
        in_specs=[smem, vmem, vmem],
        out_specs=vmem,
        scratch_shapes=[half_matrix] * 4,
        compiler_params=params,
        cost_estimate=cost(12),
        name="weights",
    )(flags, got_observed, table)
    back = pl.pallas_call(
        functools.partial(apply_kernel, sizes),
        out_shape=jax.ShapeDtypeStruct((devices, 4 * own_rows * members, LANES), BF16),
        in_specs=[vmem, vmem],
        out_specs=vmem,
        compiler_params=params,
        cost_estimate=cost(2),
        name="apply",
    )(got_states, weights)
    returned = lax.all_to_all(back, "mem", split_axis=0, concat_axis=0, tiled=True)
    result = pl.pallas_call(
        functools.partial(unpack_kernel, sizes),
        out_shape=jax.ShapeDtypeStruct((rows, grouped, LANES), F32),
        in_specs=[smem, vmem],
        out_specs=vmem,
        compiler_params=params,
        cost_estimate=cost(2),
        name="unpack",
    )(flags, returned)
    result = result.reshape(rows, members, 2, fields, LANES).transpose(0, 1, 3, 2, 4)
    return result.reshape(rows, members, fields, width)


def per_device(background, wind_east, wind_north, obs_index, obs_value, obs_scale):
    rows, members, fields, width = background.shape
    devices = lax.axis_size("mem")
    fits = (
        lax.axis_size("lat") == 2
        and members == 8
        and members * devices == LANES
        and fields == 2
        and width == 2 * LANES == PW
        and obs_index.shape[2:] == (1, LANES)
        and rows % (2 * CHUNK) == 0
        and 4 * STEPS % (rows // devices) == 0
        and (rows // devices) % 2 == 0
        and rows >= 8 * STEPS
    )
    run = per_device_pair if fits else per_device_any
    return run(background, wind_east, wind_north, obs_index, obs_value, obs_scale)


def solution(mesh):
    in_specs = (
        P("lat", "mem", None, None),
        P("lat", None),
        P("lat", None),
        P("lat", "mem", None, None),
        P("lat", "mem", None, None),
        P("lat", "mem", None, None),
    )
    out_specs = P("lat", "mem", None, None)
    return jax.shard_map(
        per_device, mesh=mesh, in_specs=in_specs, out_specs=out_specs, check_vma=False
    )
```

```python
import functools
import math

import jax
import jax.numpy as jnp
from jax import lax
from jax.experimental import pallas as pl
from jax.experimental.pallas import tpu as pltpu
from jax.sharding import PartitionSpec as P

PW = 256
NOBS = 128
STEPS = 4
ITERS = 12
LANES = 128
HALO = 4 * STEPS + 1
CHUNK = 8

HIGHEST = lax.Precision.HIGHEST
F32 = jnp.float32
BF16 = jnp.bfloat16


def padded_2(block, sides, width, periodic):
    for axis, dim in sides:
        count = lax.axis_size(axis)
        forward = [(i, i + 1) for i in range(count - 1)]
        if periodic:
            forward.append((count - 1, 0))
        backward = [(target, source) for source, target in forward]
        low = lax.ppermute(
            lax.slice_in_dim(block, block.shape[dim] - width, None, axis=dim), axis, forward
        )
        high = lax.ppermute(lax.slice_in_dim(block, 0, width, axis=dim), axis, backward)
        block = jnp.concatenate([low, block, high], axis=dim)
    return block


def tendency(padded, circumpolar_wind_speed, poleward_wind_speed):
    center_rows = padded[1:-1]
    along_diff = jnp.roll(center_rows, -1, axis=-1) - jnp.roll(center_rows, 1, axis=-1)
    across_diff = padded[2:] - padded[:-2]
    return -0.5 * (circumpolar_wind_speed * along_diff + poleward_wind_speed * across_diff)


def make_blocks(model_variables, index_rows, value_rows, scale_rows):
    row_count, members, flat_width = model_variables.shape
    patch_count = index_rows.shape[1]
    obs_count = index_rows.shape[2]
    fields = flat_width // (patch_count * PW)
    patch_values = model_variables.reshape(row_count, members, fields, patch_count, PW)
    value_ids = lax.broadcasted_iota(jnp.int32, (fields * PW, 1), 0)
    selector = (value_ids[None, None] == index_rows[:, :, None, :]).astype(jnp.float32)
    selector = selector.reshape(row_count, patch_count, fields, PW, obs_count)
    picked = jnp.einsum("akfpt,apftj->akpj", patch_values, selector, precision=HIGHEST)
    average = jnp.mean(picked, axis=1)
    spread = (picked - average[:, None]) * scale_rows[:, None] / math.sqrt(members - 1)
    innovation = (value_rows - average) * scale_rows
    return jnp.concatenate([spread, innovation[:, None]], axis=1).astype(jnp.bfloat16)


def edge_pair(extended):
    return jnp.stack([extended[-1], extended[0]])


def rows_beside(local_rows, extended, banded):
    position = lax.axis_index("mem")
    last_index = lax.axis_size("mem") - 1
    upper_rim = jnp.where(position == 0, banded[0], extended[0])
    lower_rim = jnp.where(position == last_index, banded[3], extended[-1])
    upper_adjacent = jnp.concatenate([upper_rim[None], local_rows[:-1]], axis=0)
    bottom_adjacent = jnp.concatenate([local_rows[1:], lower_rim[None]], axis=0)
    return (upper_adjacent, bottom_adjacent)


def per_device_any(background, wind_east, wind_north, obs_index, obs_value, obs_scale):
    current = background
    stacked_winds = jnp.stack([wind_east, wind_north])
    wide_winds = padded_2(stacked_winds, (("lat", 1),), 3, False).astype(jnp.float32)
    east_wide = wide_winds[0][:, None, None, :]
    north_wide = wide_winds[1][:, None, None, :]
    span = east_wide.shape[0]
    for step_index in range(STEPS):
        extended = padded_2(current, (("lat", 0),), 4, False)
        slope_one = tendency(extended, east_wide, north_wide)
        slope_two = tendency(
            extended[1:-1] + 0.5 * slope_one, east_wide[1 : span - 1], north_wide[1 : span - 1]
        )
        slope_three = tendency(
            extended[2:-2] + 0.5 * slope_two, east_wide[2 : span - 2], north_wide[2 : span - 2]
        )
        slope_four = tendency(
            extended[3:-3] + slope_three, east_wide[3 : span - 3], north_wide[3 : span - 3]
        )
        current = (
            extended[4:-4]
            + (slope_one[3:-3] + 2.0 * slope_two[2:-2] + 2.0 * slope_three[1:-1] + slope_four) / 6.0
        )
    points = lax.all_to_all(current, "mem", split_axis=0, concat_axis=1, tiled=True)
    row_count, members, fields, width = points.shape
    patch_count = obs_index.shape[2]
    model_variables = points.reshape(row_count, members, fields * width)
    index_rows = obs_index.reshape(row_count, patch_count, NOBS)
    value_rows = obs_value.reshape(row_count, patch_count, NOBS)
    scale_rows = obs_scale.reshape(row_count, patch_count, NOBS)
    own_block = make_blocks(model_variables, index_rows, value_rows, scale_rows)
    extended = padded_2(own_block, (("mem", 0),), 1, True)
    banded = padded_2(edge_pair(extended), (("lat", 0),), 1, False)
    upper_adjacent, bottom_adjacent = rows_beside(own_block, extended, banded)
    gram_sum = jnp.zeros((row_count, patch_count, members + 1, members + 1), jnp.float32)
    for neighbor_block in (
        own_block,
        jnp.roll(own_block, -1, axis=2),
        jnp.roll(own_block, 1, axis=2),
        upper_adjacent,
        bottom_adjacent,
    ):
        gram_sum = gram_sum + jnp.einsum(
            "akpj,alpj->apkl", neighbor_block, neighbor_block, preferred_element_type=jnp.float32
        )
    identity = jnp.eye(members, dtype=jnp.float32)
    system = identity + gram_sum[:, :, :members, :members]
    coupling = gram_sum[:, :, :members, members]
    trace_sum = jnp.trace(system, axis1=2, axis2=3)
    scaled = system / trace_sum[:, :, None, None]

    def newton(turn_index, carry):
        upper_iter, lower_iter = carry
        factor = 1.5 * identity - 0.5 * jnp.einsum(
            "apij,apjk->apik", lower_iter, upper_iter, precision=HIGHEST
        )
        return (
            jnp.einsum("apij,apjk->apik", upper_iter, factor, precision=HIGHEST),
            jnp.einsum("apij,apjk->apik", factor, lower_iter, precision=HIGHEST),
        )

    start_lower = jnp.broadcast_to(identity, scaled.shape)
    upper_iter, lower_iter = lax.fori_loop(0, ITERS, newton, (scaled, start_lower))
    inv_root = lower_iter / jnp.sqrt(trace_sum)[:, :, None, None]
    half_step = jnp.einsum("apkl,apl->apk", inv_root, coupling, precision=HIGHEST)
    mean_weight = jnp.einsum("apkl,apl->apk", inv_root, half_step, precision=HIGHEST) / math.sqrt(
        members - 1
    )
    weights = mean_weight[:, :, :, None] + inv_root
    patch_values = points.reshape(row_count, members, fields, patch_count, PW)
    center = jnp.mean(patch_values, axis=1)
    result = center[:, None] + jnp.einsum(
        "akfpt,apki->aifpt", patch_values - center[:, None], weights, precision=HIGHEST
    )
    analysis = result.reshape(row_count, members, fields, width)
    return lax.all_to_all(analysis, "mem", split_axis=1, concat_axis=0, tiled=True)


PAD = 8
BLOCK = 20
FINEST = 0.05
LARGEST = 16.0 * sum(1.8**power / math.factorial(power) for power in range(5)) ** STEPS
STEEPNESS = 32766.0 / math.log(1.0 + LARGEST / FINEST)


def take_lanes(values, lanes):
    return jnp.take_along_axis(values, lanes, axis=1, mode="promise_in_bounds")


def pick_lanes(states, index):
    field = jnp.right_shift(index, 8)
    lanes = jnp.bitwise_and(jnp.right_shift(index, 1), LANES - 2) + field
    is_odd = jnp.bitwise_and(index, 1) == 1
    is_late = jnp.bitwise_and(index, 2) == 2
    picks = [take_lanes(state, lanes) for state in states]
    return jnp.where(
        is_odd, jnp.where(is_late, picks[3], picks[1]), jnp.where(is_late, picks[2], picks[0])
    )


def group_place(sizes, band, group):
    return jnp.where(band == 0, group, sizes[2] - 1 - group)


def beside_info(table_ref, sizes, band, group, is_after, kind):
    devices = sizes[2]
    near = group + 1 if is_after else jnp.maximum(group - 1, 0)
    over = near == devices
    place = jnp.where(over, jnp.where(band == 0, 0, devices - 1), group_place(sizes, band, near))
    near_band = jnp.where(over, 1 - band, band)
    last = jnp.where(band == 0, 0, 1) if is_after else jnp.where(band == 0, 1, 0)
    return table_ref[near_band * devices + place, pl.ds(2 * kind + last, 1), :]


def parts_matrix(from_parts=False):
    shape = (4 * LANES, 4 * LANES)
    rows = lax.broadcasted_iota(jnp.int32, shape, 0)
    columns = lax.broadcasted_iota(jnp.int32, shape, 1)
    column, plain = (rows, columns) if from_parts else (columns, rows)
    lane = jnp.bitwise_and(column, LANES - 1)
    wanted = (
        jnp.bitwise_and(lane, 1) * (2 * LANES)
        + jnp.right_shift(lane, 1) * 4
        + jnp.right_shift(column, 7)
    )
    return jnp.where(plain == wanted, F32(1.0), F32(0.0)).astype(BF16)


def stage_states(load, row_of, count, members, matrix, q_ref, start):
    left = jnp.concatenate(
        [
            jnp.concatenate([load(row_of(k), 2 * half + field) for k in range(count)], axis=0)
            for field in range(2)
            for half in range(2)
        ],
        axis=1,
    )
    first = left.astype(BF16)
    left = left - first.astype(F32)
    second = left.astype(BF16)
    third = (left - second.astype(F32)).astype(BF16)
    size = count * members
    split = jnp.dot(
        jnp.concatenate([first, second, third], axis=0), matrix, preferred_element_type=F32
    )
    split = split[:size] + (split[size : 2 * size] + split[2 * size :])
    for part in range(4):
        values = split[:, part * LANES : (part + 1) * LANES]
        q_ref[part, pl.ds(start, count)] = values.reshape(count, members, LANES)


def stage_winds(east, north, north_sign, matrix, w_ref, start):
    count = east.shape[0]
    for side, (wind, sign) in enumerate(((east, F32(-0.25)), (north, north_sign))):
        both = jnp.concatenate([wind, wind], axis=1)
        split = jnp.dot(both, matrix, preferred_element_type=F32) * sign
        for part in range(4):
            lanes = split[:, part * LANES : (part + 1) * LANES]
            wide = jnp.broadcast_to(lanes[:, None, :], (count, w_ref.shape[2], LANES))
            w_ref[4 * side + part, pl.ds(start, count)] = wide


def rk_passes(q_ref, stage_refs, offset, w_ref, wind_row, first, count, block):
    a_ref, b_ref, c_ref = stage_refs

    def finish_one(part, at, half):
        a_ref[part, at] = q_ref[part, at] + half

    def finish_two(part, at, half):
        b_ref[part, at] = q_ref[part, at] + half

    def finish_three(part, at, half):
        c_ref[part, at] = q_ref[part, at] + (half + half)

    def finish_four(part, at, half):
        doubled = b_ref[part, at]
        gathered = (a_ref[part, at] + c_ref[part, at] - q_ref[part, at]) + (doubled + doubled)
        q_ref[part, at] = (gathered + half) * F32(1.0 / 3.0)

    for stage, finish in (
        (q_ref, finish_one),
        (a_ref, finish_two),
        (b_ref, finish_three),
        (c_ref, finish_four),
    ):

        def turn(index, _):
            base = first + index * block + offset
            states = [[stage[part, base + k - 1] for k in range(block + 2)] for part in range(4)]
            for k in range(1, block + 1):
                place = wind_row(base - offset + k - 1)
                here = [states[part][k] for part in range(4)]
                along = (
                    here[1] - pltpu.roll(here[3], 2, 1),
                    here[2] - here[0],
                    here[3] - here[1],
                    pltpu.roll(here[0], LANES - 2, 1) - here[2],
                )
                for part in range(4):
                    across = states[part][k + 1] - states[part][k - 1]
                    half = w_ref[part, place] * along[part] + w_ref[4 + part, place] * across
                    finish(part, base + k - 1, half)
            return 0

        turns = -(-count // block)
        if turns == 1:
            turn(0, 0)
        else:
            lax.fori_loop(0, turns, turn, 0)


def encode(value):
    level = jnp.round(jnp.log(1.0 + jnp.abs(value) * F32(1.0 / FINEST)) * F32(STEEPNESS))
    return jnp.where(value < 0.0, -level, level)


def decode(code):
    size = (jnp.exp(jnp.abs(code) * F32(1.0 / STEEPNESS)) - 1.0) * F32(FINEST)
    return jnp.where(code < 0.0, -size, size)


def pack_pair(low, high):
    return jnp.concatenate([low, high], axis=0).astype(jnp.int32).astype(jnp.int16)


def halo_kernel(
    sizes, flags_ref, own_ref, east_ref, north_ref, sent_ref, winds_ref, copied, winds_copied
):
    rows, members, devices = sizes
    band = flags_ref[0]
    wind_halo = -(-HALO // CHUNK) * CHUNK
    begin = jnp.where(band == 0, rows - HALO, 0)
    copies = [
        pltpu.make_async_copy(ref, winds_ref.at[side], winds_copied.at[side])
        for side, ref in enumerate((east_ref, north_ref))
    ]
    copies.append(
        pltpu.make_async_copy(own_ref.at[pl.ds(begin, HALO)], sent_ref.at[:HALO], copied)
    )
    for copy in copies:
        copy.start()
    winds = []
    for side in range(2):
        copies[side].wait()
        wind = winds_ref[side].astype(F32)
        wind = jnp.where(band == 0, wind[rows - wind_halo :], wind[:wind_halo])
        winds += [wind[:, :LANES], wind[:, LANES:]]
    sent_ref[HALO:] = jnp.concatenate(winds, axis=0).reshape(-1, sent_ref.shape[1], LANES)
    copies[2].wait()


def info_kernel(sizes, sent_ref, index_ref, value_ref, scale_ref, info_ref, ints_ref, floats_ref, copied):
    rows, members, devices = sizes
    own_rows = rows // devices
    copies = [
        pltpu.make_async_copy(index_ref, ints_ref, copied.at[0]),
        pltpu.make_async_copy(value_ref, floats_ref.at[0], copied.at[1]),
        pltpu.make_async_copy(scale_ref, floats_ref.at[1], copied.at[2]),
    ]
    for copy in copies:
        copy.start()
    for copy in copies:
        copy.wait()
    edges = []
    for array in (ints_ref[...].astype(F32), floats_ref[0], floats_ref[1]):
        edges += [array[:1], array[own_rows - 1 :]]
    edges.append(jnp.zeros((info_ref.shape[1] - len(edges), LANES), F32))
    told = jnp.concatenate(edges, axis=0)
    info_ref[...] = jnp.broadcast_to(told[None], info_ref.shape)


def stage_kernel(sizes, flags_ref, own_ref, parts_ref):
    rows, members, devices = sizes
    band = flags_ref[0]
    matrix = parts_matrix()
    block = 4 * CHUNK

    def stage(index, _):
        base = index * block

        def row_of(k):
            return jnp.where(band == 0, base + k, rows - 1 - base - k)

        def load(row, lane):
            return own_ref[row, pl.ds(lane, members, stride=4), :]

        stage_states(load, row_of, block, members, matrix, parts_ref, base)
        return 0

    lax.fori_loop(0, rows // block, stage, 0)


def forecast_kernel(
    sizes,
    flags_ref,
    own_ref,
    halo_ref,
    east_ref,
    north_ref,
    out_ref,
    edges_ref,
    w_ref,
    q_ref,
    *stage_refs,
):
    rows, members, devices = sizes
    own_rows = rows // devices
    band = flags_ref[0]
    matrix = parts_matrix()
    north_sign = jnp.where(band == 0, F32(-0.25), F32(0.25))
    wind_halo = -(-HALO // CHUNK) * CHUNK
    pair = 2 * members

    zero_rows = jnp.zeros((4, PAD, members, LANES), F32)
    for ref in (q_ref, *stage_refs):
        ref[:, :PAD] = zero_rows
    stage_winds(
        east_ref[...],
        north_ref[...],
        north_sign,
        matrix,
        w_ref,
        jnp.where(band == 0, 0, wind_halo),
    )
    halo_winds = halo_ref[HALO:].reshape(4 * wind_halo, LANES).astype(BF16)
    halo_winds = [halo_winds[k * wind_halo : (k + 1) * wind_halo] for k in range(4)]
    stage_winds(
        jnp.concatenate(halo_winds[:2], axis=1),
        jnp.concatenate(halo_winds[2:], axis=1),
        north_sign,
        matrix,
        w_ref,
        jnp.where(band == 0, rows, 0),
    )

    q_ref[:, PAD : PAD + rows] = own_ref[...]

    def row_of(k):
        row = min(k, HALO - 1)
        return jnp.where(band == 0, row, HALO - 1 - row)

    def load(row, lane):
        return halo_ref[row, pl.ds(lane, members, stride=4), :]

    stage_states(load, row_of, wind_halo, members, matrix, q_ref, PAD + rows)

    def wind_row(row):
        return jnp.where(band == 0, row, rows + wind_halo - 1 - row)

    def step(_, carry):
        rk_passes(q_ref, stage_refs, PAD, w_ref, wind_row, 0, rows + HALO - 1, BLOCK)
        return carry

    lax.fori_loop(0, STEPS, step, 0)

    def state(row):
        return [q_ref[part, PAD + row] for part in range(4)]

    def emit(group, _):
        first = group * own_rows
        place = group_place(sizes, band, group)
        for j in range(0, own_rows, 2):
            low, high = state(first + j), state(first + j + 1)
            for part in range(4):
                start = (part * own_rows + j) * members
                out_ref[place, pl.ds(start, pair), :] = pack_pair(
                    encode(low[part]), encode(high[part])
                )
        for side, row in enumerate((jnp.maximum(first - 1, 0), first + own_rows)):
            for part, values in enumerate(state(row)):
                edges_ref[place, 4 * side + part] = values
        return 0

    lax.fori_loop(0, devices, emit, 0)


def observe_kernel(sizes, flags_ref, edges_ref, coded_ref, table_ref, out_ref):
    rows, members, devices = sizes
    band = flags_ref[0]
    coded_rows = coded_ref.shape[1]
    out_ref[:, :coded_rows] = coded_ref[...]

    def emit(group, _):
        place = group_place(sizes, band, group)
        values = []
        for side in range(2):
            index = beside_info(table_ref, sizes, band, group, side == 1, 0)
            index = jnp.broadcast_to(index, (members, LANES)).astype(jnp.int32)
            states = [edges_ref[place, 4 * side + part] for part in range(4)]
            values.append(encode(pick_lanes(states, index)))
        out_ref[place, pl.ds(coded_rows, 2 * members), :] = pack_pair(*values)
        return 0

    lax.fori_loop(0, devices, emit, 0, unroll=4)


def split_value(value):
    high = value.astype(BF16)
    return high, (value - high.astype(F32)).astype(BF16)


def product(left, right):
    (left_high, left_low), (right_high, right_low) = left, right
    size = right_high.shape[1]
    both = jnp.dot(
        jnp.concatenate([left_high, left_low], axis=1),
        jnp.concatenate(
            [
                jnp.concatenate([right_high, right_low], axis=1),
                jnp.concatenate([right_high, jnp.zeros_like(right_low)], axis=1),
            ],
            axis=0,
        ),
        preferred_element_type=F32,
    )
    return both[:, :size] + both[:, size:]


def analysis_kernel(
    sizes,
    flags_ref,
    got_ref,
    table_ref,
    index_ref,
    value_ref,
    scale_ref,
    out_ref,
    states_ref,
    upper_ref,
    upper_low_ref,
    lower_ref,
    lower_low_ref,
):
    rows, members, devices = sizes
    own_rows = rows // devices
    total = members * devices
    band = flags_ref[0]
    group = group_place(sizes, band, flags_ref[1])
    pair = 2 * members
    beside_start = 4 * own_rows * members

    def pair_at(start):
        both = decode(got_ref[:, pl.ds(start, pair), :].astype(jnp.int32).astype(F32))
        both = both.reshape(devices, 2, members, LANES)
        return both[:, 0].reshape(total, LANES), both[:, 1].reshape(total, LANES)

    def info(ref, j):
        return ref[pl.ds(jnp.where(band == 0, j, own_rows - 1 - j), 1), :]

    picked_rows = [None] * (own_rows + 2)
    picked_rows[0], picked_rows[own_rows + 1] = pair_at(beside_start)
    for j in range(0, own_rows, 2):
        parts = [pair_at((part * own_rows + j) * members) for part in range(4)]
        for k in range(2):
            states_ref[j + k] = jnp.concatenate([part[k] for part in parts], axis=1)
            index = jnp.broadcast_to(info(index_ref, j + k), (total, LANES)).astype(jnp.int32)
            picked_rows[j + k + 1] = pick_lanes([part[k] for part in parts], index)

    grams = []
    couplings = []
    for j in range(-1, own_rows + 1):
        if 0 <= j < own_rows:
            value, scale = info(value_ref, j), info(scale_ref, j)
        else:
            value, scale = [
                beside_info(table_ref, sizes, band, group, j == own_rows, kind) for kind in (1, 2)
            ]
        if j == -1:
            scale = jnp.where(group == 0, 0.0, scale)
        picked = picked_rows[j + 1]
        average = jnp.mean(picked, axis=0, keepdims=True)
        spread = ((picked - average) * scale / math.sqrt(total - 1)).astype(BF16)
        innovation = jnp.broadcast_to((value - average) * scale, (16, LANES)).astype(BF16)
        contract = (((1,), (1,)), ((), ()))
        grams.append(lax.dot_general(spread, spread, contract, preferred_element_type=F32))
        couplings.append(
            lax.dot_general(innovation, spread, contract, preferred_element_type=F32)
        )

    row_ids = lax.broadcasted_iota(jnp.int32, (total, total), 0)
    column_ids = lax.broadcasted_iota(jnp.int32, (total, total), 1)
    diagonal = row_ids == column_ids
    identity = jnp.where(diagonal, F32(1.0), F32(0.0))

    def put(high_ref, low_ref, j, value):
        high_ref[j], low_ref[j] = split_value(value)

    traces = []
    for j in range(own_rows):
        system = identity + 3.0 * grams[j + 1] + grams[j] + grams[j + 2]
        trace = jnp.sum(
            jnp.sum(jnp.where(diagonal, system, 0.0), axis=0, keepdims=True),
            axis=1,
            keepdims=True,
        )
        traces.append(trace)
        scaled = system / trace
        factor = split_value(1.5 * identity - 0.5 * scaled)
        put(upper_ref, upper_low_ref, j, product(split_value(scaled), factor))
        lower_ref[j], lower_low_ref[j] = factor

    def factor_of(j):
        lower = lower_ref[j], lower_low_ref[j]
        upper = upper_ref[j], upper_low_ref[j]
        return lower, upper, split_value(1.5 * identity - 0.5 * product(lower, upper))

    def newton(turn, _):
        parts = [factor_of(j) for j in range(own_rows)]
        for j in range(own_rows):
            lower, upper, factor = parts[j]
            put(upper_ref, upper_low_ref, j, product(upper, factor))
            put(lower_ref, lower_low_ref, j, product(factor, lower))
        return 0

    lax.fori_loop(0, ITERS - 2, newton, 0)

    parts = [factor_of(j) for j in range(own_rows)]
    weights = []
    for j in range(own_rows):
        lower, upper, factor = parts[j]
        inv_root = product(factor, lower) / jnp.sqrt(traces[j])
        coupling = 3.0 * couplings[j + 1] + couplings[j] + couplings[j + 2]
        root_parts = split_value(inv_root)
        half_step = product(split_value(coupling), root_parts)
        mean_weight = product(split_value(half_step), root_parts)[:1] / math.sqrt(total - 1)
        weights.append(split_value(inv_root + mean_weight))

    for j in range(0, own_rows, 2):
        for part in range(4):
            place = (part * own_rows + j) * members
            moved = []
            for k in range(2):
                state = states_ref[j + k, :, part * LANES : (part + 1) * LANES]
                center = jnp.mean(state, axis=0, keepdims=True)
                high, low = split_value(state - center)
                weights_high, weights_low = weights[j + k]
                result = center + (
                    jnp.dot(weights_high, high, preferred_element_type=F32)
                    + jnp.dot(weights_high, low, preferred_element_type=F32)
                    + jnp.dot(weights_low, high, preferred_element_type=F32)
                )
                moved.append(result.reshape(devices, members, LANES))
            out_ref[:, pl.ds(place, pair), :] = jnp.concatenate(moved, axis=1).astype(BF16)


def unpack_kernel(sizes, flags_ref, got_ref, out_ref):
    rows, members, devices = sizes
    own_rows = rows // devices
    band = flags_ref[0]
    matrix = parts_matrix(from_parts=True)

    batch = 4

    def place(index, _):
        device = index * batch
        parts = jnp.concatenate(
            [
                jnp.concatenate(
                    [
                        got_ref[device + d, pl.ds(part * own_rows * members, own_rows * members), :]
                        for d in range(batch)
                    ],
                    axis=0,
                )
                for part in range(4)
            ],
            axis=1,
        )
        joined = jnp.dot(parts, matrix, preferred_element_type=F32)
        for k in range(batch * own_rows):
            row = device * own_rows + k
            if own_rows > 1:
                flipped = (device + k // own_rows) * own_rows + own_rows - 1 - k % own_rows
                row = jnp.where(band == 0, row, flipped)
            values = joined[k * members : (k + 1) * members]
            for field in range(2):
                for half in range(2):
                    first = (2 * field + half) * LANES
                    out_ref[row, pl.ds(2 * half + field, members, stride=4), :] = values[
                        :, first : first + LANES
                    ]
        return 0

    lax.fori_loop(0, devices // batch, place, 0)


def per_device_pair(background, wind_east, wind_north, obs_index, obs_value, obs_scale):
    rows, members, fields, width = background.shape
    devices = lax.axis_size("mem")
    bands = lax.axis_size("lat")
    own_rows = rows // devices
    total = members * devices
    sizes = (rows, members, devices)
    band = lax.axis_index("lat")
    flags = jnp.stack([band, lax.axis_index("mem")]).astype(jnp.int32)
    smem = pl.BlockSpec(memory_space=pltpu.SMEM)
    vmem = pl.BlockSpec(memory_space=pltpu.VMEM)
    params = pltpu.CompilerParams(vmem_limit_bytes=40 * 1024 * 1024)

    def cost(microseconds):
        return pl.CostEstimate(
            flops=0, bytes_accessed=int(microseconds * 3_000_000), transcendentals=0
        )

    grouped = members * fields * 2
    own = background.reshape(rows, members, fields, 2, LANES)
    own = own.transpose(0, 1, 3, 2, 4).reshape(rows, grouped, LANES)

    wind_halo = -(-HALO // CHUNK) * CHUNK
    hbm = pl.BlockSpec(memory_space=pltpu.HBM)
    dma = pltpu.SemaphoreType.DMA
    sent = pl.pallas_call(
        functools.partial(halo_kernel, sizes),
        out_shape=jax.ShapeDtypeStruct((HALO + 4 * wind_halo // grouped, grouped, LANES), F32),
        in_specs=[smem, hbm, hbm, hbm],
        out_specs=vmem,
        scratch_shapes=[pltpu.VMEM((2, rows, width), BF16), dma, dma((2,))],
        compiler_params=params,
        cost_estimate=cost(1),
        name="halo_rows",
    )(flags, own, wind_east, wind_north)
    halo = lax.ppermute(sent, "lat", [(0, 1), (1, 0)])
    staged = pl.pallas_call(
        functools.partial(stage_kernel, sizes),
        out_shape=jax.ShapeDtypeStruct((4, rows, members, LANES), F32),
        in_specs=[smem, vmem],
        out_specs=vmem,
        compiler_params=params,
        cost_estimate=cost(2),
        name="stage",
    )(flags, own)
    observations = [
        array.reshape(own_rows, NOBS) for array in (obs_index, obs_value, obs_scale)
    ]
    info = pl.pallas_call(
        functools.partial(info_kernel, sizes),
        out_shape=jax.ShapeDtypeStruct((bands * devices, CHUNK, LANES), F32),
        in_specs=[pl.BlockSpec(memory_space=pl.ANY)] + [hbm] * 3,
        out_specs=vmem,
        scratch_shapes=[
            pltpu.VMEM((own_rows, LANES), jnp.int32),
            pltpu.VMEM((2, own_rows, LANES), F32),
            dma((3,)),
        ],
        compiler_params=params,
        cost_estimate=cost(1),
        name="info_rows",
    )(
        staged,
        *observations,
    )
    table = lax.all_to_all(info, ("lat", "mem"), split_axis=0, concat_axis=0, tiled=True)

    per_target = (4 * own_rows + 2) * members
    wind_rows = pltpu.VMEM((8, rows + wind_halo, members, LANES), F32)
    field_rows = pltpu.VMEM((4, PAD + rows + wind_halo, members, LANES), F32)
    coded, edges = pl.pallas_call(
        functools.partial(forecast_kernel, sizes),
        out_shape=(
            jax.ShapeDtypeStruct((devices, 4 * own_rows * members, LANES), jnp.int16),
            jax.ShapeDtypeStruct((devices, 8, members, LANES), F32),
        ),
        in_specs=[smem] + [vmem] * 4,
        out_specs=(vmem, vmem),
        scratch_shapes=[wind_rows] + [field_rows] * 4,
        compiler_params=params,
        cost_estimate=cost(12),
        name="forecast",
    )(flags, staged, halo, wind_east, wind_north)
    packed = pl.pallas_call(
        functools.partial(observe_kernel, sizes),
        out_shape=jax.ShapeDtypeStruct((devices, per_target, LANES), jnp.int16),
        in_specs=[smem] + [vmem] * 3,
        out_specs=vmem,
        compiler_params=params,
        cost_estimate=cost(1),
        name="observe",
    )(flags, edges, coded, table)
    got = lax.all_to_all(packed, "mem", split_axis=0, concat_axis=0, tiled=True)
    half_matrix = pltpu.VMEM((own_rows, total, total), BF16)
    back = pl.pallas_call(
        functools.partial(analysis_kernel, sizes),
        out_shape=jax.ShapeDtypeStruct((devices, 4 * own_rows * members, LANES), BF16),
        in_specs=[smem] + [vmem] * 5,
        out_specs=vmem,
        scratch_shapes=[pltpu.VMEM((own_rows, total, 4 * LANES), F32)] + [half_matrix] * 4,
        compiler_params=params,
        cost_estimate=cost(12),
        name="analysis",
    )(flags, got, table, *observations)
    returned = lax.all_to_all(back, "mem", split_axis=0, concat_axis=0, tiled=True)
    result = pl.pallas_call(
        functools.partial(unpack_kernel, sizes),
        out_shape=jax.ShapeDtypeStruct((rows, grouped, LANES), F32),
        in_specs=[smem, vmem],
        out_specs=vmem,
        compiler_params=params,
        cost_estimate=cost(2),
        name="unpack",
    )(flags, returned)
    result = result.reshape(rows, members, 2, fields, LANES).transpose(0, 1, 3, 2, 4)
    return result.reshape(rows, members, fields, width)


def per_device(background, wind_east, wind_north, obs_index, obs_value, obs_scale):
    rows, members, fields, width = background.shape
    devices = lax.axis_size("mem")
    fits = (
        lax.axis_size("lat") == 2
        and members == 8
        and members * devices == LANES
        and fields == 2
        and width == 2 * LANES == PW
        and obs_index.shape[2:] == (1, LANES)
        and rows % (4 * CHUNK) == 0
        and devices % 4 == 0
        and 4 * STEPS % (rows // devices) == 0
        and (rows // devices) % 2 == 0
        and rows >= 8 * STEPS
    )
    run = per_device_pair if fits else per_device_any
    return run(background, wind_east, wind_north, obs_index, obs_value, obs_scale)


def solution(mesh):
    in_specs = (
        P("lat", "mem", None, None),
        P("lat", None),
        P("lat", None),
        P("lat", "mem", None, None),
        P("lat", "mem", None, None),
        P("lat", "mem", None, None),
    )
    out_specs = P("lat", "mem", None, None)
    return jax.shard_map(
        per_device, mesh=mesh, in_specs=in_specs, out_specs=out_specs, check_vma=False
    )
```

```python
import functools
import math

import jax
import jax.numpy as jnp
from jax import lax
from jax.experimental import pallas as pl
from jax.experimental.pallas import tpu as pltpu
from jax.sharding import PartitionSpec as P

PW = 256
NOBS = 128
STEPS = 4
ITERS = 12
LANES = 128
HALO = 4 * STEPS + 1
CHUNK = 8

HIGHEST = lax.Precision.HIGHEST
F32 = jnp.float32
BF16 = jnp.bfloat16


def padded_2(block, sides, width, periodic):
    for axis, dim in sides:
        count = lax.axis_size(axis)
        forward = [(i, i + 1) for i in range(count - 1)]
        if periodic:
            forward.append((count - 1, 0))
        backward = [(target, source) for source, target in forward]
        low = lax.ppermute(
            lax.slice_in_dim(block, block.shape[dim] - width, None, axis=dim), axis, forward
        )
        high = lax.ppermute(lax.slice_in_dim(block, 0, width, axis=dim), axis, backward)
        block = jnp.concatenate([low, block, high], axis=dim)
    return block


def tendency(padded, circumpolar_wind_speed, poleward_wind_speed):
    center_rows = padded[1:-1]
    along_diff = jnp.roll(center_rows, -1, axis=-1) - jnp.roll(center_rows, 1, axis=-1)
    across_diff = padded[2:] - padded[:-2]
    return -0.5 * (circumpolar_wind_speed * along_diff + poleward_wind_speed * across_diff)


def make_blocks(model_variables, index_rows, value_rows, scale_rows):
    row_count, members, flat_width = model_variables.shape
    patch_count = index_rows.shape[1]
    obs_count = index_rows.shape[2]
    fields = flat_width // (patch_count * PW)
    patch_values = model_variables.reshape(row_count, members, fields, patch_count, PW)
    value_ids = lax.broadcasted_iota(jnp.int32, (fields * PW, 1), 0)
    selector = (value_ids[None, None] == index_rows[:, :, None, :]).astype(jnp.float32)
    selector = selector.reshape(row_count, patch_count, fields, PW, obs_count)
    picked = jnp.einsum("akfpt,apftj->akpj", patch_values, selector, precision=HIGHEST)
    average = jnp.mean(picked, axis=1)
    spread = (picked - average[:, None]) * scale_rows[:, None] / math.sqrt(members - 1)
    innovation = (value_rows - average) * scale_rows
    return jnp.concatenate([spread, innovation[:, None]], axis=1).astype(jnp.bfloat16)


def edge_pair(extended):
    return jnp.stack([extended[-1], extended[0]])


def rows_beside(local_rows, extended, banded):
    position = lax.axis_index("mem")
    last_index = lax.axis_size("mem") - 1
    upper_rim = jnp.where(position == 0, banded[0], extended[0])
    lower_rim = jnp.where(position == last_index, banded[3], extended[-1])
    upper_adjacent = jnp.concatenate([upper_rim[None], local_rows[:-1]], axis=0)
    bottom_adjacent = jnp.concatenate([local_rows[1:], lower_rim[None]], axis=0)
    return (upper_adjacent, bottom_adjacent)


def per_device_any(background, wind_east, wind_north, obs_index, obs_value, obs_scale):
    current = background
    stacked_winds = jnp.stack([wind_east, wind_north])
    wide_winds = padded_2(stacked_winds, (("lat", 1),), 3, False).astype(jnp.float32)
    east_wide = wide_winds[0][:, None, None, :]
    north_wide = wide_winds[1][:, None, None, :]
    span = east_wide.shape[0]
    for step_index in range(STEPS):
        extended = padded_2(current, (("lat", 0),), 4, False)
        slope_one = tendency(extended, east_wide, north_wide)
        slope_two = tendency(
            extended[1:-1] + 0.5 * slope_one, east_wide[1 : span - 1], north_wide[1 : span - 1]
        )
        slope_three = tendency(
            extended[2:-2] + 0.5 * slope_two, east_wide[2 : span - 2], north_wide[2 : span - 2]
        )
        slope_four = tendency(
            extended[3:-3] + slope_three, east_wide[3 : span - 3], north_wide[3 : span - 3]
        )
        current = (
            extended[4:-4]
            + (slope_one[3:-3] + 2.0 * slope_two[2:-2] + 2.0 * slope_three[1:-1] + slope_four) / 6.0
        )
    points = lax.all_to_all(current, "mem", split_axis=0, concat_axis=1, tiled=True)
    row_count, members, fields, width = points.shape
    patch_count = obs_index.shape[2]
    model_variables = points.reshape(row_count, members, fields * width)
    index_rows = obs_index.reshape(row_count, patch_count, NOBS)
    value_rows = obs_value.reshape(row_count, patch_count, NOBS)
    scale_rows = obs_scale.reshape(row_count, patch_count, NOBS)
    own_block = make_blocks(model_variables, index_rows, value_rows, scale_rows)
    extended = padded_2(own_block, (("mem", 0),), 1, True)
    banded = padded_2(edge_pair(extended), (("lat", 0),), 1, False)
    upper_adjacent, bottom_adjacent = rows_beside(own_block, extended, banded)
    gram_sum = jnp.zeros((row_count, patch_count, members + 1, members + 1), jnp.float32)
    for neighbor_block in (
        own_block,
        jnp.roll(own_block, -1, axis=2),
        jnp.roll(own_block, 1, axis=2),
        upper_adjacent,
        bottom_adjacent,
    ):
        gram_sum = gram_sum + jnp.einsum(
            "akpj,alpj->apkl", neighbor_block, neighbor_block, preferred_element_type=jnp.float32
        )
    identity = jnp.eye(members, dtype=jnp.float32)
    system = identity + gram_sum[:, :, :members, :members]
    coupling = gram_sum[:, :, :members, members]
    trace_sum = jnp.trace(system, axis1=2, axis2=3)
    scaled = system / trace_sum[:, :, None, None]

    def newton(turn_index, carry):
        upper_iter, lower_iter = carry
        factor = 1.5 * identity - 0.5 * jnp.einsum(
            "apij,apjk->apik", lower_iter, upper_iter, precision=HIGHEST
        )
        return (
            jnp.einsum("apij,apjk->apik", upper_iter, factor, precision=HIGHEST),
            jnp.einsum("apij,apjk->apik", factor, lower_iter, precision=HIGHEST),
        )

    start_lower = jnp.broadcast_to(identity, scaled.shape)
    upper_iter, lower_iter = lax.fori_loop(0, ITERS, newton, (scaled, start_lower))
    inv_root = lower_iter / jnp.sqrt(trace_sum)[:, :, None, None]
    half_step = jnp.einsum("apkl,apl->apk", inv_root, coupling, precision=HIGHEST)
    mean_weight = jnp.einsum("apkl,apl->apk", inv_root, half_step, precision=HIGHEST) / math.sqrt(
        members - 1
    )
    weights = mean_weight[:, :, :, None] + inv_root
    patch_values = points.reshape(row_count, members, fields, patch_count, PW)
    center = jnp.mean(patch_values, axis=1)
    result = center[:, None] + jnp.einsum(
        "akfpt,apki->aifpt", patch_values - center[:, None], weights, precision=HIGHEST
    )
    analysis = result.reshape(row_count, members, fields, width)
    return lax.all_to_all(analysis, "mem", split_axis=1, concat_axis=0, tiled=True)


PAD = 8
TURNS = 4
FINEST = 0.05
LARGEST = 16.0 * sum(1.8**power / math.factorial(power) for power in range(5)) ** STEPS
STATE_LEVELS = 2047.0
WIND_LEVELS = 32767.0
VALUE_LEVELS = 8191.0
SCALE_LEVELS = 4095.0
STEEPNESS = 32766.0 / math.log(1.0 + LARGEST / FINEST)


def take_lanes(values, lanes):
    return jnp.take_along_axis(values, lanes, axis=1, mode="promise_in_bounds")


def pick_lanes(states, index):
    field = jnp.right_shift(index, 8)
    lanes = jnp.bitwise_and(jnp.right_shift(index, 1), LANES - 2) + field
    is_odd = jnp.bitwise_and(index, 1) == 1
    is_late = jnp.bitwise_and(index, 2) == 2
    picks = [take_lanes(state, lanes) for state in states]
    return jnp.where(
        is_odd, jnp.where(is_late, picks[3], picks[1]), jnp.where(is_late, picks[2], picks[0])
    )


def group_place(sizes, band, group):
    return jnp.where(band == 0, group, sizes[2] - 1 - group)


def beside_rows(table_ref, sizes, band, group, is_after):
    devices = sizes[2]
    near = group + 1 if is_after else jnp.maximum(group - 1, 0)
    over = near == devices
    place = jnp.where(over, jnp.where(band == 0, 0, devices - 1), group_place(sizes, band, near))
    near_band = jnp.where(over, 1 - band, band)
    last = jnp.where(band == 0, 0, 1) if is_after else jnp.where(band == 0, 1, 0)
    return near_band * devices + place, last


def beside_index(table_ref, sizes, band, group, is_after):
    place, last = beside_rows(table_ref, sizes, band, group, is_after)
    return jnp.bitwise_and(table_ref[place, pl.ds(last, 1), :], 65535)


def beside_observation(table_ref, sizes, band, group, is_after):
    place, last = beside_rows(table_ref, sizes, band, group, is_after)
    value = jnp.right_shift(table_ref[place, pl.ds(last, 1), :], 16)
    scales = table_ref[place, 2:3, :]
    scale = jnp.where(last == 1, jnp.right_shift(scales, 16), jnp.bitwise_and(scales, 65535))
    return value.astype(F32) * F32(1.0 / VALUE_LEVELS), scale.astype(F32) * F32(1.0 / SCALE_LEVELS)


def parts_matrix(from_parts=False):
    shape = (4 * LANES, 4 * LANES)
    rows = lax.broadcasted_iota(jnp.int32, shape, 0)
    columns = lax.broadcasted_iota(jnp.int32, shape, 1)
    column, plain = (rows, columns) if from_parts else (columns, rows)
    lane = jnp.bitwise_and(column, LANES - 1)
    wanted = (
        jnp.bitwise_and(lane, 1) * (2 * LANES)
        + jnp.right_shift(lane, 1) * 4
        + jnp.right_shift(column, 7)
    )
    return jnp.where(plain == wanted, F32(1.0), F32(0.0)).astype(BF16)


def stage_states(load, row_of, count, members, matrix, q_ref, start):
    left = jnp.concatenate(
        [
            jnp.concatenate([load(row_of(k), 2 * half + field) for k in range(count)], axis=0)
            for field in range(2)
            for half in range(2)
        ],
        axis=1,
    )
    first = left.astype(BF16)
    left = left - first.astype(F32)
    second = left.astype(BF16)
    third = (left - second.astype(F32)).astype(BF16)
    size = count * members
    split = jnp.dot(
        jnp.concatenate([first, second, third], axis=0), matrix, preferred_element_type=F32
    )
    split = split[:size] + (split[size : 2 * size] + split[2 * size :])
    for part in range(4):
        values = split[:, part * LANES : (part + 1) * LANES]
        q_ref[part, pl.ds(start, count)] = values.reshape(count, members, LANES)


def stage_winds(east, north, north_sign, matrix, w_ref, start):
    count = east.shape[0]
    for side, (wind, sign) in enumerate(((east, F32(-0.25)), (north, north_sign))):
        both = jnp.concatenate([wind, wind], axis=1)
        split = jnp.dot(both, matrix, preferred_element_type=F32) * sign
        for part in range(4):
            lanes = split[:, part * LANES : (part + 1) * LANES]
            wide = jnp.broadcast_to(lanes[:, None, :], (count, w_ref.shape[2], LANES))
            w_ref[4 * side + part, pl.ds(start, count)] = wide


def rk_passes(q_ref, stage_refs, offset, w_ref, wind_row, first, count, block):
    a_ref, b_ref, c_ref = stage_refs

    def finish_one(part, at, half):
        a_ref[part, at] = q_ref[part, at] + half

    def finish_two(part, at, half):
        b_ref[part, at] = q_ref[part, at] + half

    def finish_three(part, at, half):
        c_ref[part, at] = q_ref[part, at] + (half + half)

    def finish_four(part, at, half):
        doubled = b_ref[part, at]
        gathered = (a_ref[part, at] + c_ref[part, at] - q_ref[part, at]) + (doubled + doubled)
        q_ref[part, at] = (gathered + half) * F32(1.0 / 3.0)

    for stage, finish in (
        (q_ref, finish_one),
        (a_ref, finish_two),
        (b_ref, finish_three),
        (c_ref, finish_four),
    ):

        def turn(index, _):
            base = first + index * block + offset
            states = [[stage[part, base + k - 1] for k in range(block + 2)] for part in range(4)]
            for k in range(1, block + 1):
                place = wind_row(base - offset + k - 1)
                here = [states[part][k] for part in range(4)]
                along = (
                    here[1] - pltpu.roll(here[3], 2, 1),
                    here[2] - here[0],
                    here[3] - here[1],
                    pltpu.roll(here[0], LANES - 2, 1) - here[2],
                )
                for part in range(4):
                    across = states[part][k + 1] - states[part][k - 1]
                    half = w_ref[part, place] * along[part] + w_ref[4 + part, place] * across
                    finish(part, base + k - 1, half)
            return 0

        turns = -(-count // block)
        if turns == 1:
            turn(0, 0)
        else:
            lax.fori_loop(0, turns, turn, 0)


def encode(value):
    level = jnp.round(jnp.log(1.0 + jnp.abs(value) * F32(1.0 / FINEST)) * F32(STEEPNESS))
    return jnp.where(value < 0.0, -level, level)


def decode(code):
    size = (jnp.exp(jnp.abs(code) * F32(1.0 / STEEPNESS)) - 1.0) * F32(FINEST)
    return jnp.where(code < 0.0, -size, size)


def pack_pair(low, high):
    return jnp.concatenate([low, high], axis=0).astype(jnp.int32).astype(jnp.int16)


def tell_kernel(
    sizes,
    own_ref,
    east_ref,
    north_ref,
    index_ref,
    value_ref,
    scale_ref,
    sent_ref,
    told_ref,
    edge_ref,
    winds_ref,
    ints_ref,
    floats_ref,
    copied,
):
    rows, members, devices = sizes
    own_rows = rows // devices
    band = lax.axis_index("lat")
    wind_halo = -(-HALO // CHUNK) * CHUNK
    begin = jnp.where(band == 0, rows - HALO, 0)
    pairs = (
        (own_ref.at[pl.ds(begin, HALO)], edge_ref),
        (east_ref, winds_ref.at[0]),
        (north_ref, winds_ref.at[1]),
        (index_ref, ints_ref),
        (value_ref, floats_ref.at[0]),
        (scale_ref, floats_ref.at[1]),
    )
    copies = [
        pltpu.make_async_copy(source, target, copied.at[turn])
        for turn, (source, target) in enumerate(pairs)
    ]
    for copy in copies:
        copy.start()
    for copy in copies[1:]:
        copy.wait()
    winds = []
    for side in range(2):
        wind = winds_ref[side].astype(F32) * F32(WIND_LEVELS)
        wind = jnp.where(band == 0, wind[rows - wind_halo :], wind[:wind_halo])
        winds += [wind[:, :LANES], wind[:, LANES:]]
    winds = jnp.round(jnp.concatenate(winds, axis=0)).astype(jnp.int32).astype(jnp.int16)
    sent_ref[HALO:] = winds.reshape(-1, sent_ref.shape[1], LANES)
    values = jnp.round(floats_ref[0] * F32(VALUE_LEVELS)).astype(jnp.int32)
    scales = jnp.round(floats_ref[1] * F32(SCALE_LEVELS)).astype(jnp.int32)
    pairs = ints_ref[...] + values * 65536
    ends = [row[end : end + 1] for row in (pairs, scales) for end in (0, own_rows - 1)]
    told = jnp.concatenate(ends[:2] + [ends[2] + ends[3] * 65536, jnp.zeros_like(ends[0])], axis=0)
    told_ref[...] = jnp.broadcast_to(told[None], told_ref.shape)
    copies[0].wait()
    edge = jnp.round(edge_ref[...] * F32(STATE_LEVELS))
    sent_ref[:HALO] = edge.astype(jnp.int32).astype(jnp.int16)


def stage_kernel(sizes, own_ref, parts_ref):
    rows, members, devices = sizes
    band = lax.axis_index("lat")
    matrix = parts_matrix()
    block = 4 * CHUNK

    def stage(index, _):
        base = index * block

        def row_of(k):
            return jnp.where(band == 0, base + k, rows - 1 - base - k)

        def load(row, lane):
            return own_ref[row, pl.ds(lane, members, stride=4), :]

        stage_states(load, row_of, block, members, matrix, parts_ref, base)
        return 0

    lax.fori_loop(0, rows // block, stage, 0)


def forecast_kernel(
    sizes,
    own_ref,
    halo_ref,
    east_ref,
    north_ref,
    out_ref,
    edges_ref,
    edge_ref,
    w_ref,
    q_ref,
    *stage_refs,
):
    rows, members, devices = sizes
    own_rows = rows // devices
    band = lax.axis_index("lat")
    matrix = parts_matrix()
    north_sign = jnp.where(band == 0, F32(-0.25), F32(0.25))
    wind_halo = -(-HALO // CHUNK) * CHUNK
    pair = 2 * members

    zero_rows = jnp.zeros((4, PAD, members, LANES), F32)
    for ref in (q_ref, *stage_refs):
        ref[:, :PAD] = zero_rows
    stage_winds(
        east_ref[...],
        north_ref[...],
        north_sign,
        matrix,
        w_ref,
        jnp.where(band == 0, 0, wind_halo),
    )
    edge_ref[...] = halo_ref[:HALO].astype(jnp.int32).astype(F32) * F32(1.0 / STATE_LEVELS)
    halo_winds = halo_ref[HALO:].astype(jnp.int32).astype(F32).reshape(4 * wind_halo, LANES)
    halo_winds = (halo_winds * F32(1.0 / WIND_LEVELS)).astype(BF16)
    halo_winds = [halo_winds[k * wind_halo : (k + 1) * wind_halo] for k in range(4)]
    stage_winds(
        jnp.concatenate(halo_winds[:2], axis=1),
        jnp.concatenate(halo_winds[2:], axis=1),
        north_sign,
        matrix,
        w_ref,
        jnp.where(band == 0, rows, 0),
    )

    q_ref[:, PAD : PAD + rows] = own_ref[...]

    def row_of(k):
        row = min(k, HALO - 1)
        return jnp.where(band == 0, row, HALO - 1 - row)

    def load(row, lane):
        return edge_ref[row, pl.ds(lane, members, stride=4), :]

    stage_states(load, row_of, wind_halo, members, matrix, q_ref, PAD + rows)

    def wind_row(row):
        return jnp.where(band == 0, row, rows + wind_halo - 1 - row)

    for step in range(STEPS):
        count = rows + HALO - 1 - 4 * step
        rk_passes(q_ref, stage_refs, PAD, w_ref, wind_row, 0, count, -(-count // TURNS))

    def state(row):
        return [q_ref[part, PAD + row] for part in range(4)]

    def emit(group, _):
        first = group * own_rows
        place = group_place(sizes, band, group)
        for j in range(0, own_rows, 2):
            low, high = state(first + j), state(first + j + 1)
            for part in range(4):
                start = (part * own_rows + j) * members
                out_ref[place, pl.ds(start, pair), :] = pack_pair(
                    encode(low[part]), encode(high[part])
                )
        for side, row in enumerate((jnp.maximum(first - 1, 0), first + own_rows)):
            for part, values in enumerate(state(row)):
                edges_ref[place, 4 * side + part] = values
        return 0

    lax.fori_loop(0, devices, emit, 0)


def observe_kernel(sizes, edges_ref, coded_ref, table_ref, out_ref):
    rows, members, devices = sizes
    band = lax.axis_index("lat")
    coded_rows = coded_ref.shape[1]
    out_ref[:, :coded_rows] = coded_ref[...]

    def emit(group, _):
        place = group_place(sizes, band, group)
        values = []
        for side in range(2):
            index = beside_index(table_ref, sizes, band, group, side == 1)
            index = jnp.broadcast_to(index, (members, LANES))
            states = [edges_ref[place, 4 * side + part] for part in range(4)]
            values.append(encode(pick_lanes(states, index)))
        out_ref[place, pl.ds(coded_rows, 2 * members), :] = pack_pair(*values)
        return 0

    lax.fori_loop(0, devices, emit, 0, unroll=4)


def split_value(value):
    high = value.astype(BF16)
    return high, (value - high.astype(F32)).astype(BF16)


def product(left, right):
    (left_high, left_low), (right_high, right_low) = left, right
    size = right_high.shape[1]
    both = jnp.dot(
        jnp.concatenate([left_high, left_low], axis=1),
        jnp.concatenate(
            [
                jnp.concatenate([right_high, right_low], axis=1),
                jnp.concatenate([right_high, jnp.zeros_like(right_low)], axis=1),
            ],
            axis=0,
        ),
        preferred_element_type=F32,
    )
    return both[:, :size] + both[:, size:]


def analysis_kernel(
    sizes,
    got_ref,
    table_ref,
    index_ref,
    value_ref,
    scale_ref,
    out_ref,
    states_ref,
    upper_ref,
    upper_low_ref,
    lower_ref,
    lower_low_ref,
):
    rows, members, devices = sizes
    own_rows = rows // devices
    total = members * devices
    band = lax.axis_index("lat")
    group = group_place(sizes, band, lax.axis_index("mem"))
    pair = 2 * members
    beside_start = 4 * own_rows * members

    def pair_at(start):
        both = decode(got_ref[:, pl.ds(start, pair), :].astype(jnp.int32).astype(F32))
        both = both.reshape(devices, 2, members, LANES)
        return both[:, 0].reshape(total, LANES), both[:, 1].reshape(total, LANES)

    def info(ref, j):
        return ref[pl.ds(jnp.where(band == 0, j, own_rows - 1 - j), 1), :]

    picked_rows = [None] * (own_rows + 2)
    picked_rows[0], picked_rows[own_rows + 1] = pair_at(beside_start)
    for j in range(0, own_rows, 2):
        parts = [pair_at((part * own_rows + j) * members) for part in range(4)]
        for k in range(2):
            states_ref[j + k] = jnp.concatenate([part[k] for part in parts], axis=1)
            index = jnp.broadcast_to(info(index_ref, j + k), (total, LANES)).astype(jnp.int32)
            picked_rows[j + k + 1] = pick_lanes([part[k] for part in parts], index)

    grams = []
    couplings = []
    for j in range(-1, own_rows + 1):
        if 0 <= j < own_rows:
            value, scale = info(value_ref, j), info(scale_ref, j)
        else:
            value, scale = beside_observation(table_ref, sizes, band, group, j == own_rows)
        if j == -1:
            scale = jnp.where(group == 0, 0.0, scale)
        picked = picked_rows[j + 1]
        average = jnp.mean(picked, axis=0, keepdims=True)
        spread = ((picked - average) * scale / math.sqrt(total - 1)).astype(BF16)
        innovation = jnp.broadcast_to((value - average) * scale, (16, LANES)).astype(BF16)
        contract = (((1,), (1,)), ((), ()))
        grams.append(lax.dot_general(spread, spread, contract, preferred_element_type=F32))
        couplings.append(
            lax.dot_general(innovation, spread, contract, preferred_element_type=F32)
        )

    row_ids = lax.broadcasted_iota(jnp.int32, (total, total), 0)
    column_ids = lax.broadcasted_iota(jnp.int32, (total, total), 1)
    diagonal = row_ids == column_ids
    identity = jnp.where(diagonal, F32(1.0), F32(0.0))

    def put(high_ref, low_ref, j, value):
        high_ref[j], low_ref[j] = split_value(value)

    traces = []
    for j in range(own_rows):
        system = identity + 3.0 * grams[j + 1] + grams[j] + grams[j + 2]
        trace = jnp.sum(
            jnp.sum(jnp.where(diagonal, system, 0.0), axis=0, keepdims=True),
            axis=1,
            keepdims=True,
        )
        traces.append(trace)
        scaled = system / trace
        factor = split_value(1.5 * identity - 0.5 * scaled)
        put(upper_ref, upper_low_ref, j, product(split_value(scaled), factor))
        lower_ref[j], lower_low_ref[j] = factor

    def factor_of(j):
        lower = lower_ref[j], lower_low_ref[j]
        upper = upper_ref[j], upper_low_ref[j]
        return lower, upper, split_value(1.5 * identity - 0.5 * product(lower, upper))

    def newton(turn, _):
        parts = [factor_of(j) for j in range(own_rows)]
        for j in range(own_rows):
            lower, upper, factor = parts[j]
            put(upper_ref, upper_low_ref, j, product(upper, factor))
            put(lower_ref, lower_low_ref, j, product(factor, lower))
        return 0

    lax.fori_loop(0, ITERS - 2, newton, 0)

    parts = [factor_of(j) for j in range(own_rows)]
    weights = []
    for j in range(own_rows):
        lower, upper, factor = parts[j]
        inv_root = product(factor, lower) / jnp.sqrt(traces[j])
        coupling = 3.0 * couplings[j + 1] + couplings[j] + couplings[j + 2]
        root_parts = split_value(inv_root)
        half_step = product(split_value(coupling), root_parts)
        mean_weight = product(split_value(half_step), root_parts)[:1] / math.sqrt(total - 1)
        weights.append(split_value(inv_root + mean_weight))

    for j in range(0, own_rows, 2):
        for part in range(4):
            place = (part * own_rows + j) * members
            moved = []
            for k in range(2):
                state = states_ref[j + k, :, part * LANES : (part + 1) * LANES]
                center = jnp.mean(state, axis=0, keepdims=True)
                high, low = split_value(state - center)
                weights_high, weights_low = weights[j + k]
                result = center + (
                    jnp.dot(weights_high, high, preferred_element_type=F32)
                    + jnp.dot(weights_high, low, preferred_element_type=F32)
                    + jnp.dot(weights_low, high, preferred_element_type=F32)
                )
                moved.append(result.reshape(devices, members, LANES))
            out_ref[:, pl.ds(place, pair), :] = jnp.concatenate(moved, axis=1).astype(BF16)


def unpack_kernel(sizes, got_ref, out_ref):
    rows, members, devices = sizes
    own_rows = rows // devices
    band = lax.axis_index("lat")
    matrix = parts_matrix(from_parts=True)

    batch = devices

    def place(index, _):
        device = index * batch
        parts = jnp.concatenate(
            [
                jnp.concatenate(
                    [
                        got_ref[device + d, pl.ds(part * own_rows * members, own_rows * members), :]
                        for d in range(batch)
                    ],
                    axis=0,
                )
                for part in range(4)
            ],
            axis=1,
        )
        joined = jnp.dot(parts, matrix, preferred_element_type=F32)
        for k in range(batch * own_rows):
            row = device * own_rows + k
            if own_rows > 1:
                flipped = (device + k // own_rows) * own_rows + own_rows - 1 - k % own_rows
                row = jnp.where(band == 0, row, flipped)
            values = joined[k * members : (k + 1) * members]
            for field in range(2):
                for half in range(2):
                    first = (2 * field + half) * LANES
                    out_ref[row, pl.ds(2 * half + field, members, stride=4), :] = values[
                        :, first : first + LANES
                    ]
        return 0

    lax.fori_loop(0, devices // batch, place, 0)


def per_device_pair(background, wind_east, wind_north, obs_index, obs_value, obs_scale):
    rows, members, fields, width = background.shape
    devices = lax.axis_size("mem")
    bands = lax.axis_size("lat")
    own_rows = rows // devices
    total = members * devices
    sizes = (rows, members, devices)
    vmem = pl.BlockSpec(memory_space=pltpu.VMEM)
    params = pltpu.CompilerParams(vmem_limit_bytes=40 * 1024 * 1024)
    whole = pltpu.CompilerParams(vmem_limit_bytes=127 * 512 * 1024)

    def cost(microseconds):
        return pl.CostEstimate(
            flops=0, bytes_accessed=int(microseconds * 3_000_000), transcendentals=0
        )

    grouped = members * fields * 2
    own = background.reshape(rows, members, fields, 2, LANES)
    own = own.transpose(0, 1, 3, 2, 4).reshape(rows, grouped, LANES)

    wind_halo = -(-HALO // CHUNK) * CHUNK
    hbm = pl.BlockSpec(memory_space=pltpu.HBM)
    dma = pltpu.SemaphoreType.DMA
    observations = [
        array.reshape(own_rows, NOBS) for array in (obs_index, obs_value, obs_scale)
    ]
    edge_rows = pltpu.VMEM((HALO, grouped, LANES), F32)
    sent, told = pl.pallas_call(
        functools.partial(tell_kernel, sizes),
        out_shape=(
            jax.ShapeDtypeStruct((HALO + 4 * wind_halo // grouped, grouped, LANES), jnp.int16),
            jax.ShapeDtypeStruct((bands * devices, 4, LANES), jnp.int32),
        ),
        in_specs=[hbm] * 6,
        out_specs=(vmem, vmem),
        scratch_shapes=[
            edge_rows,
            pltpu.VMEM((2, rows, width), BF16),
            pltpu.VMEM((own_rows, LANES), jnp.int32),
            pltpu.VMEM((2, own_rows, LANES), F32),
            dma((6,)),
        ],
        compiler_params=whole,
        cost_estimate=cost(1),
        name="tell",
    )(own, wind_east, wind_north, *observations)
    halo = lax.ppermute(sent, "lat", [(0, 1), (1, 0)])
    table = lax.all_to_all(told, ("lat", "mem"), split_axis=0, concat_axis=0, tiled=True)
    staged = pl.pallas_call(
        functools.partial(stage_kernel, sizes),
        out_shape=jax.ShapeDtypeStruct((4, rows, members, LANES), F32),
        in_specs=[vmem],
        out_specs=vmem,
        compiler_params=params,
        cost_estimate=cost(2),
        name="stage",
    )(own)

    per_target = (4 * own_rows + 2) * members
    wind_rows = pltpu.VMEM((8, rows + wind_halo, members, LANES), F32)
    field_rows = pltpu.VMEM((4, PAD + rows + wind_halo, members, LANES), F32)
    coded, edges = pl.pallas_call(
        functools.partial(forecast_kernel, sizes),
        out_shape=(
            jax.ShapeDtypeStruct((devices, 4 * own_rows * members, LANES), jnp.int16),
            jax.ShapeDtypeStruct((devices, 8, members, LANES), F32),
        ),
        in_specs=[vmem] * 4,
        out_specs=(vmem, vmem),
        scratch_shapes=[edge_rows, wind_rows] + [field_rows] * 4,
        compiler_params=params,
        cost_estimate=cost(12),
        name="forecast",
    )(staged, halo, wind_east, wind_north)
    packed = pl.pallas_call(
        functools.partial(observe_kernel, sizes),
        out_shape=jax.ShapeDtypeStruct((devices, per_target, LANES), jnp.int16),
        in_specs=[vmem] * 3,
        out_specs=vmem,
        compiler_params=params,
        cost_estimate=cost(1),
        name="observe",
    )(edges, coded, table)
    got = lax.all_to_all(packed, "mem", split_axis=0, concat_axis=0, tiled=True)
    half_matrix = pltpu.VMEM((own_rows, total, total), BF16)
    back = pl.pallas_call(
        functools.partial(analysis_kernel, sizes),
        out_shape=jax.ShapeDtypeStruct((devices, 4 * own_rows * members, LANES), BF16),
        in_specs=[vmem] * 5,
        out_specs=vmem,
        scratch_shapes=[pltpu.VMEM((own_rows, total, 4 * LANES), F32)] + [half_matrix] * 4,
        compiler_params=params,
        cost_estimate=cost(12),
        name="analysis",
    )(got, table, *observations)
    returned = lax.all_to_all(back, "mem", split_axis=0, concat_axis=0, tiled=True)
    result = pl.pallas_call(
        functools.partial(unpack_kernel, sizes),
        out_shape=jax.ShapeDtypeStruct((rows, grouped, LANES), F32),
        in_specs=[vmem],
        out_specs=vmem,
        compiler_params=params,
        cost_estimate=cost(2),
        name="unpack",
    )(returned)
    result = result.reshape(rows, members, 2, fields, LANES).transpose(0, 1, 3, 2, 4)
    return result.reshape(rows, members, fields, width)


def per_device(background, wind_east, wind_north, obs_index, obs_value, obs_scale):
    rows, members, fields, width = background.shape
    devices = lax.axis_size("mem")
    fits = (
        lax.axis_size("lat") == 2
        and members == 8
        and members * devices == LANES
        and fields == 2
        and width == 2 * LANES == PW
        and obs_index.shape[2:] == (1, LANES)
        and rows % (4 * CHUNK) == 0
        and 4 * STEPS % (rows // devices) == 0
        and (rows // devices) % 2 == 0
        and rows >= 8 * STEPS
    )
    run = per_device_pair if fits else per_device_any
    return run(background, wind_east, wind_north, obs_index, obs_value, obs_scale)


def solution(mesh):
    in_specs = (
        P("lat", "mem", None, None),
        P("lat", None),
        P("lat", None),
        P("lat", "mem", None, None),
        P("lat", "mem", None, None),
        P("lat", "mem", None, None),
    )
    out_specs = P("lat", "mem", None, None)
    return jax.shard_map(
        per_device, mesh=mesh, in_specs=in_specs, out_specs=out_specs, check_vma=False
    )
```

```python
import functools
import math

import jax
import jax.numpy as jnp
from jax import lax
from jax.experimental import pallas as pl
from jax.experimental.pallas import tpu as pltpu
from jax.sharding import PartitionSpec as P

PW = 256
NOBS = 128
STEPS = 4
ITERS = 12
LANES = 128
HALO = 4 * STEPS + 1
CHUNK = 8

HIGHEST = lax.Precision.HIGHEST
F32 = jnp.float32
BF16 = jnp.bfloat16


def padded_2(block, sides, width, periodic):
    for axis, dim in sides:
        count = lax.axis_size(axis)
        forward = [(i, i + 1) for i in range(count - 1)]
        if periodic:
            forward.append((count - 1, 0))
        backward = [(target, source) for source, target in forward]
        low = lax.ppermute(
            lax.slice_in_dim(block, block.shape[dim] - width, None, axis=dim), axis, forward
        )
        high = lax.ppermute(lax.slice_in_dim(block, 0, width, axis=dim), axis, backward)
        block = jnp.concatenate([low, block, high], axis=dim)
    return block


def tendency(padded, circumpolar_wind_speed, poleward_wind_speed):
    center_rows = padded[1:-1]
    along_diff = jnp.roll(center_rows, -1, axis=-1) - jnp.roll(center_rows, 1, axis=-1)
    across_diff = padded[2:] - padded[:-2]
    return -0.5 * (circumpolar_wind_speed * along_diff + poleward_wind_speed * across_diff)


def make_blocks(model_variables, index_rows, value_rows, scale_rows):
    row_count, members, flat_width = model_variables.shape
    patch_count = index_rows.shape[1]
    obs_count = index_rows.shape[2]
    fields = flat_width // (patch_count * PW)
    patch_values = model_variables.reshape(row_count, members, fields, patch_count, PW)
    value_ids = lax.broadcasted_iota(jnp.int32, (fields * PW, 1), 0)
    selector = (value_ids[None, None] == index_rows[:, :, None, :]).astype(jnp.float32)
    selector = selector.reshape(row_count, patch_count, fields, PW, obs_count)
    picked = jnp.einsum("akfpt,apftj->akpj", patch_values, selector, precision=HIGHEST)
    average = jnp.mean(picked, axis=1)
    spread = (picked - average[:, None]) * scale_rows[:, None] / math.sqrt(members - 1)
    innovation = (value_rows - average) * scale_rows
    return jnp.concatenate([spread, innovation[:, None]], axis=1).astype(jnp.bfloat16)


def edge_pair(extended):
    return jnp.stack([extended[-1], extended[0]])


def rows_beside(local_rows, extended, banded):
    position = lax.axis_index("mem")
    last_index = lax.axis_size("mem") - 1
    upper_rim = jnp.where(position == 0, banded[0], extended[0])
    lower_rim = jnp.where(position == last_index, banded[3], extended[-1])
    upper_adjacent = jnp.concatenate([upper_rim[None], local_rows[:-1]], axis=0)
    bottom_adjacent = jnp.concatenate([local_rows[1:], lower_rim[None]], axis=0)
    return (upper_adjacent, bottom_adjacent)


def per_device_any(background, wind_east, wind_north, obs_index, obs_value, obs_scale):
    current = background
    stacked_winds = jnp.stack([wind_east, wind_north])
    wide_winds = padded_2(stacked_winds, (("lat", 1),), 3, False).astype(jnp.float32)
    east_wide = wide_winds[0][:, None, None, :]
    north_wide = wide_winds[1][:, None, None, :]
    span = east_wide.shape[0]
    for step_index in range(STEPS):
        extended = padded_2(current, (("lat", 0),), 4, False)
        slope_one = tendency(extended, east_wide, north_wide)
        slope_two = tendency(
            extended[1:-1] + 0.5 * slope_one, east_wide[1 : span - 1], north_wide[1 : span - 1]
        )
        slope_three = tendency(
            extended[2:-2] + 0.5 * slope_two, east_wide[2 : span - 2], north_wide[2 : span - 2]
        )
        slope_four = tendency(
            extended[3:-3] + slope_three, east_wide[3 : span - 3], north_wide[3 : span - 3]
        )
        current = (
            extended[4:-4]
            + (slope_one[3:-3] + 2.0 * slope_two[2:-2] + 2.0 * slope_three[1:-1] + slope_four) / 6.0
        )
    points = lax.all_to_all(current, "mem", split_axis=0, concat_axis=1, tiled=True)
    row_count, members, fields, width = points.shape
    patch_count = obs_index.shape[2]
    model_variables = points.reshape(row_count, members, fields * width)
    index_rows = obs_index.reshape(row_count, patch_count, NOBS)
    value_rows = obs_value.reshape(row_count, patch_count, NOBS)
    scale_rows = obs_scale.reshape(row_count, patch_count, NOBS)
    own_block = make_blocks(model_variables, index_rows, value_rows, scale_rows)
    extended = padded_2(own_block, (("mem", 0),), 1, True)
    banded = padded_2(edge_pair(extended), (("lat", 0),), 1, False)
    upper_adjacent, bottom_adjacent = rows_beside(own_block, extended, banded)
    gram_sum = jnp.zeros((row_count, patch_count, members + 1, members + 1), jnp.float32)
    for neighbor_block in (
        own_block,
        jnp.roll(own_block, -1, axis=2),
        jnp.roll(own_block, 1, axis=2),
        upper_adjacent,
        bottom_adjacent,
    ):
        gram_sum = gram_sum + jnp.einsum(
            "akpj,alpj->apkl", neighbor_block, neighbor_block, preferred_element_type=jnp.float32
        )
    identity = jnp.eye(members, dtype=jnp.float32)
    system = identity + gram_sum[:, :, :members, :members]
    coupling = gram_sum[:, :, :members, members]
    trace_sum = jnp.trace(system, axis1=2, axis2=3)
    scaled = system / trace_sum[:, :, None, None]

    def newton(turn_index, carry):
        upper_iter, lower_iter = carry
        factor = 1.5 * identity - 0.5 * jnp.einsum(
            "apij,apjk->apik", lower_iter, upper_iter, precision=HIGHEST
        )
        return (
            jnp.einsum("apij,apjk->apik", upper_iter, factor, precision=HIGHEST),
            jnp.einsum("apij,apjk->apik", factor, lower_iter, precision=HIGHEST),
        )

    start_lower = jnp.broadcast_to(identity, scaled.shape)
    upper_iter, lower_iter = lax.fori_loop(0, ITERS, newton, (scaled, start_lower))
    inv_root = lower_iter / jnp.sqrt(trace_sum)[:, :, None, None]
    half_step = jnp.einsum("apkl,apl->apk", inv_root, coupling, precision=HIGHEST)
    mean_weight = jnp.einsum("apkl,apl->apk", inv_root, half_step, precision=HIGHEST) / math.sqrt(
        members - 1
    )
    weights = mean_weight[:, :, :, None] + inv_root
    patch_values = points.reshape(row_count, members, fields, patch_count, PW)
    center = jnp.mean(patch_values, axis=1)
    result = center[:, None] + jnp.einsum(
        "akfpt,apki->aifpt", patch_values - center[:, None], weights, precision=HIGHEST
    )
    analysis = result.reshape(row_count, members, fields, width)
    return lax.all_to_all(analysis, "mem", split_axis=1, concat_axis=0, tiled=True)


PAD = 8
TURNS = 2
FINEST = 0.05
LARGEST = 16.0 * sum(1.8**power / math.factorial(power) for power in range(5)) ** STEPS
STATE_LEVELS = 2047.0
WIND_LEVELS = 32767.0
VALUE_LEVELS = 8191.0
SCALE_LEVELS = 4095.0
STEEPNESS = 32766.0 / math.log(1.0 + LARGEST / FINEST)


def take_lanes(values, lanes):
    return jnp.take_along_axis(values, lanes, axis=1, mode="promise_in_bounds")


def pick_lanes(states, index):
    field = jnp.right_shift(index, 8)
    lanes = jnp.bitwise_and(jnp.right_shift(index, 1), LANES - 2) + field
    is_odd = jnp.bitwise_and(index, 1) == 1
    is_late = jnp.bitwise_and(index, 2) == 2
    picks = [take_lanes(state, lanes) for state in states]
    return jnp.where(
        is_odd, jnp.where(is_late, picks[3], picks[1]), jnp.where(is_late, picks[2], picks[0])
    )


def group_place(sizes, band, group):
    return jnp.where(band == 0, group, sizes[2] - 1 - group)


def beside_rows(table_ref, sizes, band, group, is_after):
    devices = sizes[2]
    near = group + 1 if is_after else jnp.maximum(group - 1, 0)
    over = near == devices
    place = jnp.where(over, jnp.where(band == 0, 0, devices - 1), group_place(sizes, band, near))
    near_band = jnp.where(over, 1 - band, band)
    last = jnp.where(band == 0, 0, 1) if is_after else jnp.where(band == 0, 1, 0)
    return near_band * devices + place, last


def beside_index(table_ref, sizes, band, group, is_after):
    place, last = beside_rows(table_ref, sizes, band, group, is_after)
    return jnp.bitwise_and(table_ref[place, pl.ds(last, 1), :], 65535)


def beside_observation(table_ref, sizes, band, group, is_after):
    place, last = beside_rows(table_ref, sizes, band, group, is_after)
    value = jnp.right_shift(table_ref[place, pl.ds(last, 1), :], 16)
    scales = table_ref[place, 2:3, :]
    scale = jnp.where(last == 1, jnp.right_shift(scales, 16), jnp.bitwise_and(scales, 65535))
    return value.astype(F32) * F32(1.0 / VALUE_LEVELS), scale.astype(F32) * F32(1.0 / SCALE_LEVELS)


def parts_matrix(from_parts=False):
    shape = (4 * LANES, 4 * LANES)
    rows = lax.broadcasted_iota(jnp.int32, shape, 0)
    columns = lax.broadcasted_iota(jnp.int32, shape, 1)
    column, plain = (rows, columns) if from_parts else (columns, rows)
    lane = jnp.bitwise_and(column, LANES - 1)
    wanted = (
        jnp.bitwise_and(lane, 1) * (2 * LANES)
        + jnp.right_shift(lane, 1) * 4
        + jnp.right_shift(column, 7)
    )
    return jnp.where(plain == wanted, F32(1.0), F32(0.0)).astype(BF16)


def stage_states(load, row_of, count, members, matrix, q_ref, start):
    left = jnp.concatenate(
        [
            jnp.concatenate([load(row_of(k), 2 * half + field) for k in range(count)], axis=0)
            for field in range(2)
            for half in range(2)
        ],
        axis=1,
    )
    first = left.astype(BF16)
    left = left - first.astype(F32)
    second = left.astype(BF16)
    third = (left - second.astype(F32)).astype(BF16)
    size = count * members
    split = jnp.dot(
        jnp.concatenate([first, second, third], axis=0), matrix, preferred_element_type=F32
    )
    split = split[:size] + (split[size : 2 * size] + split[2 * size :])
    for part in range(4):
        values = split[:, part * LANES : (part + 1) * LANES]
        q_ref[part, pl.ds(start, count)] = values.reshape(count, members, LANES)


def stage_winds(east, north, north_sign, matrix, w_ref, start):
    count = east.shape[0]
    for side, (wind, sign) in enumerate(((east, F32(-0.25)), (north, north_sign))):
        both = jnp.concatenate([wind, wind], axis=1)
        split = jnp.dot(both, matrix, preferred_element_type=F32) * sign
        for part in range(4):
            lanes = split[:, part * LANES : (part + 1) * LANES]
            wide = jnp.broadcast_to(lanes[:, None, :], (count, w_ref.shape[2], LANES))
            w_ref[4 * side + part, pl.ds(start, count)] = wide


def rk_passes(q_ref, stage_refs, offset, w_ref, wind_row, first, count, block):
    a_ref, b_ref, c_ref = stage_refs

    def finish_one(part, at, half):
        a_ref[part, at] = q_ref[part, at] + half

    def finish_two(part, at, half):
        b_ref[part, at] = q_ref[part, at] + half

    def finish_three(part, at, half):
        c_ref[part, at] = q_ref[part, at] + (half + half)

    def finish_four(part, at, half):
        doubled = b_ref[part, at]
        gathered = (a_ref[part, at] + c_ref[part, at] - q_ref[part, at]) + (doubled + doubled)
        q_ref[part, at] = (gathered + half) * F32(1.0 / 3.0)

    for stage, finish in (
        (q_ref, finish_one),
        (a_ref, finish_two),
        (b_ref, finish_three),
        (c_ref, finish_four),
    ):

        def turn(index, _):
            base = first + index * block + offset

            def load(k):
                return [stage[part, base + k - 1] for part in range(4)]

            before, here = load(0), load(1)
            for k in range(1, block + 1):
                after = load(k + 1)
                place = wind_row(base - offset + k - 1)
                along = (
                    here[1] - pltpu.roll(here[3], 2, 1),
                    here[2] - here[0],
                    here[3] - here[1],
                    pltpu.roll(here[0], LANES - 2, 1) - here[2],
                )
                for part in range(4):
                    across = after[part] - before[part]
                    half = w_ref[part, place] * along[part] + w_ref[4 + part, place] * across
                    finish(part, base + k - 1, half)
                before, here = here, after
            return 0

        turns = -(-count // block)
        if turns == 1:
            turn(0, 0)
        else:
            lax.fori_loop(0, turns, turn, 0)


def encode(value):
    level = jnp.round(jnp.log(1.0 + jnp.abs(value) * F32(1.0 / FINEST)) * F32(STEEPNESS))
    return jnp.where(value < 0.0, -level, level)


def decode(code):
    size = (jnp.exp(jnp.abs(code) * F32(1.0 / STEEPNESS)) - 1.0) * F32(FINEST)
    return jnp.where(code < 0.0, -size, size)


def pack_pair(low, high):
    return jnp.concatenate([low, high], axis=0).astype(jnp.int32).astype(jnp.int16)


def tell_kernel(
    sizes,
    own_ref,
    east_ref,
    north_ref,
    index_ref,
    value_ref,
    scale_ref,
    sent_ref,
    told_ref,
    edge_ref,
    winds_ref,
    ints_ref,
    floats_ref,
    copied,
):
    rows, members, devices = sizes
    own_rows = rows // devices
    band = lax.axis_index("lat")
    wind_halo = -(-HALO // CHUNK) * CHUNK
    begin = jnp.where(band == 0, rows - HALO, 0)
    pairs = (
        (own_ref.at[pl.ds(begin, HALO)], edge_ref),
        (east_ref, winds_ref.at[0]),
        (north_ref, winds_ref.at[1]),
        (index_ref, ints_ref),
        (value_ref, floats_ref.at[0]),
        (scale_ref, floats_ref.at[1]),
    )
    copies = [
        pltpu.make_async_copy(source, target, copied.at[turn])
        for turn, (source, target) in enumerate(pairs)
    ]
    for copy in copies:
        copy.start()
    for copy in copies[1:]:
        copy.wait()
    winds = []
    for side in range(2):
        wind = winds_ref[side].astype(F32) * F32(WIND_LEVELS)
        wind = jnp.where(band == 0, wind[rows - wind_halo :], wind[:wind_halo])
        winds += [wind[:, :LANES], wind[:, LANES:]]
    winds = jnp.round(jnp.concatenate(winds, axis=0)).astype(jnp.int32).astype(jnp.int16)
    sent_ref[HALO:] = winds.reshape(-1, sent_ref.shape[1], LANES)
    values = jnp.round(floats_ref[0] * F32(VALUE_LEVELS)).astype(jnp.int32)
    scales = jnp.round(floats_ref[1] * F32(SCALE_LEVELS)).astype(jnp.int32)
    pairs = ints_ref[...] + values * 65536
    ends = [row[end : end + 1] for row in (pairs, scales) for end in (0, own_rows - 1)]
    told = jnp.concatenate(ends[:2] + [ends[2] + ends[3] * 65536, jnp.zeros_like(ends[0])], axis=0)
    told_ref[...] = jnp.broadcast_to(told[None], told_ref.shape)
    copies[0].wait()
    edge = jnp.round(edge_ref[...] * F32(STATE_LEVELS))
    sent_ref[:HALO] = edge.astype(jnp.int32).astype(jnp.int16)


def stage_kernel(sizes, own_ref, parts_ref):
    rows, members, devices = sizes
    band = lax.axis_index("lat")
    matrix = parts_matrix()
    block = 4 * CHUNK

    def stage(index, _):
        base = index * block

        def row_of(k):
            return jnp.where(band == 0, base + k, rows - 1 - base - k)

        def load(row, lane):
            return own_ref[row, pl.ds(lane, members, stride=4), :]

        stage_states(load, row_of, block, members, matrix, parts_ref, base)
        return 0

    lax.fori_loop(0, rows // block, stage, 0)


def forecast_kernel(
    sizes,
    own_ref,
    halo_ref,
    east_ref,
    north_ref,
    out_ref,
    edges_ref,
    edge_ref,
    w_ref,
    q_ref,
    *stage_refs,
):
    rows, members, devices = sizes
    own_rows = rows // devices
    band = lax.axis_index("lat")
    matrix = parts_matrix()
    north_sign = jnp.where(band == 0, F32(-0.25), F32(0.25))
    wind_halo = -(-HALO // CHUNK) * CHUNK
    pair = 2 * members

    zero_rows = jnp.zeros((4, PAD, members, LANES), F32)
    for ref in (q_ref, *stage_refs):
        ref[:, :PAD] = zero_rows
    stage_winds(
        east_ref[...],
        north_ref[...],
        north_sign,
        matrix,
        w_ref,
        jnp.where(band == 0, 0, wind_halo),
    )
    edge_ref[...] = halo_ref[:HALO].astype(jnp.int32).astype(F32) * F32(1.0 / STATE_LEVELS)
    halo_winds = halo_ref[HALO:].astype(jnp.int32).astype(F32).reshape(4 * wind_halo, LANES)
    halo_winds = (halo_winds * F32(1.0 / WIND_LEVELS)).astype(BF16)
    halo_winds = [halo_winds[k * wind_halo : (k + 1) * wind_halo] for k in range(4)]
    stage_winds(
        jnp.concatenate(halo_winds[:2], axis=1),
        jnp.concatenate(halo_winds[2:], axis=1),
        north_sign,
        matrix,
        w_ref,
        jnp.where(band == 0, rows, 0),
    )

    q_ref[:, PAD : PAD + rows] = own_ref[...]

    def row_of(k):
        row = min(k, HALO - 1)
        return jnp.where(band == 0, row, HALO - 1 - row)

    def load(row, lane):
        return edge_ref[row, pl.ds(lane, members, stride=4), :]

    stage_states(load, row_of, wind_halo, members, matrix, q_ref, PAD + rows)

    def wind_row(row):
        return jnp.where(band == 0, row, rows + wind_halo - 1 - row)

    for step in range(STEPS):
        count = rows + HALO - 1 - 4 * step
        rk_passes(q_ref, stage_refs, PAD, w_ref, wind_row, 0, count, -(-count // TURNS))

    def state(row):
        return [q_ref[part, PAD + row] for part in range(4)]

    def emit(group, _):
        first = group * own_rows
        place = group_place(sizes, band, group)
        for j in range(0, own_rows, 2):
            low, high = state(first + j), state(first + j + 1)
            for part in range(4):
                start = (part * own_rows + j) * members
                out_ref[place, pl.ds(start, pair), :] = pack_pair(
                    encode(low[part]), encode(high[part])
                )
        for side, row in enumerate((jnp.maximum(first - 1, 0), first + own_rows)):
            for part, values in enumerate(state(row)):
                edges_ref[place, 4 * side + part] = values
        return 0

    lax.fori_loop(0, devices, emit, 0, unroll=4)


def observe_kernel(sizes, edges_ref, coded_ref, table_ref, out_ref):
    rows, members, devices = sizes
    band = lax.axis_index("lat")
    coded_rows = coded_ref.shape[1]
    out_ref[:, :coded_rows] = coded_ref[...]

    def emit(group, _):
        place = group_place(sizes, band, group)
        values = []
        for side in range(2):
            index = beside_index(table_ref, sizes, band, group, side == 1)
            index = jnp.broadcast_to(index, (members, LANES))
            states = [edges_ref[place, 4 * side + part] for part in range(4)]
            values.append(encode(pick_lanes(states, index)))
        out_ref[place, pl.ds(coded_rows, 2 * members), :] = pack_pair(*values)
        return 0

    lax.fori_loop(0, devices, emit, 0, unroll=4)


def split_value(value):
    high = value.astype(BF16)
    return high, (value - high.astype(F32)).astype(BF16)


def product(left, right):
    (left_high, left_low), (right_high, right_low) = left, right
    size = right_high.shape[1]
    both = jnp.dot(
        jnp.concatenate([left_high, left_low], axis=1),
        jnp.concatenate(
            [
                jnp.concatenate([right_high, right_low], axis=1),
                jnp.concatenate([right_high, jnp.zeros_like(right_low)], axis=1),
            ],
            axis=0,
        ),
        preferred_element_type=F32,
    )
    return both[:, :size] + both[:, size:]


def analysis_kernel(
    sizes,
    got_ref,
    table_ref,
    index_ref,
    value_ref,
    scale_ref,
    out_ref,
    states_ref,
    center_ref,
    high_ref,
    low_ref,
    *iterates,
):
    rows, members, devices = sizes
    own_rows = rows // devices
    total = members * devices
    band = lax.axis_index("lat")
    group = group_place(sizes, band, lax.axis_index("mem"))
    pair = 2 * members
    beside_start = 4 * own_rows * members

    def pair_at(start):
        both = decode(got_ref[:, pl.ds(start, pair), :].astype(jnp.int32).astype(F32))
        both = both.reshape(devices, 2, members, LANES)
        return both[:, 0].reshape(total, LANES), both[:, 1].reshape(total, LANES)

    def info(ref, j):
        return ref[pl.ds(jnp.where(band == 0, j, own_rows - 1 - j), 1), :]

    picked_rows = [None] * (own_rows + 2)
    picked_rows[0], picked_rows[own_rows + 1] = pair_at(beside_start)
    for j in range(0, own_rows, 2):
        parts = [pair_at((part * own_rows + j) * members) for part in range(4)]
        for k in range(2):
            for part in range(4):
                states_ref[4 * (j + k) + part] = parts[part][k]
            index = jnp.broadcast_to(info(index_ref, j + k), (total, LANES)).astype(jnp.int32)
            picked_rows[j + k + 1] = pick_lanes([part[k] for part in parts], index)

    grams = []
    couplings = []
    for j in range(-1, own_rows + 1):
        if 0 <= j < own_rows:
            value, scale = info(value_ref, j), info(scale_ref, j)
        else:
            value, scale = beside_observation(table_ref, sizes, band, group, j == own_rows)
        if j == -1:
            scale = jnp.where(group == 0, 0.0, scale)
        picked = picked_rows[j + 1]
        average = jnp.mean(picked, axis=0, keepdims=True)
        spread = ((picked - average) * scale / math.sqrt(total - 1)).astype(BF16)
        innovation = jnp.broadcast_to((value - average) * scale, (16, LANES)).astype(BF16)
        contract = (((1,), (1,)), ((), ()))
        grams.append(lax.dot_general(spread, spread, contract, preferred_element_type=F32))
        couplings.append(
            lax.dot_general(innovation, spread, contract, preferred_element_type=F32)
        )

    row_ids = lax.broadcasted_iota(jnp.int32, (total, total), 0)
    column_ids = lax.broadcasted_iota(jnp.int32, (total, total), 1)
    diagonal = row_ids == column_ids
    identity = jnp.where(diagonal, F32(1.0), F32(0.0))

    def put(refs, j, value):
        refs[0][j], refs[1][j] = split_value(value)

    upper_refs, lower_refs = iterates[:2], iterates[2:]
    traces = []
    for j in range(own_rows):
        system = identity + 3.0 * grams[j + 1] + grams[j] + grams[j + 2]
        trace = jnp.sum(
            jnp.sum(jnp.where(diagonal, system, 0.0), axis=0, keepdims=True),
            axis=1,
            keepdims=True,
        )
        traces.append(trace)
        scaled = system / trace
        factor = 1.5 * identity - 0.5 * scaled
        put(upper_refs, j, product(split_value(scaled), split_value(factor)))
        put(lower_refs, j, factor)

    def factor_of(j):
        lower, upper = lower_refs, upper_refs
        lower, upper = (lower[0][j], lower[1][j]), (upper[0][j], upper[1][j])
        return lower, upper, split_value(1.5 * identity - 0.5 * product(lower, upper))

    per_turn = -(-4 * own_rows // (ITERS - 2))

    def newton(turn, _):
        for k in range(per_turn):
            entry = jnp.minimum(turn * per_turn + k, 4 * own_rows - 1)
            state = states_ref[entry]
            center = jnp.mean(state, axis=0, keepdims=True)
            center_ref[entry] = jnp.broadcast_to(center, (8, LANES))
            high_ref[entry], low_ref[entry] = split_value(state - center)
        parts = [factor_of(j) for j in range(own_rows)]
        for j in range(own_rows):
            lower, upper, factor = parts[j]
            put(upper_refs, j, product(upper, factor))
            put(lower_refs, j, product(factor, lower))
        return 0

    lax.fori_loop(0, ITERS - 2, newton, 0)

    def joined(ref, j):
        return jnp.concatenate([ref[4 * j + part] for part in range(4)], axis=1)

    parts = [factor_of(j) for j in range(own_rows)]
    roots = [
        split_value(product(parts[j][2], parts[j][0]) / jnp.sqrt(traces[j]))
        for j in range(own_rows)
    ]
    half_steps = []
    for j in range(own_rows):
        coupling = 3.0 * couplings[j + 1] + couplings[j] + couplings[j + 2]
        half_steps.append(product(split_value(coupling), roots[j]))
    spreads = [
        jnp.dot(roots[j][0], joined(high_ref, j), preferred_element_type=F32)
        for j in range(own_rows)
    ]
    results = []
    for j in range(own_rows):
        mean_weight = product(split_value(half_steps[j]), roots[j]) / math.sqrt(total - 1)
        high, low = split_value(mean_weight[:8])
        moved = jnp.dot(
            jnp.concatenate([high, low], axis=0), joined(high_ref, j), preferred_element_type=F32
        )
        rest = jnp.dot(
            jnp.concatenate([high, low], axis=0), joined(low_ref, j), preferred_element_type=F32
        )
        center = joined(center_ref, j)[:1]
        results.append(spreads[j] + (center + (moved[:1] + moved[8:9]) + rest[:1]))
    for j in range(0, own_rows, 2):
        for part in range(4):
            both = [
                results[k][:, part * LANES : (part + 1) * LANES].reshape(devices, members, LANES)
                for k in (j, j + 1)
            ]
            out_ref[:, pl.ds((part * own_rows + j) * members, pair), :] = jnp.concatenate(
                both, axis=1
            ).astype(BF16)


def unpack_kernel(sizes, got_ref, out_ref):
    rows, members, devices = sizes
    own_rows = rows // devices
    band = lax.axis_index("lat")
    matrix = parts_matrix(from_parts=True)

    batch = devices

    def place(index, _):
        device = index * batch
        parts = jnp.concatenate(
            [
                jnp.concatenate(
                    [
                        got_ref[device + d, pl.ds(part * own_rows * members, own_rows * members), :]
                        for d in range(batch)
                    ],
                    axis=0,
                )
                for part in range(4)
            ],
            axis=1,
        )
        joined = jnp.dot(parts, matrix, preferred_element_type=F32)
        for k in range(batch * own_rows):
            row = device * own_rows + k
            if own_rows > 1:
                flipped = (device + k // own_rows) * own_rows + own_rows - 1 - k % own_rows
                row = jnp.where(band == 0, row, flipped)
            values = joined[k * members : (k + 1) * members]
            for field in range(2):
                for half in range(2):
                    first = (2 * field + half) * LANES
                    out_ref[row, pl.ds(2 * half + field, members, stride=4), :] = values[
                        :, first : first + LANES
                    ]
        return 0

    lax.fori_loop(0, devices // batch, place, 0)


def per_device_pair(background, wind_east, wind_north, obs_index, obs_value, obs_scale):
    rows, members, fields, width = background.shape
    devices = lax.axis_size("mem")
    bands = lax.axis_size("lat")
    own_rows = rows // devices
    total = members * devices
    sizes = (rows, members, devices)
    vmem = pl.BlockSpec(memory_space=pltpu.VMEM)
    params = pltpu.CompilerParams(vmem_limit_bytes=40 * 1024 * 1024)
    whole = pltpu.CompilerParams(vmem_limit_bytes=127 * 512 * 1024)

    def cost(microseconds):
        return pl.CostEstimate(
            flops=0, bytes_accessed=int(microseconds * 3_000_000), transcendentals=0
        )

    grouped = members * fields * 2
    own = background.reshape(rows, members, fields, 2, LANES)
    own = own.transpose(0, 1, 3, 2, 4).reshape(rows, grouped, LANES)

    wind_halo = -(-HALO // CHUNK) * CHUNK
    hbm = pl.BlockSpec(memory_space=pltpu.HBM)
    dma = pltpu.SemaphoreType.DMA
    observations = [
        array.reshape(own_rows, NOBS) for array in (obs_index, obs_value, obs_scale)
    ]
    edge_rows = pltpu.VMEM((HALO, grouped, LANES), F32)
    sent, told = pl.pallas_call(
        functools.partial(tell_kernel, sizes),
        out_shape=(
            jax.ShapeDtypeStruct((HALO + 4 * wind_halo // grouped, grouped, LANES), jnp.int16),
            jax.ShapeDtypeStruct((bands * devices, 4, LANES), jnp.int32),
        ),
        in_specs=[hbm] * 6,
        out_specs=(vmem, vmem),
        scratch_shapes=[
            edge_rows,
            pltpu.VMEM((2, rows, width), BF16),
            pltpu.VMEM((own_rows, LANES), jnp.int32),
            pltpu.VMEM((2, own_rows, LANES), F32),
            dma((6,)),
        ],
        compiler_params=whole,
        cost_estimate=cost(1),
        name="tell",
    )(own, wind_east, wind_north, *observations)
    halo = lax.ppermute(sent, "lat", [(0, 1), (1, 0)])
    table = lax.all_to_all(told, ("lat", "mem"), split_axis=0, concat_axis=0, tiled=True)
    staged = pl.pallas_call(
        functools.partial(stage_kernel, sizes),
        out_shape=jax.ShapeDtypeStruct((4, rows, members, LANES), F32),
        in_specs=[vmem],
        out_specs=vmem,
        compiler_params=params,
        cost_estimate=cost(2),
        name="stage",
    )(own)

    per_target = (4 * own_rows + 2) * members
    wind_rows = pltpu.VMEM((8, rows + wind_halo, members, LANES), F32)
    field_rows = pltpu.VMEM((4, PAD + rows + wind_halo, members, LANES), F32)
    coded, edges = pl.pallas_call(
        functools.partial(forecast_kernel, sizes),
        out_shape=(
            jax.ShapeDtypeStruct((devices, 4 * own_rows * members, LANES), jnp.int16),
            jax.ShapeDtypeStruct((devices, 8, members, LANES), F32),
        ),
        in_specs=[vmem] * 4,
        out_specs=(vmem, vmem),
        scratch_shapes=[edge_rows, wind_rows] + [field_rows] * 4,
        compiler_params=params,
        cost_estimate=cost(12),
        name="forecast",
    )(staged, halo, wind_east, wind_north)
    packed = pl.pallas_call(
        functools.partial(observe_kernel, sizes),
        out_shape=jax.ShapeDtypeStruct((devices, per_target, LANES), jnp.int16),
        in_specs=[vmem] * 3,
        out_specs=vmem,
        compiler_params=params,
        cost_estimate=cost(1),
        name="observe",
    )(edges, coded, table)
    got = lax.all_to_all(packed, "mem", split_axis=0, concat_axis=0, tiled=True)
    iterate = pltpu.VMEM((own_rows, total, total), BF16)
    back = pl.pallas_call(
        functools.partial(analysis_kernel, sizes),
        out_shape=jax.ShapeDtypeStruct((devices, 4 * own_rows * members, LANES), BF16),
        in_specs=[vmem] * 5,
        out_specs=vmem,
        scratch_shapes=[
            pltpu.VMEM((4 * own_rows, total, LANES), F32),
            pltpu.VMEM((4 * own_rows, 8, LANES), F32),
            pltpu.VMEM((4 * own_rows, total, LANES), BF16),
            pltpu.VMEM((4 * own_rows, total, LANES), BF16),
        ]
        + [iterate] * 4,
        compiler_params=params,
        cost_estimate=cost(12),
        name="analysis",
    )(got, table, *observations)
    returned = lax.all_to_all(back, "mem", split_axis=0, concat_axis=0, tiled=True)
    result = pl.pallas_call(
        functools.partial(unpack_kernel, sizes),
        out_shape=jax.ShapeDtypeStruct((rows, grouped, LANES), F32),
        in_specs=[vmem],
        out_specs=vmem,
        compiler_params=params,
        cost_estimate=cost(2),
        name="unpack",
    )(returned)
    result = result.reshape(rows, members, 2, fields, LANES).transpose(0, 1, 3, 2, 4)
    return result.reshape(rows, members, fields, width)


def per_device(background, wind_east, wind_north, obs_index, obs_value, obs_scale):
    rows, members, fields, width = background.shape
    devices = lax.axis_size("mem")
    fits = (
        lax.axis_size("lat") == 2
        and members == 8
        and members * devices == LANES
        and fields == 2
        and width == 2 * LANES == PW
        and obs_index.shape[2:] == (1, LANES)
        and rows % (4 * CHUNK) == 0
        and 4 * STEPS % (rows // devices) == 0
        and (rows // devices) % 2 == 0
        and rows >= 8 * STEPS
    )
    run = per_device_pair if fits else per_device_any
    return run(background, wind_east, wind_north, obs_index, obs_value, obs_scale)


def solution(mesh):
    in_specs = (
        P("lat", "mem", None, None),
        P("lat", None),
        P("lat", None),
        P("lat", "mem", None, None),
        P("lat", "mem", None, None),
        P("lat", "mem", None, None),
    )
    out_specs = P("lat", "mem", None, None)
    return jax.shard_map(
        per_device, mesh=mesh, in_specs=in_specs, out_specs=out_specs, check_vma=False
    )
```

```python
import functools
import math

import jax
import jax.numpy as jnp
from jax import lax
from jax.experimental import pallas as pl
from jax.experimental.pallas import tpu as pltpu
from jax.sharding import PartitionSpec as P

PW = 256
NOBS = 128
STEPS = 4
ITERS = 12
LANES = 128
HALO = 4 * STEPS + 1
CHUNK = 8

HIGHEST = lax.Precision.HIGHEST
F32 = jnp.float32
BF16 = jnp.bfloat16


def padded_2(block, sides, width, periodic):
    for axis, dim in sides:
        count = lax.axis_size(axis)
        forward = [(i, i + 1) for i in range(count - 1)]
        if periodic:
            forward.append((count - 1, 0))
        backward = [(target, source) for source, target in forward]
        low = lax.ppermute(
            lax.slice_in_dim(block, block.shape[dim] - width, None, axis=dim), axis, forward
        )
        high = lax.ppermute(lax.slice_in_dim(block, 0, width, axis=dim), axis, backward)
        block = jnp.concatenate([low, block, high], axis=dim)
    return block


def tendency(padded, circumpolar_wind_speed, poleward_wind_speed):
    center_rows = padded[1:-1]
    along_diff = jnp.roll(center_rows, -1, axis=-1) - jnp.roll(center_rows, 1, axis=-1)
    across_diff = padded[2:] - padded[:-2]
    return -0.5 * (circumpolar_wind_speed * along_diff + poleward_wind_speed * across_diff)


def make_blocks(model_variables, index_rows, value_rows, scale_rows):
    row_count, members, flat_width = model_variables.shape
    patch_count = index_rows.shape[1]
    obs_count = index_rows.shape[2]
    fields = flat_width // (patch_count * PW)
    patch_values = model_variables.reshape(row_count, members, fields, patch_count, PW)
    value_ids = lax.broadcasted_iota(jnp.int32, (fields * PW, 1), 0)
    selector = (value_ids[None, None] == index_rows[:, :, None, :]).astype(jnp.float32)
    selector = selector.reshape(row_count, patch_count, fields, PW, obs_count)
    picked = jnp.einsum("akfpt,apftj->akpj", patch_values, selector, precision=HIGHEST)
    average = jnp.mean(picked, axis=1)
    spread = (picked - average[:, None]) * scale_rows[:, None] / math.sqrt(members - 1)
    innovation = (value_rows - average) * scale_rows
    return jnp.concatenate([spread, innovation[:, None]], axis=1).astype(jnp.bfloat16)


def edge_pair(extended):
    return jnp.stack([extended[-1], extended[0]])


def rows_beside(local_rows, extended, banded):
    position = lax.axis_index("mem")
    last_index = lax.axis_size("mem") - 1
    upper_rim = jnp.where(position == 0, banded[0], extended[0])
    lower_rim = jnp.where(position == last_index, banded[3], extended[-1])
    upper_adjacent = jnp.concatenate([upper_rim[None], local_rows[:-1]], axis=0)
    bottom_adjacent = jnp.concatenate([local_rows[1:], lower_rim[None]], axis=0)
    return (upper_adjacent, bottom_adjacent)


def per_device_any(background, wind_east, wind_north, obs_index, obs_value, obs_scale):
    current = background
    stacked_winds = jnp.stack([wind_east, wind_north])
    wide_winds = padded_2(stacked_winds, (("lat", 1),), 3, False).astype(jnp.float32)
    east_wide = wide_winds[0][:, None, None, :]
    north_wide = wide_winds[1][:, None, None, :]
    span = east_wide.shape[0]
    for step_index in range(STEPS):
        extended = padded_2(current, (("lat", 0),), 4, False)
        slope_one = tendency(extended, east_wide, north_wide)
        slope_two = tendency(
            extended[1:-1] + 0.5 * slope_one, east_wide[1 : span - 1], north_wide[1 : span - 1]
        )
        slope_three = tendency(
            extended[2:-2] + 0.5 * slope_two, east_wide[2 : span - 2], north_wide[2 : span - 2]
        )
        slope_four = tendency(
            extended[3:-3] + slope_three, east_wide[3 : span - 3], north_wide[3 : span - 3]
        )
        current = (
            extended[4:-4]
            + (slope_one[3:-3] + 2.0 * slope_two[2:-2] + 2.0 * slope_three[1:-1] + slope_four) / 6.0
        )
    points = lax.all_to_all(current, "mem", split_axis=0, concat_axis=1, tiled=True)
    row_count, members, fields, width = points.shape
    patch_count = obs_index.shape[2]
    model_variables = points.reshape(row_count, members, fields * width)
    index_rows = obs_index.reshape(row_count, patch_count, NOBS)
    value_rows = obs_value.reshape(row_count, patch_count, NOBS)
    scale_rows = obs_scale.reshape(row_count, patch_count, NOBS)
    own_block = make_blocks(model_variables, index_rows, value_rows, scale_rows)
    extended = padded_2(own_block, (("mem", 0),), 1, True)
    banded = padded_2(edge_pair(extended), (("lat", 0),), 1, False)
    upper_adjacent, bottom_adjacent = rows_beside(own_block, extended, banded)
    gram_sum = jnp.zeros((row_count, patch_count, members + 1, members + 1), jnp.float32)
    for neighbor_block in (
        own_block,
        jnp.roll(own_block, -1, axis=2),
        jnp.roll(own_block, 1, axis=2),
        upper_adjacent,
        bottom_adjacent,
    ):
        gram_sum = gram_sum + jnp.einsum(
            "akpj,alpj->apkl", neighbor_block, neighbor_block, preferred_element_type=jnp.float32
        )
    identity = jnp.eye(members, dtype=jnp.float32)
    system = identity + gram_sum[:, :, :members, :members]
    coupling = gram_sum[:, :, :members, members]
    trace_sum = jnp.trace(system, axis1=2, axis2=3)
    scaled = system / trace_sum[:, :, None, None]

    def newton(turn_index, carry):
        upper_iter, lower_iter = carry
        factor = 1.5 * identity - 0.5 * jnp.einsum(
            "apij,apjk->apik", lower_iter, upper_iter, precision=HIGHEST
        )
        return (
            jnp.einsum("apij,apjk->apik", upper_iter, factor, precision=HIGHEST),
            jnp.einsum("apij,apjk->apik", factor, lower_iter, precision=HIGHEST),
        )

    start_lower = jnp.broadcast_to(identity, scaled.shape)
    upper_iter, lower_iter = lax.fori_loop(0, ITERS, newton, (scaled, start_lower))
    inv_root = lower_iter / jnp.sqrt(trace_sum)[:, :, None, None]
    half_step = jnp.einsum("apkl,apl->apk", inv_root, coupling, precision=HIGHEST)
    mean_weight = jnp.einsum("apkl,apl->apk", inv_root, half_step, precision=HIGHEST) / math.sqrt(
        members - 1
    )
    weights = mean_weight[:, :, :, None] + inv_root
    patch_values = points.reshape(row_count, members, fields, patch_count, PW)
    center = jnp.mean(patch_values, axis=1)
    result = center[:, None] + jnp.einsum(
        "akfpt,apki->aifpt", patch_values - center[:, None], weights, precision=HIGHEST
    )
    analysis = result.reshape(row_count, members, fields, width)
    return lax.all_to_all(analysis, "mem", split_axis=1, concat_axis=0, tiled=True)


PAD = 8
TURNS = 2
FINEST = 0.05
LARGEST = 16.0 * sum(1.8**power / math.factorial(power) for power in range(5)) ** STEPS
STATE_LEVELS = 2047.0
WIND_LEVELS = 32767.0
VALUE_LEVELS = 8191.0
SCALE_LEVELS = 4095.0
STEEPNESS = 32766.0 / math.log(1.0 + LARGEST / FINEST)


def take_lanes(values, lanes):
    return jnp.take_along_axis(values, lanes, axis=1, mode="promise_in_bounds")


def pick_lanes(states, index):
    field = jnp.right_shift(index, 8)
    lanes = jnp.bitwise_and(jnp.right_shift(index, 1), LANES - 2) + field
    is_odd = jnp.bitwise_and(index, 1) == 1
    is_late = jnp.bitwise_and(index, 2) == 2
    picks = [take_lanes(state, lanes) for state in states]
    return jnp.where(
        is_odd, jnp.where(is_late, picks[3], picks[1]), jnp.where(is_late, picks[2], picks[0])
    )


def group_place(sizes, band, group):
    return jnp.where(band == 0, group, sizes[2] - 1 - group)


def beside_rows(table_ref, sizes, band, group, is_after):
    devices = sizes[2]
    near = group + 1 if is_after else jnp.maximum(group - 1, 0)
    over = near == devices
    place = jnp.where(over, jnp.where(band == 0, 0, devices - 1), group_place(sizes, band, near))
    near_band = jnp.where(over, 1 - band, band)
    last = jnp.where(band == 0, 0, 1) if is_after else jnp.where(band == 0, 1, 0)
    return near_band * devices + place, last


def beside_index(table_ref, sizes, band, group, is_after):
    place, last = beside_rows(table_ref, sizes, band, group, is_after)
    return jnp.bitwise_and(table_ref[place, pl.ds(last, 1), :], 65535)


def beside_observation(table_ref, sizes, band, group, is_after):
    place, last = beside_rows(table_ref, sizes, band, group, is_after)
    value = jnp.right_shift(table_ref[place, pl.ds(last, 1), :], 16)
    scales = table_ref[place, 2:3, :]
    scale = jnp.where(last == 1, jnp.right_shift(scales, 16), jnp.bitwise_and(scales, 65535))
    return value.astype(F32) * F32(1.0 / VALUE_LEVELS), scale.astype(F32) * F32(1.0 / SCALE_LEVELS)


def parts_matrix(from_parts=False):
    shape = (4 * LANES, 4 * LANES)
    rows = lax.broadcasted_iota(jnp.int32, shape, 0)
    columns = lax.broadcasted_iota(jnp.int32, shape, 1)
    column, plain = (rows, columns) if from_parts else (columns, rows)
    lane = jnp.bitwise_and(column, LANES - 1)
    wanted = (
        jnp.bitwise_and(lane, 1) * (2 * LANES)
        + jnp.right_shift(lane, 1) * 4
        + jnp.right_shift(column, 7)
    )
    return jnp.where(plain == wanted, F32(1.0), F32(0.0)).astype(BF16)


def stage_states(load, row_of, count, members, matrix, q_ref, start):
    left = jnp.concatenate(
        [
            jnp.concatenate([load(row_of(k), 2 * half + field) for k in range(count)], axis=0)
            for field in range(2)
            for half in range(2)
        ],
        axis=1,
    )
    first = left.astype(BF16)
    left = left - first.astype(F32)
    second = left.astype(BF16)
    third = (left - second.astype(F32)).astype(BF16)
    size = count * members
    split = jnp.dot(
        jnp.concatenate([first, second, third], axis=0), matrix, preferred_element_type=F32
    )
    split = split[:size] + (split[size : 2 * size] + split[2 * size :])
    for part in range(4):
        values = split[:, part * LANES : (part + 1) * LANES]
        q_ref[part, pl.ds(start, count)] = values.reshape(count, members, LANES)


def stage_winds(east, north, north_sign, matrix, w_ref, row_of):
    count, members = east.shape[0], w_ref.shape[2]
    for side, (wind, sign) in enumerate(((east, F32(-0.25)), (north, north_sign))):
        both = jnp.concatenate([wind, wind], axis=1)
        split = jnp.dot(both, matrix, preferred_element_type=F32) * sign
        for k in range(count):
            for part in range(4):
                lanes = split[k : k + 1, part * LANES : (part + 1) * LANES]
                w_ref[4 * side + part, row_of(k)] = jnp.broadcast_to(lanes, (members, LANES))


def rk_passes(q_ref, stage_refs, w_ref, count, block):
    a_ref, b_ref, c_ref = stage_refs

    def finish_one(part, at, half):
        a_ref[part, at] = q_ref[part, at] + half

    def finish_two(part, at, half):
        b_ref[part, at] = q_ref[part, at] + half

    def finish_three(part, at, half):
        c_ref[part, at] = q_ref[part, at] + (half + half)

    def finish_four(part, at, half):
        doubled = b_ref[part, at]
        gathered = (a_ref[part, at] + c_ref[part, at] - q_ref[part, at]) + (doubled + doubled)
        q_ref[part, at] = (gathered + half) * F32(1.0 / 3.0)

    for stage, finish in (
        (q_ref, finish_one),
        (a_ref, finish_two),
        (b_ref, finish_three),
        (c_ref, finish_four),
    ):

        def turn(index, _):
            base = PAD + index * block

            def load(k):
                return [stage[part, base + k - 1] for part in range(4)]

            before, here = load(0), load(1)
            for k in range(1, block + 1):
                after = load(k + 1)
                place = index * block + k - 1
                along = (
                    here[1] - pltpu.roll(here[3], 2, 1),
                    here[2] - here[0],
                    here[3] - here[1],
                    pltpu.roll(here[0], LANES - 2, 1) - here[2],
                )
                for part in range(4):
                    across = after[part] - before[part]
                    half = w_ref[part, place] * along[part] + w_ref[4 + part, place] * across
                    finish(part, base + k - 1, half)
                before, here = here, after
            return 0

        turns = -(-count // block)
        if turns == 1:
            turn(0, 0)
        else:
            lax.fori_loop(0, turns, turn, 0)


def encode(value):
    level = jnp.round(jnp.log(1.0 + jnp.abs(value) * F32(1.0 / FINEST)) * F32(STEEPNESS))
    return jnp.where(value < 0.0, -level, level)


def decode(code):
    size = (jnp.exp(jnp.abs(code) * F32(1.0 / STEEPNESS)) - 1.0) * F32(FINEST)
    return jnp.where(code < 0.0, -size, size)


def pack_pair(low, high):
    return jnp.concatenate([low, high], axis=0).astype(jnp.int32).astype(jnp.int16)


def tell_kernel(
    sizes,
    own_ref,
    east_ref,
    north_ref,
    index_ref,
    value_ref,
    scale_ref,
    sent_ref,
    told_ref,
    edge_ref,
    winds_ref,
    ints_ref,
    floats_ref,
    copied,
):
    rows, members, devices = sizes
    own_rows = rows // devices
    band = lax.axis_index("lat")
    wind_halo = -(-HALO // CHUNK) * CHUNK
    begin = jnp.where(band == 0, rows - HALO, 0)
    pairs = (
        (own_ref.at[pl.ds(begin, HALO)], edge_ref),
        (east_ref, winds_ref.at[0]),
        (north_ref, winds_ref.at[1]),
        (index_ref, ints_ref),
        (value_ref, floats_ref.at[0]),
        (scale_ref, floats_ref.at[1]),
    )
    copies = [
        pltpu.make_async_copy(source, target, copied.at[turn])
        for turn, (source, target) in enumerate(pairs)
    ]
    for copy in copies:
        copy.start()
    for copy in copies[1:]:
        copy.wait()
    winds = []
    for side in range(2):
        wind = winds_ref[side].astype(F32) * F32(WIND_LEVELS)
        wind = jnp.where(band == 0, wind[rows - wind_halo :], wind[:wind_halo])
        winds += [wind[:, :LANES], wind[:, LANES:]]
    winds = jnp.round(jnp.concatenate(winds, axis=0)).astype(jnp.int32).astype(jnp.int16)
    sent_ref[HALO:] = winds.reshape(-1, sent_ref.shape[1], LANES)
    values = jnp.round(floats_ref[0] * F32(VALUE_LEVELS)).astype(jnp.int32)
    scales = jnp.round(floats_ref[1] * F32(SCALE_LEVELS)).astype(jnp.int32)
    pairs = ints_ref[...] + values * 65536
    ends = [row[end : end + 1] for row in (pairs, scales) for end in (0, own_rows - 1)]
    told = jnp.concatenate(ends[:2] + [ends[2] + ends[3] * 65536, jnp.zeros_like(ends[0])], axis=0)
    told_ref[...] = jnp.broadcast_to(told[None], told_ref.shape)
    copies[0].wait()
    edge = jnp.round(edge_ref[...] * F32(STATE_LEVELS))
    sent_ref[:HALO] = edge.astype(jnp.int32).astype(jnp.int16)


def stage_kernel(sizes, own_ref, parts_ref):
    rows, members, devices = sizes
    band = lax.axis_index("lat")
    matrix = parts_matrix()
    block = 4 * CHUNK

    def stage(index, _):
        base = index * block

        def row_of(k):
            return jnp.where(band == 0, base + k, rows - 1 - base - k)

        def load(row, lane):
            return own_ref[row, pl.ds(lane, members, stride=4), :]

        stage_states(load, row_of, block, members, matrix, parts_ref, base)
        return 0

    lax.fori_loop(0, rows // block, stage, 0)


def forecast_kernel(
    sizes,
    own_ref,
    halo_ref,
    east_ref,
    north_ref,
    out_ref,
    edges_ref,
    edge_ref,
    w_ref,
    q_ref,
    *stage_refs,
):
    rows, members, devices = sizes
    own_rows = rows // devices
    band = lax.axis_index("lat")
    matrix = parts_matrix()
    north_sign = jnp.where(band == 0, F32(-0.25), F32(0.25))
    wind_halo = -(-HALO // CHUNK) * CHUNK
    pair = 2 * members

    zero_rows = jnp.zeros((4, PAD, members, LANES), F32)
    for ref in (q_ref, *stage_refs):
        ref[:, :PAD] = zero_rows
    stage_winds(
        east_ref[...],
        north_ref[...],
        north_sign,
        matrix,
        w_ref,
        lambda k: jnp.where(band == 0, k, rows - 1 - k),
    )
    edge_ref[...] = halo_ref[:HALO].astype(jnp.int32).astype(F32) * F32(1.0 / STATE_LEVELS)
    halo_winds = halo_ref[HALO:].astype(jnp.int32).astype(F32).reshape(4 * wind_halo, LANES)
    halo_winds = (halo_winds * F32(1.0 / WIND_LEVELS)).astype(BF16)
    halo_winds = [halo_winds[k * wind_halo : (k + 1) * wind_halo] for k in range(4)]
    stage_winds(
        jnp.concatenate(halo_winds[:2], axis=1),
        jnp.concatenate(halo_winds[2:], axis=1),
        north_sign,
        matrix,
        w_ref,
        lambda k: rows + jnp.where(band == 0, k, wind_halo - 1 - k),
    )

    q_ref[:, PAD : PAD + rows] = own_ref[...]

    def row_of(k):
        row = min(k, HALO - 1)
        return jnp.where(band == 0, row, HALO - 1 - row)

    def load(row, lane):
        return edge_ref[row, pl.ds(lane, members, stride=4), :]

    stage_states(load, row_of, wind_halo, members, matrix, q_ref, PAD + rows)

    for step in range(STEPS):
        count = rows + HALO - 1 - 4 * step
        rk_passes(q_ref, stage_refs, w_ref, count, -(-count // TURNS))

    def state(row):
        return [q_ref[part, PAD + row] for part in range(4)]

    def emit(group, _):
        first = group * own_rows
        place = group_place(sizes, band, group)
        for j in range(0, own_rows, 2):
            low, high = state(first + j), state(first + j + 1)
            for part in range(4):
                start = (part * own_rows + j) * members
                out_ref[place, pl.ds(start, pair), :] = pack_pair(
                    encode(low[part]), encode(high[part])
                )
        for side, row in enumerate((jnp.maximum(first - 1, 0), first + own_rows)):
            for part, values in enumerate(state(row)):
                edges_ref[place, 4 * side + part] = values
        return 0

    lax.fori_loop(0, devices, emit, 0, unroll=4)


def observe_kernel(sizes, edges_ref, coded_ref, table_ref, out_ref):
    rows, members, devices = sizes
    band = lax.axis_index("lat")
    coded_rows = coded_ref.shape[1]
    out_ref[:, :coded_rows] = coded_ref[...]

    def emit(group, _):
        place = group_place(sizes, band, group)
        values = []
        for side in range(2):
            index = beside_index(table_ref, sizes, band, group, side == 1)
            index = jnp.broadcast_to(index, (members, LANES))
            states = [edges_ref[place, 4 * side + part] for part in range(4)]
            values.append(encode(pick_lanes(states, index)))
        out_ref[place, pl.ds(coded_rows, 2 * members), :] = pack_pair(*values)
        return 0

    lax.fori_loop(0, devices, emit, 0, unroll=4)


def split_value(value):
    high = value.astype(BF16)
    return high, (value - high.astype(F32)).astype(BF16)


def product(left, right):
    (left_high, left_low), (right_high, right_low) = left, right
    size = right_high.shape[1]
    both = jnp.dot(
        jnp.concatenate([left_high, left_low], axis=1),
        jnp.concatenate(
            [
                jnp.concatenate([right_high, right_low], axis=1),
                jnp.concatenate([right_high, jnp.zeros_like(right_low)], axis=1),
            ],
            axis=0,
        ),
        preferred_element_type=F32,
    )
    return both[:, :size] + both[:, size:]


def analysis_kernel(
    sizes,
    got_ref,
    table_ref,
    index_ref,
    value_ref,
    scale_ref,
    out_ref,
    states_ref,
    center_ref,
    high_ref,
    low_ref,
    *iterates,
):
    rows, members, devices = sizes
    own_rows = rows // devices
    total = members * devices
    band = lax.axis_index("lat")
    group = group_place(sizes, band, lax.axis_index("mem"))
    pair = 2 * members
    beside_start = 4 * own_rows * members

    def pair_at(start):
        both = decode(got_ref[:, pl.ds(start, pair), :].astype(jnp.int32).astype(F32))
        both = both.reshape(devices, 2, members, LANES)
        return both[:, 0].reshape(total, LANES), both[:, 1].reshape(total, LANES)

    def info(ref, j):
        return ref[pl.ds(jnp.where(band == 0, j, own_rows - 1 - j), 1), :]

    picked_rows = [None] * (own_rows + 2)
    picked_rows[0], picked_rows[own_rows + 1] = pair_at(beside_start)
    for j in range(0, own_rows, 2):
        parts = [pair_at((part * own_rows + j) * members) for part in range(4)]
        for k in range(2):
            for part in range(4):
                states_ref[4 * (j + k) + part] = parts[part][k]
            index = jnp.broadcast_to(info(index_ref, j + k), (total, LANES)).astype(jnp.int32)
            picked_rows[j + k + 1] = pick_lanes([part[k] for part in parts], index)

    grams = []
    couplings = []
    for j in range(-1, own_rows + 1):
        if 0 <= j < own_rows:
            value, scale = info(value_ref, j), info(scale_ref, j)
        else:
            value, scale = beside_observation(table_ref, sizes, band, group, j == own_rows)
        if j == -1:
            scale = jnp.where(group == 0, 0.0, scale)
        picked = picked_rows[j + 1]
        average = jnp.mean(picked, axis=0, keepdims=True)
        spread = ((picked - average) * scale / math.sqrt(total - 1)).astype(BF16)
        innovation = jnp.broadcast_to((value - average) * scale, (16, LANES)).astype(BF16)
        contract = (((1,), (1,)), ((), ()))
        grams.append(lax.dot_general(spread, spread, contract, preferred_element_type=F32))
        couplings.append(
            lax.dot_general(innovation, spread, contract, preferred_element_type=F32)
        )

    row_ids = lax.broadcasted_iota(jnp.int32, (total, total), 0)
    column_ids = lax.broadcasted_iota(jnp.int32, (total, total), 1)
    diagonal = row_ids == column_ids
    identity = jnp.where(diagonal, F32(1.0), F32(0.0))

    def put(refs, j, value):
        refs[0][j], refs[1][j] = split_value(value)

    upper_refs, lower_refs = iterates[:2], iterates[2:]
    traces = []
    for j in range(own_rows):
        system = identity + 3.0 * grams[j + 1] + grams[j] + grams[j + 2]
        trace = jnp.sum(
            jnp.sum(jnp.where(diagonal, system, 0.0), axis=0, keepdims=True),
            axis=1,
            keepdims=True,
        )
        traces.append(trace)
        scaled = system / trace
        factor = 1.5 * identity - 0.5 * scaled
        put(upper_refs, j, product(split_value(scaled), split_value(factor)))
        put(lower_refs, j, factor)

    def factor_of(j):
        lower, upper = lower_refs, upper_refs
        lower, upper = (lower[0][j], lower[1][j]), (upper[0][j], upper[1][j])
        return lower, upper, split_value(1.5 * identity - 0.5 * product(lower, upper))

    per_turn = -(-4 * own_rows // (ITERS - 2))

    def newton(turn, _):
        for k in range(per_turn):
            entry = jnp.minimum(turn * per_turn + k, 4 * own_rows - 1)
            state = states_ref[entry]
            center = jnp.mean(state, axis=0, keepdims=True)
            center_ref[entry] = jnp.broadcast_to(center, (8, LANES))
            high_ref[entry], low_ref[entry] = split_value(state - center)
        parts = [factor_of(j) for j in range(own_rows)]
        for j in range(own_rows):
            lower, upper, factor = parts[j]
            put(upper_refs, j, product(upper, factor))
            put(lower_refs, j, product(factor, lower))
        return 0

    lax.fori_loop(0, ITERS - 2, newton, 0)

    def joined(ref, j):
        return jnp.concatenate([ref[4 * j + part] for part in range(4)], axis=1)

    parts = [factor_of(j) for j in range(own_rows)]
    roots = [
        split_value(product(parts[j][2], parts[j][0]) / jnp.sqrt(traces[j]))
        for j in range(own_rows)
    ]
    half_steps = []
    for j in range(own_rows):
        coupling = 3.0 * couplings[j + 1] + couplings[j] + couplings[j + 2]
        half_steps.append(product(split_value(coupling), roots[j]))
    spreads = [
        jnp.dot(roots[j][0], joined(high_ref, j), preferred_element_type=F32)
        for j in range(own_rows)
    ]
    results = []
    for j in range(own_rows):
        mean_weight = product(split_value(half_steps[j]), roots[j]) / math.sqrt(total - 1)
        high, low = split_value(mean_weight[:8])
        moved = jnp.dot(
            jnp.concatenate([high, low], axis=0), joined(high_ref, j), preferred_element_type=F32
        )
        rest = jnp.dot(
            jnp.concatenate([high, low], axis=0), joined(low_ref, j), preferred_element_type=F32
        )
        center = joined(center_ref, j)[:1]
        results.append(spreads[j] + (center + (moved[:1] + moved[8:9]) + rest[:1]))
    for j in range(0, own_rows, 2):
        for part in range(4):
            both = [
                results[k][:, part * LANES : (part + 1) * LANES].reshape(devices, members, LANES)
                for k in (j, j + 1)
            ]
            out_ref[:, pl.ds((part * own_rows + j) * members, pair), :] = jnp.concatenate(
                both, axis=1
            ).astype(BF16)


def unpack_kernel(sizes, got_ref, out_ref):
    rows, members, devices = sizes
    own_rows = rows // devices
    band = lax.axis_index("lat")
    matrix = parts_matrix(from_parts=True)

    batch = devices

    def place(index, _):
        device = index * batch
        parts = jnp.concatenate(
            [
                jnp.concatenate(
                    [
                        got_ref[device + d, pl.ds(part * own_rows * members, own_rows * members), :]
                        for d in range(batch)
                    ],
                    axis=0,
                )
                for part in range(4)
            ],
            axis=1,
        )
        joined = jnp.dot(parts, matrix, preferred_element_type=F32)
        for k in range(batch * own_rows):
            row = device * own_rows + k
            if own_rows > 1:
                flipped = (device + k // own_rows) * own_rows + own_rows - 1 - k % own_rows
                row = jnp.where(band == 0, row, flipped)
            values = joined[k * members : (k + 1) * members]
            for field in range(2):
                for half in range(2):
                    first = (2 * field + half) * LANES
                    out_ref[row, pl.ds(2 * half + field, members, stride=4), :] = values[
                        :, first : first + LANES
                    ]
        return 0

    lax.fori_loop(0, devices // batch, place, 0)


def per_device_pair(background, wind_east, wind_north, obs_index, obs_value, obs_scale):
    rows, members, fields, width = background.shape
    devices = lax.axis_size("mem")
    bands = lax.axis_size("lat")
    own_rows = rows // devices
    total = members * devices
    sizes = (rows, members, devices)
    vmem = pl.BlockSpec(memory_space=pltpu.VMEM)
    params = pltpu.CompilerParams(vmem_limit_bytes=40 * 1024 * 1024)
    whole = pltpu.CompilerParams(vmem_limit_bytes=127 * 512 * 1024)

    def cost(microseconds):
        return pl.CostEstimate(
            flops=0, bytes_accessed=int(microseconds * 3_000_000), transcendentals=0
        )

    grouped = members * fields * 2
    own = background.reshape(rows, members, fields, 2, LANES)
    own = own.transpose(0, 1, 3, 2, 4).reshape(rows, grouped, LANES)

    wind_halo = -(-HALO // CHUNK) * CHUNK
    hbm = pl.BlockSpec(memory_space=pltpu.HBM)
    dma = pltpu.SemaphoreType.DMA
    observations = [
        array.reshape(own_rows, NOBS) for array in (obs_index, obs_value, obs_scale)
    ]
    edge_rows = pltpu.VMEM((HALO, grouped, LANES), F32)
    sent, told = pl.pallas_call(
        functools.partial(tell_kernel, sizes),
        out_shape=(
            jax.ShapeDtypeStruct((HALO + 4 * wind_halo // grouped, grouped, LANES), jnp.int16),
            jax.ShapeDtypeStruct((bands * devices, 4, LANES), jnp.int32),
        ),
        in_specs=[hbm] * 6,
        out_specs=(vmem, vmem),
        scratch_shapes=[
            edge_rows,
            pltpu.VMEM((2, rows, width), BF16),
            pltpu.VMEM((own_rows, LANES), jnp.int32),
            pltpu.VMEM((2, own_rows, LANES), F32),
            dma((6,)),
        ],
        compiler_params=whole,
        cost_estimate=cost(1),
        name="tell",
    )(own, wind_east, wind_north, *observations)
    halo = lax.ppermute(sent, "lat", [(0, 1), (1, 0)])
    table = lax.all_to_all(told, ("lat", "mem"), split_axis=0, concat_axis=0, tiled=True)
    staged = pl.pallas_call(
        functools.partial(stage_kernel, sizes),
        out_shape=jax.ShapeDtypeStruct((4, rows, members, LANES), F32),
        in_specs=[vmem],
        out_specs=vmem,
        compiler_params=params,
        cost_estimate=cost(2),
        name="stage",
    )(own)

    per_target = (4 * own_rows + 2) * members
    wind_rows = pltpu.VMEM((8, rows + wind_halo, members, LANES), F32)
    field_rows = pltpu.VMEM((4, PAD + rows + wind_halo, members, LANES), F32)
    coded, edges = pl.pallas_call(
        functools.partial(forecast_kernel, sizes),
        out_shape=(
            jax.ShapeDtypeStruct((devices, 4 * own_rows * members, LANES), jnp.int16),
            jax.ShapeDtypeStruct((devices, 8, members, LANES), F32),
        ),
        in_specs=[vmem] * 4,
        out_specs=(vmem, vmem),
        scratch_shapes=[edge_rows, wind_rows] + [field_rows] * 4,
        compiler_params=params,
        cost_estimate=cost(12),
        name="forecast",
    )(staged, halo, wind_east, wind_north)
    packed = pl.pallas_call(
        functools.partial(observe_kernel, sizes),
        out_shape=jax.ShapeDtypeStruct((devices, per_target, LANES), jnp.int16),
        in_specs=[vmem] * 3,
        out_specs=vmem,
        compiler_params=params,
        cost_estimate=cost(1),
        name="observe",
    )(edges, coded, table)
    got = lax.all_to_all(packed, "mem", split_axis=0, concat_axis=0, tiled=True)
    iterate = pltpu.VMEM((own_rows, total, total), BF16)
    back = pl.pallas_call(
        functools.partial(analysis_kernel, sizes),
        out_shape=jax.ShapeDtypeStruct((devices, 4 * own_rows * members, LANES), BF16),
        in_specs=[vmem] * 5,
        out_specs=vmem,
        scratch_shapes=[
            pltpu.VMEM((4 * own_rows, total, LANES), F32),
            pltpu.VMEM((4 * own_rows, 8, LANES), F32),
            pltpu.VMEM((4 * own_rows, total, LANES), BF16),
            pltpu.VMEM((4 * own_rows, total, LANES), BF16),
        ]
        + [iterate] * 4,
        compiler_params=params,
        cost_estimate=cost(12),
        name="analysis",
    )(got, table, *observations)
    returned = lax.all_to_all(back, "mem", split_axis=0, concat_axis=0, tiled=True)
    result = pl.pallas_call(
        functools.partial(unpack_kernel, sizes),
        out_shape=jax.ShapeDtypeStruct((rows, grouped, LANES), F32),
        in_specs=[vmem],
        out_specs=vmem,
        compiler_params=params,
        cost_estimate=cost(2),
        name="unpack",
    )(returned)
    result = result.reshape(rows, members, 2, fields, LANES).transpose(0, 1, 3, 2, 4)
    return result.reshape(rows, members, fields, width)


def per_device(background, wind_east, wind_north, obs_index, obs_value, obs_scale):
    rows, members, fields, width = background.shape
    devices = lax.axis_size("mem")
    fits = (
        lax.axis_size("lat") == 2
        and members == 8
        and members * devices == LANES
        and fields == 2
        and width == 2 * LANES == PW
        and obs_index.shape[2:] == (1, LANES)
        and rows % (4 * CHUNK) == 0
        and 4 * STEPS % (rows // devices) == 0
        and (rows // devices) % 2 == 0
        and rows >= 8 * STEPS
    )
    run = per_device_pair if fits else per_device_any
    return run(background, wind_east, wind_north, obs_index, obs_value, obs_scale)


def solution(mesh):
    in_specs = (
        P("lat", "mem", None, None),
        P("lat", None),
        P("lat", None),
        P("lat", "mem", None, None),
        P("lat", "mem", None, None),
        P("lat", "mem", None, None),
    )
    out_specs = P("lat", "mem", None, None)
    return jax.shard_map(
        per_device, mesh=mesh, in_specs=in_specs, out_specs=out_specs, check_vma=False
    )
```

```python
import functools
import math

import jax
import jax.numpy as jnp
from jax import lax
from jax.experimental import pallas as pl
from jax.experimental.pallas import tpu as pltpu
from jax.sharding import PartitionSpec as P

PW = 256
NOBS = 128
STEPS = 4
ITERS = 12
LANES = 128
HALO = 4 * STEPS + 1
CHUNK = 8

HIGHEST = lax.Precision.HIGHEST
F32 = jnp.float32
BF16 = jnp.bfloat16


def padded_2(block, sides, width, periodic):
    for axis, dim in sides:
        count = lax.axis_size(axis)
        forward = [(i, i + 1) for i in range(count - 1)]
        if periodic:
            forward.append((count - 1, 0))
        backward = [(target, source) for source, target in forward]
        low = lax.ppermute(
            lax.slice_in_dim(block, block.shape[dim] - width, None, axis=dim), axis, forward
        )
        high = lax.ppermute(lax.slice_in_dim(block, 0, width, axis=dim), axis, backward)
        block = jnp.concatenate([low, block, high], axis=dim)
    return block


def tendency(padded, circumpolar_wind_speed, poleward_wind_speed):
    center_rows = padded[1:-1]
    along_diff = jnp.roll(center_rows, -1, axis=-1) - jnp.roll(center_rows, 1, axis=-1)
    across_diff = padded[2:] - padded[:-2]
    return -0.5 * (circumpolar_wind_speed * along_diff + poleward_wind_speed * across_diff)


def make_blocks(model_variables, index_rows, value_rows, scale_rows):
    row_count, members, flat_width = model_variables.shape
    patch_count = index_rows.shape[1]
    obs_count = index_rows.shape[2]
    fields = flat_width // (patch_count * PW)
    patch_values = model_variables.reshape(row_count, members, fields, patch_count, PW)
    value_ids = lax.broadcasted_iota(jnp.int32, (fields * PW, 1), 0)
    selector = (value_ids[None, None] == index_rows[:, :, None, :]).astype(jnp.float32)
    selector = selector.reshape(row_count, patch_count, fields, PW, obs_count)
    picked = jnp.einsum("akfpt,apftj->akpj", patch_values, selector, precision=HIGHEST)
    average = jnp.mean(picked, axis=1)
    spread = (picked - average[:, None]) * scale_rows[:, None] / math.sqrt(members - 1)
    innovation = (value_rows - average) * scale_rows
    return jnp.concatenate([spread, innovation[:, None]], axis=1).astype(jnp.bfloat16)


def edge_pair(extended):
    return jnp.stack([extended[-1], extended[0]])


def rows_beside(local_rows, extended, banded):
    position = lax.axis_index("mem")
    last_index = lax.axis_size("mem") - 1
    upper_rim = jnp.where(position == 0, banded[0], extended[0])
    lower_rim = jnp.where(position == last_index, banded[3], extended[-1])
    upper_adjacent = jnp.concatenate([upper_rim[None], local_rows[:-1]], axis=0)
    bottom_adjacent = jnp.concatenate([local_rows[1:], lower_rim[None]], axis=0)
    return (upper_adjacent, bottom_adjacent)


def per_device_any(background, wind_east, wind_north, obs_index, obs_value, obs_scale):
    current = background
    stacked_winds = jnp.stack([wind_east, wind_north])
    wide_winds = padded_2(stacked_winds, (("lat", 1),), 3, False).astype(jnp.float32)
    east_wide = wide_winds[0][:, None, None, :]
    north_wide = wide_winds[1][:, None, None, :]
    span = east_wide.shape[0]
    for step_index in range(STEPS):
        extended = padded_2(current, (("lat", 0),), 4, False)
        slope_one = tendency(extended, east_wide, north_wide)
        slope_two = tendency(
            extended[1:-1] + 0.5 * slope_one, east_wide[1 : span - 1], north_wide[1 : span - 1]
        )
        slope_three = tendency(
            extended[2:-2] + 0.5 * slope_two, east_wide[2 : span - 2], north_wide[2 : span - 2]
        )
        slope_four = tendency(
            extended[3:-3] + slope_three, east_wide[3 : span - 3], north_wide[3 : span - 3]
        )
        current = (
            extended[4:-4]
            + (slope_one[3:-3] + 2.0 * slope_two[2:-2] + 2.0 * slope_three[1:-1] + slope_four) / 6.0
        )
    points = lax.all_to_all(current, "mem", split_axis=0, concat_axis=1, tiled=True)
    row_count, members, fields, width = points.shape
    patch_count = obs_index.shape[2]
    model_variables = points.reshape(row_count, members, fields * width)
    index_rows = obs_index.reshape(row_count, patch_count, NOBS)
    value_rows = obs_value.reshape(row_count, patch_count, NOBS)
    scale_rows = obs_scale.reshape(row_count, patch_count, NOBS)
    own_block = make_blocks(model_variables, index_rows, value_rows, scale_rows)
    extended = padded_2(own_block, (("mem", 0),), 1, True)
    banded = padded_2(edge_pair(extended), (("lat", 0),), 1, False)
    upper_adjacent, bottom_adjacent = rows_beside(own_block, extended, banded)
    gram_sum = jnp.zeros((row_count, patch_count, members + 1, members + 1), jnp.float32)
    for neighbor_block in (
        own_block,
        jnp.roll(own_block, -1, axis=2),
        jnp.roll(own_block, 1, axis=2),
        upper_adjacent,
        bottom_adjacent,
    ):
        gram_sum = gram_sum + jnp.einsum(
            "akpj,alpj->apkl", neighbor_block, neighbor_block, preferred_element_type=jnp.float32
        )
    identity = jnp.eye(members, dtype=jnp.float32)
    system = identity + gram_sum[:, :, :members, :members]
    coupling = gram_sum[:, :, :members, members]
    trace_sum = jnp.trace(system, axis1=2, axis2=3)
    scaled = system / trace_sum[:, :, None, None]

    def newton(turn_index, carry):
        upper_iter, lower_iter = carry
        factor = 1.5 * identity - 0.5 * jnp.einsum(
            "apij,apjk->apik", lower_iter, upper_iter, precision=HIGHEST
        )
        return (
            jnp.einsum("apij,apjk->apik", upper_iter, factor, precision=HIGHEST),
            jnp.einsum("apij,apjk->apik", factor, lower_iter, precision=HIGHEST),
        )

    start_lower = jnp.broadcast_to(identity, scaled.shape)
    upper_iter, lower_iter = lax.fori_loop(0, ITERS, newton, (scaled, start_lower))
    inv_root = lower_iter / jnp.sqrt(trace_sum)[:, :, None, None]
    half_step = jnp.einsum("apkl,apl->apk", inv_root, coupling, precision=HIGHEST)
    mean_weight = jnp.einsum("apkl,apl->apk", inv_root, half_step, precision=HIGHEST) / math.sqrt(
        members - 1
    )
    weights = mean_weight[:, :, :, None] + inv_root
    patch_values = points.reshape(row_count, members, fields, patch_count, PW)
    center = jnp.mean(patch_values, axis=1)
    result = center[:, None] + jnp.einsum(
        "akfpt,apki->aifpt", patch_values - center[:, None], weights, precision=HIGHEST
    )
    analysis = result.reshape(row_count, members, fields, width)
    return lax.all_to_all(analysis, "mem", split_axis=1, concat_axis=0, tiled=True)


PAD = 8
TURNS = 2
FINEST = 0.05
LARGEST = 16.0 * sum(1.8**power / math.factorial(power) for power in range(5)) ** STEPS
STATE_LEVELS = 2047.0
WIND_LEVELS = 32767.0
VALUE_LEVELS = 8191.0
SCALE_LEVELS = 4095.0
STEEPNESS = 32766.0 / math.log(1.0 + LARGEST / FINEST)


def take_lanes(values, lanes):
    return jnp.take_along_axis(values, lanes, axis=1, mode="promise_in_bounds")


def pick_lanes(states, index):
    field = jnp.right_shift(index, 8)
    lanes = jnp.bitwise_and(jnp.right_shift(index, 1), LANES - 2) + field
    is_odd = jnp.bitwise_and(index, 1) == 1
    is_late = jnp.bitwise_and(index, 2) == 2
    picks = [take_lanes(state, lanes) for state in states]
    return jnp.where(
        is_odd, jnp.where(is_late, picks[3], picks[1]), jnp.where(is_late, picks[2], picks[0])
    )


def group_place(sizes, band, group):
    return jnp.where(band == 0, group, sizes[2] - 1 - group)


def beside_rows(table_ref, sizes, band, group, is_after):
    devices = sizes[2]
    near = group + 1 if is_after else jnp.maximum(group - 1, 0)
    over = near == devices
    place = jnp.where(over, jnp.where(band == 0, 0, devices - 1), group_place(sizes, band, near))
    near_band = jnp.where(over, 1 - band, band)
    last = jnp.where(band == 0, 0, 1) if is_after else jnp.where(band == 0, 1, 0)
    return near_band * devices + place, last


def beside_index(table_ref, sizes, band, group, is_after):
    place, last = beside_rows(table_ref, sizes, band, group, is_after)
    return jnp.bitwise_and(table_ref[place, pl.ds(last, 1), :], 65535)


def beside_observation(table_ref, sizes, band, group, is_after):
    place, last = beside_rows(table_ref, sizes, band, group, is_after)
    value = jnp.right_shift(table_ref[place, pl.ds(last, 1), :], 16)
    scales = table_ref[place, 2:3, :]
    scale = jnp.where(last == 1, jnp.right_shift(scales, 16), jnp.bitwise_and(scales, 65535))
    return value.astype(F32) * F32(1.0 / VALUE_LEVELS), scale.astype(F32) * F32(1.0 / SCALE_LEVELS)


def parts_matrix(from_parts=False):
    shape = (4 * LANES, 4 * LANES)
    rows = lax.broadcasted_iota(jnp.int32, shape, 0)
    columns = lax.broadcasted_iota(jnp.int32, shape, 1)
    column, plain = (rows, columns) if from_parts else (columns, rows)
    lane = jnp.bitwise_and(column, LANES - 1)
    wanted = (
        jnp.bitwise_and(lane, 1) * (2 * LANES)
        + jnp.right_shift(lane, 1) * 4
        + jnp.right_shift(column, 7)
    )
    return jnp.where(plain == wanted, F32(1.0), F32(0.0)).astype(BF16)


def stage_states(load, row_of, count, members, matrix, q_ref, start):
    left = jnp.concatenate(
        [
            jnp.concatenate([load(row_of(k), 2 * half + field) for k in range(count)], axis=0)
            for field in range(2)
            for half in range(2)
        ],
        axis=1,
    )
    first = left.astype(BF16)
    left = left - first.astype(F32)
    second = left.astype(BF16)
    third = (left - second.astype(F32)).astype(BF16)
    size = count * members
    split = jnp.dot(
        jnp.concatenate([first, second, third], axis=0), matrix, preferred_element_type=F32
    )
    split = split[:size] + (split[size : 2 * size] + split[2 * size :])
    for part in range(4):
        values = split[:, part * LANES : (part + 1) * LANES]
        q_ref[part, pl.ds(start, count)] = values.reshape(count, members, LANES)


def stage_winds(east, north, north_sign, matrix, w_ref, row_of):
    count, members = east.shape[0], w_ref.shape[2]
    for side, (wind, sign) in enumerate(((east, F32(-0.25)), (north, north_sign))):
        both = jnp.concatenate([wind, wind], axis=1)
        split = jnp.dot(both, matrix, preferred_element_type=F32) * sign
        for k in range(count):
            for part in range(4):
                lanes = split[k : k + 1, part * LANES : (part + 1) * LANES]
                w_ref[4 * side + part, row_of(k)] = jnp.broadcast_to(lanes, (members, LANES))


def rk_passes(q_ref, stage_refs, w_ref, count, block):
    a_ref, b_ref, c_ref = stage_refs

    def finish_one(part, at, half, here):
        a_ref[part, at] = here + half

    def finish_two(part, at, half, here):
        b_ref[part, at] = q_ref[part, at] + half

    def finish_three(part, at, half, here):
        moved = half + half
        c_ref[part, at] = q_ref[part, at] + moved
        a_ref[part, at] = (a_ref[part, at] + moved) + (here + here)

    def finish_four(part, at, half, here):
        q_ref[part, at] = (a_ref[part, at] + half) * F32(1.0 / 3.0)

    for stage, finish in (
        (q_ref, finish_one),
        (a_ref, finish_two),
        (b_ref, finish_three),
        (c_ref, finish_four),
    ):

        def turn(index, _):
            base = PAD + index * block

            def load(k):
                return [stage[part, base + k - 1] for part in range(4)]

            before, here = load(0), load(1)
            for k in range(1, block + 1):
                after = load(k + 1)
                place = index * block + k - 1
                along = (
                    here[1] - pltpu.roll(here[3], 2, 1),
                    here[2] - here[0],
                    here[3] - here[1],
                    pltpu.roll(here[0], LANES - 2, 1) - here[2],
                )
                for part in range(4):
                    across = after[part] - before[part]
                    half = w_ref[part, place] * along[part] + w_ref[4 + part, place] * across
                    finish(part, base + k - 1, half, here[part])
                before, here = here, after
            return 0

        turns = -(-count // block)
        if turns == 1:
            turn(0, 0)
        else:
            lax.fori_loop(0, turns, turn, 0)


def encode(value):
    level = jnp.round(jnp.log(1.0 + jnp.abs(value) * F32(1.0 / FINEST)) * F32(STEEPNESS))
    return jnp.where(value < 0.0, -level, level)


def decode(code):
    size = (jnp.exp(jnp.abs(code) * F32(1.0 / STEEPNESS)) - 1.0) * F32(FINEST)
    return jnp.where(code < 0.0, -size, size)


def pack_pair(low, high):
    return jnp.concatenate([low, high], axis=0).astype(jnp.int32).astype(jnp.int16)


def tell_kernel(
    sizes,
    own_ref,
    east_ref,
    north_ref,
    index_ref,
    value_ref,
    scale_ref,
    sent_ref,
    told_ref,
    edge_ref,
    winds_ref,
    ints_ref,
    floats_ref,
    copied,
):
    rows, members, devices = sizes
    own_rows = rows // devices
    band = lax.axis_index("lat")
    wind_halo = -(-HALO // CHUNK) * CHUNK
    begin = jnp.where(band == 0, rows - HALO, 0)
    pairs = (
        (own_ref.at[pl.ds(begin, HALO)], edge_ref),
        (east_ref, winds_ref.at[0]),
        (north_ref, winds_ref.at[1]),
        (index_ref, ints_ref),
        (value_ref, floats_ref.at[0]),
        (scale_ref, floats_ref.at[1]),
    )
    copies = [
        pltpu.make_async_copy(source, target, copied.at[turn])
        for turn, (source, target) in enumerate(pairs)
    ]
    for copy in copies:
        copy.start()
    for copy in copies[1:]:
        copy.wait()
    winds = []
    for side in range(2):
        wind = winds_ref[side].astype(F32) * F32(WIND_LEVELS)
        wind = jnp.where(band == 0, wind[rows - wind_halo :], wind[:wind_halo])
        winds += [wind[:, :LANES], wind[:, LANES:]]
    winds = jnp.round(jnp.concatenate(winds, axis=0)).astype(jnp.int32).astype(jnp.int16)
    sent_ref[HALO:] = winds.reshape(-1, sent_ref.shape[1], LANES)
    values = jnp.round(floats_ref[0] * F32(VALUE_LEVELS)).astype(jnp.int32)
    scales = jnp.round(floats_ref[1] * F32(SCALE_LEVELS)).astype(jnp.int32)
    pairs = ints_ref[...] + values * 65536
    ends = [row[end : end + 1] for row in (pairs, scales) for end in (0, own_rows - 1)]
    told = jnp.concatenate(ends[:2] + [ends[2] + ends[3] * 65536, jnp.zeros_like(ends[0])], axis=0)
    told_ref[...] = jnp.broadcast_to(told[None], told_ref.shape)
    copies[0].wait()
    edge = jnp.round(edge_ref[...] * F32(STATE_LEVELS))
    sent_ref[:HALO] = edge.astype(jnp.int32).astype(jnp.int16)


def forecast_kernel(
    sizes,
    own_ref,
    halo_ref,
    east_ref,
    north_ref,
    out_ref,
    edges_ref,
    edge_ref,
    w_ref,
    q_ref,
    *stage_refs,
):
    rows, members, devices = sizes
    own_rows = rows // devices
    band = lax.axis_index("lat")
    matrix = parts_matrix()
    north_sign = jnp.where(band == 0, F32(-0.25), F32(0.25))
    wind_halo = -(-HALO // CHUNK) * CHUNK
    pair = 2 * members

    zero_rows = jnp.zeros((4, PAD, members, LANES), F32)
    for ref in (q_ref, *stage_refs):
        ref[:, :PAD] = zero_rows
    stage_winds(
        east_ref[...],
        north_ref[...],
        north_sign,
        matrix,
        w_ref,
        lambda k: jnp.where(band == 0, k, rows - 1 - k),
    )
    edge_ref[...] = halo_ref[:HALO].astype(jnp.int32).astype(F32) * F32(1.0 / STATE_LEVELS)
    halo_winds = halo_ref[HALO:].astype(jnp.int32).astype(F32).reshape(4 * wind_halo, LANES)
    halo_winds = (halo_winds * F32(1.0 / WIND_LEVELS)).astype(BF16)
    halo_winds = [halo_winds[k * wind_halo : (k + 1) * wind_halo] for k in range(4)]
    stage_winds(
        jnp.concatenate(halo_winds[:2], axis=1),
        jnp.concatenate(halo_winds[2:], axis=1),
        north_sign,
        matrix,
        w_ref,
        lambda k: rows + jnp.where(band == 0, k, wind_halo - 1 - k),
    )

    def row_of(k):
        row = min(k, HALO - 1)
        return jnp.where(band == 0, row, HALO - 1 - row)

    def load(row, lane):
        return edge_ref[row, pl.ds(lane, members, stride=4), :]

    stage_states(load, row_of, wind_halo, members, matrix, q_ref, PAD + rows)

    def load_own(row, lane):
        return own_ref[row, pl.ds(lane, members, stride=4), :]

    block = 4 * CHUNK
    for start in range(0, rows, block):
        place = PAD + jnp.where(band == 0, start, rows - block - start)
        stage_states(
            load_own,
            lambda k: start + jnp.where(band == 0, k, block - 1 - k),
            block,
            members,
            matrix,
            q_ref,
            place,
        )

    for step in range(STEPS):
        count = rows + HALO - 1 - 4 * step
        rk_passes(q_ref, stage_refs, w_ref, count, -(-count // TURNS))

    def state(row):
        return [q_ref[part, PAD + row] for part in range(4)]

    def emit(group, _):
        first = group * own_rows
        place = group_place(sizes, band, group)
        for j in range(0, own_rows, 2):
            low, high = state(first + j), state(first + j + 1)
            for part in range(4):
                start = (part * own_rows + j) * members
                out_ref[place, pl.ds(start, pair), :] = pack_pair(
                    encode(low[part]), encode(high[part])
                )
        for side, row in enumerate((jnp.maximum(first - 1, 0), first + own_rows)):
            for part, values in enumerate(state(row)):
                edges_ref[place, 4 * side + part] = values
        return 0

    lax.fori_loop(0, devices, emit, 0, unroll=4)


def observe_kernel(sizes, edges_ref, coded_ref, table_ref, out_ref):
    rows, members, devices = sizes
    band = lax.axis_index("lat")
    coded_rows = coded_ref.shape[1]
    out_ref[:, :coded_rows] = coded_ref[...]

    def emit(group, _):
        place = group_place(sizes, band, group)
        values = []
        for side in range(2):
            index = beside_index(table_ref, sizes, band, group, side == 1)
            index = jnp.broadcast_to(index, (members, LANES))
            states = [edges_ref[place, 4 * side + part] for part in range(4)]
            values.append(encode(pick_lanes(states, index)))
        out_ref[place, pl.ds(coded_rows, 2 * members), :] = pack_pair(*values)
        return 0

    lax.fori_loop(0, devices, emit, 0, unroll=4)


def split_value(value):
    high = value.astype(BF16)
    return high, (value - high.astype(F32)).astype(BF16)


def product(left, right):
    (left_high, left_low), (right_high, right_low) = left, right
    size = right_high.shape[1]
    both = jnp.dot(
        jnp.concatenate([left_high, left_low], axis=1),
        jnp.concatenate(
            [
                jnp.concatenate([right_high, right_low], axis=1),
                jnp.concatenate([right_high, jnp.zeros_like(right_low)], axis=1),
            ],
            axis=0,
        ),
        preferred_element_type=F32,
    )
    return both[:, :size] + both[:, size:]


def analysis_kernel(
    sizes,
    got_ref,
    table_ref,
    index_ref,
    value_ref,
    scale_ref,
    out_ref,
    states_ref,
    center_ref,
    high_ref,
    low_ref,
    *iterates,
):
    rows, members, devices = sizes
    own_rows = rows // devices
    total = members * devices
    band = lax.axis_index("lat")
    group = group_place(sizes, band, lax.axis_index("mem"))
    pair = 2 * members
    beside_start = 4 * own_rows * members

    def pair_at(start):
        both = decode(got_ref[:, pl.ds(start, pair), :].astype(jnp.int32).astype(F32))
        both = both.reshape(devices, 2, members, LANES)
        return both[:, 0].reshape(total, LANES), both[:, 1].reshape(total, LANES)

    def info(ref, j):
        return ref[pl.ds(jnp.where(band == 0, j, own_rows - 1 - j), 1), :]

    picked_rows = [None] * (own_rows + 2)
    picked_rows[0], picked_rows[own_rows + 1] = pair_at(beside_start)
    for j in range(0, own_rows, 2):
        parts = [pair_at((part * own_rows + j) * members) for part in range(4)]
        for k in range(2):
            for part in range(4):
                states_ref[4 * (j + k) + part] = parts[part][k]
            index = jnp.broadcast_to(info(index_ref, j + k), (total, LANES)).astype(jnp.int32)
            picked_rows[j + k + 1] = pick_lanes([part[k] for part in parts], index)

    grams = []
    couplings = []
    for j in range(-1, own_rows + 1):
        if 0 <= j < own_rows:
            value, scale = info(value_ref, j), info(scale_ref, j)
        else:
            value, scale = beside_observation(table_ref, sizes, band, group, j == own_rows)
        if j == -1:
            scale = jnp.where(group == 0, 0.0, scale)
        picked = picked_rows[j + 1]
        average = jnp.mean(picked, axis=0, keepdims=True)
        spread = ((picked - average) * scale / math.sqrt(total - 1)).astype(BF16)
        innovation = jnp.broadcast_to((value - average) * scale, (16, LANES)).astype(BF16)
        contract = (((1,), (1,)), ((), ()))
        grams.append(lax.dot_general(spread, spread, contract, preferred_element_type=F32))
        couplings.append(
            lax.dot_general(innovation, spread, contract, preferred_element_type=F32)
        )

    row_ids = lax.broadcasted_iota(jnp.int32, (total, total), 0)
    column_ids = lax.broadcasted_iota(jnp.int32, (total, total), 1)
    diagonal = row_ids == column_ids
    identity = jnp.where(diagonal, F32(1.0), F32(0.0))

    def put(refs, j, value):
        refs[0][j], refs[1][j] = split_value(value)

    upper_refs, lower_refs = iterates[:2], iterates[2:]
    traces = []
    for j in range(own_rows):
        system = identity + 3.0 * grams[j + 1] + grams[j] + grams[j + 2]
        trace = jnp.sum(
            jnp.sum(jnp.where(diagonal, system, 0.0), axis=0, keepdims=True),
            axis=1,
            keepdims=True,
        )
        traces.append(trace)
        scaled = system / trace
        factor = 1.5 * identity - 0.5 * scaled
        put(upper_refs, j, product(split_value(scaled), split_value(factor)))
        put(lower_refs, j, factor)

    def factor_of(j):
        lower, upper = lower_refs, upper_refs
        lower, upper = (lower[0][j], lower[1][j]), (upper[0][j], upper[1][j])
        return lower, upper, split_value(1.5 * identity - 0.5 * product(lower, upper))

    per_turn = -(-4 * own_rows // (ITERS - 2))

    def newton(turn, _):
        for k in range(per_turn):
            entry = jnp.minimum(turn * per_turn + k, 4 * own_rows - 1)
            state = states_ref[entry]
            center = jnp.mean(state, axis=0, keepdims=True)
            center_ref[entry] = jnp.broadcast_to(center, (8, LANES))
            high_ref[entry], low_ref[entry] = split_value(state - center)
        parts = [factor_of(j) for j in range(own_rows)]
        for j in range(own_rows):
            lower, upper, factor = parts[j]
            put(upper_refs, j, product(upper, factor))
            put(lower_refs, j, product(factor, lower))
        return 0

    lax.fori_loop(0, ITERS - 2, newton, 0, unroll=2)

    def joined(ref, j):
        return jnp.concatenate([ref[4 * j + part] for part in range(4)], axis=1)

    parts = [factor_of(j) for j in range(own_rows)]
    roots = [
        split_value(product(parts[j][2], parts[j][0]) / jnp.sqrt(traces[j]))
        for j in range(own_rows)
    ]
    half_steps = []
    for j in range(own_rows):
        coupling = 3.0 * couplings[j + 1] + couplings[j] + couplings[j + 2]
        half_steps.append(product(split_value(coupling), roots[j]))
    spreads = [
        jnp.dot(roots[j][0], joined(high_ref, j), preferred_element_type=F32)
        for j in range(own_rows)
    ]
    results = []
    for j in range(own_rows):
        mean_weight = product(split_value(half_steps[j]), roots[j]) / math.sqrt(total - 1)
        high, low = split_value(mean_weight[:8])
        moved = jnp.dot(
            jnp.concatenate([high, low], axis=0), joined(high_ref, j), preferred_element_type=F32
        )
        rest = jnp.dot(
            jnp.concatenate([high, low], axis=0), joined(low_ref, j), preferred_element_type=F32
        )
        center = joined(center_ref, j)[:1]
        results.append(spreads[j] + (center + (moved[:1] + moved[8:9]) + rest[:1]))
    for j in range(0, own_rows, 2):
        for part in range(4):
            both = [
                results[k][:, part * LANES : (part + 1) * LANES].reshape(devices, members, LANES)
                for k in (j, j + 1)
            ]
            out_ref[:, pl.ds((part * own_rows + j) * members, pair), :] = jnp.concatenate(
                both, axis=1
            ).astype(BF16)


def unpack_kernel(sizes, got_ref, out_ref, rows_ref, copied):
    rows, members, devices = sizes
    own_rows = rows // devices
    band = lax.axis_index("lat")
    matrix = parts_matrix(from_parts=True)
    share = devices // 2
    copies = []
    for start in range(0, devices, share):
        parts = jnp.concatenate(
            [
                got_ref[
                    start : start + share,
                    part * own_rows * members : (part + 1) * own_rows * members,
                ].reshape(share * own_rows * members, LANES)
                for part in range(4)
            ],
            axis=1,
        )
        joined = jnp.dot(parts, matrix, preferred_element_type=F32)
        for k in range(share * own_rows):
            row = start * own_rows + k
            flipped = (start + k // own_rows) * own_rows + own_rows - 1 - k % own_rows
            row = jnp.where(band == 0, row, flipped)
            values = joined[k * members : (k + 1) * members]
            for field in range(2):
                for half in range(2):
                    first = (2 * field + half) * LANES
                    rows_ref[row, pl.ds(2 * half + field, members, stride=4), :] = values[
                        :, first : first + LANES
                    ]
        part_rows = pl.ds(start * own_rows, share * own_rows)
        copies.append(
            pltpu.make_async_copy(
                rows_ref.at[part_rows], out_ref.at[part_rows], copied.at[start // share]
            )
        )
        copies[-1].start()
    for copy in copies:
        copy.wait()


def per_device_pair(background, wind_east, wind_north, obs_index, obs_value, obs_scale):
    rows, members, fields, width = background.shape
    devices = lax.axis_size("mem")
    bands = lax.axis_size("lat")
    own_rows = rows // devices
    total = members * devices
    sizes = (rows, members, devices)
    vmem = pl.BlockSpec(memory_space=pltpu.VMEM)
    params = pltpu.CompilerParams(vmem_limit_bytes=40 * 1024 * 1024)
    whole = pltpu.CompilerParams(vmem_limit_bytes=127 * 512 * 1024)

    def cost(microseconds):
        return pl.CostEstimate(
            flops=0, bytes_accessed=int(microseconds * 3_000_000), transcendentals=0
        )

    grouped = members * fields * 2
    own = background.reshape(rows, members, fields, 2, LANES)
    own = own.transpose(0, 1, 3, 2, 4).reshape(rows, grouped, LANES)

    wind_halo = -(-HALO // CHUNK) * CHUNK
    hbm = pl.BlockSpec(memory_space=pltpu.HBM)
    dma = pltpu.SemaphoreType.DMA
    observations = [
        array.reshape(own_rows, NOBS) for array in (obs_index, obs_value, obs_scale)
    ]
    edge_rows = pltpu.VMEM((HALO, grouped, LANES), F32)
    sent, told = pl.pallas_call(
        functools.partial(tell_kernel, sizes),
        out_shape=(
            jax.ShapeDtypeStruct((HALO + 4 * wind_halo // grouped, grouped, LANES), jnp.int16),
            jax.ShapeDtypeStruct((bands * devices, 4, LANES), jnp.int32),
        ),
        in_specs=[hbm] * 6,
        out_specs=(vmem, vmem),
        scratch_shapes=[
            edge_rows,
            pltpu.VMEM((2, rows, width), BF16),
            pltpu.VMEM((own_rows, LANES), jnp.int32),
            pltpu.VMEM((2, own_rows, LANES), F32),
            dma((6,)),
        ],
        compiler_params=whole,
        cost_estimate=cost(1),
        name="tell",
    )(own, wind_east, wind_north, *observations)
    halo = lax.ppermute(sent, "lat", [(0, 1), (1, 0)])
    table = lax.all_to_all(told, ("lat", "mem"), split_axis=0, concat_axis=0, tiled=True)
    per_target = (4 * own_rows + 2) * members
    wind_rows = pltpu.VMEM((8, rows + wind_halo, members, LANES), F32)
    field_rows = pltpu.VMEM((4, PAD + rows + wind_halo, members, LANES), F32)
    coded, edges = pl.pallas_call(
        functools.partial(forecast_kernel, sizes),
        out_shape=(
            jax.ShapeDtypeStruct((devices, 4 * own_rows * members, LANES), jnp.int16),
            jax.ShapeDtypeStruct((devices, 8, members, LANES), F32),
        ),
        in_specs=[vmem] * 4,
        out_specs=(vmem, vmem),
        scratch_shapes=[edge_rows, wind_rows] + [field_rows] * 4,
        compiler_params=params,
        cost_estimate=cost(12),
        name="forecast",
    )(own, halo, wind_east, wind_north)
    packed = pl.pallas_call(
        functools.partial(observe_kernel, sizes),
        out_shape=jax.ShapeDtypeStruct((devices, per_target, LANES), jnp.int16),
        in_specs=[vmem] * 3,
        out_specs=vmem,
        compiler_params=params,
        cost_estimate=cost(1),
        name="observe",
    )(edges, coded, table)
    got = lax.all_to_all(packed, "mem", split_axis=0, concat_axis=0, tiled=True)
    iterate = pltpu.VMEM((own_rows, total, total), BF16)
    back = pl.pallas_call(
        functools.partial(analysis_kernel, sizes),
        out_shape=jax.ShapeDtypeStruct((devices, 4 * own_rows * members, LANES), BF16),
        in_specs=[vmem] * 5,
        out_specs=vmem,
        scratch_shapes=[
            pltpu.VMEM((4 * own_rows, total, LANES), F32),
            pltpu.VMEM((4 * own_rows, 8, LANES), F32),
            pltpu.VMEM((4 * own_rows, total, LANES), BF16),
            pltpu.VMEM((4 * own_rows, total, LANES), BF16),
        ]
        + [iterate] * 4,
        compiler_params=params,
        cost_estimate=cost(12),
        name="analysis",
    )(got, table, *observations)
    returned = lax.all_to_all(back, "mem", split_axis=0, concat_axis=0, tiled=True)
    result = pl.pallas_call(
        functools.partial(unpack_kernel, sizes),
        out_shape=jax.ShapeDtypeStruct((rows, grouped, LANES), F32),
        in_specs=[vmem],
        out_specs=hbm,
        scratch_shapes=[pltpu.VMEM((rows, grouped, LANES), F32), dma((2,))],
        compiler_params=params,
        cost_estimate=cost(2),
        name="unpack",
    )(returned)
    result = result.reshape(rows, members, 2, fields, LANES).transpose(0, 1, 3, 2, 4)
    return result.reshape(rows, members, fields, width)


def per_device(background, wind_east, wind_north, obs_index, obs_value, obs_scale):
    rows, members, fields, width = background.shape
    devices = lax.axis_size("mem")
    fits = (
        lax.axis_size("lat") == 2
        and members == 8
        and members * devices == LANES
        and fields == 2
        and width == 2 * LANES == PW
        and obs_index.shape[2:] == (1, LANES)
        and rows % (4 * CHUNK) == 0
        and 4 * STEPS % (rows // devices) == 0
        and (rows // devices) % 2 == 0
        and rows >= 8 * STEPS
    )
    run = per_device_pair if fits else per_device_any
    return run(background, wind_east, wind_north, obs_index, obs_value, obs_scale)


def solution(mesh):
    in_specs = (
        P("lat", "mem", None, None),
        P("lat", None),
        P("lat", None),
        P("lat", "mem", None, None),
        P("lat", "mem", None, None),
        P("lat", "mem", None, None),
    )
    out_specs = P("lat", "mem", None, None)
    return jax.shard_map(
        per_device, mesh=mesh, in_specs=in_specs, out_specs=out_specs, check_vma=False
    )
```

```python
import functools
import math

import jax
import jax.numpy as jnp
from jax import lax
from jax.experimental import pallas as pl
from jax.experimental.pallas import tpu as pltpu
from jax.sharding import PartitionSpec as P

PW = 256
NOBS = 128
STEPS = 4
ITERS = 12
LANES = 128
HALO = 4 * STEPS + 1
CHUNK = 8

HIGHEST = lax.Precision.HIGHEST
F32 = jnp.float32
BF16 = jnp.bfloat16


def padded_2(block, sides, width, periodic):
    for axis, dim in sides:
        count = lax.axis_size(axis)
        forward = [(i, i + 1) for i in range(count - 1)]
        if periodic:
            forward.append((count - 1, 0))
        backward = [(target, source) for source, target in forward]
        low = lax.ppermute(
            lax.slice_in_dim(block, block.shape[dim] - width, None, axis=dim), axis, forward
        )
        high = lax.ppermute(lax.slice_in_dim(block, 0, width, axis=dim), axis, backward)
        block = jnp.concatenate([low, block, high], axis=dim)
    return block


def tendency(padded, circumpolar_wind_speed, poleward_wind_speed):
    center_rows = padded[1:-1]
    along_diff = jnp.roll(center_rows, -1, axis=-1) - jnp.roll(center_rows, 1, axis=-1)
    across_diff = padded[2:] - padded[:-2]
    return -0.5 * (circumpolar_wind_speed * along_diff + poleward_wind_speed * across_diff)


def make_blocks(model_variables, index_rows, value_rows, scale_rows):
    row_count, members, flat_width = model_variables.shape
    patch_count = index_rows.shape[1]
    obs_count = index_rows.shape[2]
    fields = flat_width // (patch_count * PW)
    patch_values = model_variables.reshape(row_count, members, fields, patch_count, PW)
    value_ids = lax.broadcasted_iota(jnp.int32, (fields * PW, 1), 0)
    selector = (value_ids[None, None] == index_rows[:, :, None, :]).astype(jnp.float32)
    selector = selector.reshape(row_count, patch_count, fields, PW, obs_count)
    picked = jnp.einsum("akfpt,apftj->akpj", patch_values, selector, precision=HIGHEST)
    average = jnp.mean(picked, axis=1)
    spread = (picked - average[:, None]) * scale_rows[:, None] / math.sqrt(members - 1)
    innovation = (value_rows - average) * scale_rows
    return jnp.concatenate([spread, innovation[:, None]], axis=1).astype(jnp.bfloat16)


def edge_pair(extended):
    return jnp.stack([extended[-1], extended[0]])


def rows_beside(local_rows, extended, banded):
    position = lax.axis_index("mem")
    last_index = lax.axis_size("mem") - 1
    upper_rim = jnp.where(position == 0, banded[0], extended[0])
    lower_rim = jnp.where(position == last_index, banded[3], extended[-1])
    upper_adjacent = jnp.concatenate([upper_rim[None], local_rows[:-1]], axis=0)
    bottom_adjacent = jnp.concatenate([local_rows[1:], lower_rim[None]], axis=0)
    return (upper_adjacent, bottom_adjacent)


def per_device_any(background, wind_east, wind_north, obs_index, obs_value, obs_scale):
    current = background
    stacked_winds = jnp.stack([wind_east, wind_north])
    wide_winds = padded_2(stacked_winds, (("lat", 1),), 3, False).astype(jnp.float32)
    east_wide = wide_winds[0][:, None, None, :]
    north_wide = wide_winds[1][:, None, None, :]
    span = east_wide.shape[0]
    for step_index in range(STEPS):
        extended = padded_2(current, (("lat", 0),), 4, False)
        slope_one = tendency(extended, east_wide, north_wide)
        slope_two = tendency(
            extended[1:-1] + 0.5 * slope_one, east_wide[1 : span - 1], north_wide[1 : span - 1]
        )
        slope_three = tendency(
            extended[2:-2] + 0.5 * slope_two, east_wide[2 : span - 2], north_wide[2 : span - 2]
        )
        slope_four = tendency(
            extended[3:-3] + slope_three, east_wide[3 : span - 3], north_wide[3 : span - 3]
        )
        current = (
            extended[4:-4]
            + (slope_one[3:-3] + 2.0 * slope_two[2:-2] + 2.0 * slope_three[1:-1] + slope_four) / 6.0
        )
    points = lax.all_to_all(current, "mem", split_axis=0, concat_axis=1, tiled=True)
    row_count, members, fields, width = points.shape
    patch_count = obs_index.shape[2]
    model_variables = points.reshape(row_count, members, fields * width)
    index_rows = obs_index.reshape(row_count, patch_count, NOBS)
    value_rows = obs_value.reshape(row_count, patch_count, NOBS)
    scale_rows = obs_scale.reshape(row_count, patch_count, NOBS)
    own_block = make_blocks(model_variables, index_rows, value_rows, scale_rows)
    extended = padded_2(own_block, (("mem", 0),), 1, True)
    banded = padded_2(edge_pair(extended), (("lat", 0),), 1, False)
    upper_adjacent, bottom_adjacent = rows_beside(own_block, extended, banded)
    gram_sum = jnp.zeros((row_count, patch_count, members + 1, members + 1), jnp.float32)
    for neighbor_block in (
        own_block,
        jnp.roll(own_block, -1, axis=2),
        jnp.roll(own_block, 1, axis=2),
        upper_adjacent,
        bottom_adjacent,
    ):
        gram_sum = gram_sum + jnp.einsum(
            "akpj,alpj->apkl", neighbor_block, neighbor_block, preferred_element_type=jnp.float32
        )
    identity = jnp.eye(members, dtype=jnp.float32)
    system = identity + gram_sum[:, :, :members, :members]
    coupling = gram_sum[:, :, :members, members]
    trace_sum = jnp.trace(system, axis1=2, axis2=3)
    scaled = system / trace_sum[:, :, None, None]

    def newton(turn_index, carry):
        upper_iter, lower_iter = carry
        factor = 1.5 * identity - 0.5 * jnp.einsum(
            "apij,apjk->apik", lower_iter, upper_iter, precision=HIGHEST
        )
        return (
            jnp.einsum("apij,apjk->apik", upper_iter, factor, precision=HIGHEST),
            jnp.einsum("apij,apjk->apik", factor, lower_iter, precision=HIGHEST),
        )

    start_lower = jnp.broadcast_to(identity, scaled.shape)
    upper_iter, lower_iter = lax.fori_loop(0, ITERS, newton, (scaled, start_lower))
    inv_root = lower_iter / jnp.sqrt(trace_sum)[:, :, None, None]
    half_step = jnp.einsum("apkl,apl->apk", inv_root, coupling, precision=HIGHEST)
    mean_weight = jnp.einsum("apkl,apl->apk", inv_root, half_step, precision=HIGHEST) / math.sqrt(
        members - 1
    )
    weights = mean_weight[:, :, :, None] + inv_root
    patch_values = points.reshape(row_count, members, fields, patch_count, PW)
    center = jnp.mean(patch_values, axis=1)
    result = center[:, None] + jnp.einsum(
        "akfpt,apki->aifpt", patch_values - center[:, None], weights, precision=HIGHEST
    )
    analysis = result.reshape(row_count, members, fields, width)
    return lax.all_to_all(analysis, "mem", split_axis=1, concat_axis=0, tiled=True)


PAD = 8
TURNS = 2
FINEST = 0.05
LARGEST = 16.0 * sum(1.8**power / math.factorial(power) for power in range(5)) ** STEPS
STATE_LEVELS = 2047.0
WIND_LEVELS = 32767.0
VALUE_LEVELS = 8191.0
SCALE_LEVELS = 4095.0
STEEPNESS = 32766.0 / math.log(1.0 + LARGEST / FINEST)


def take_lanes(values, lanes):
    return jnp.take_along_axis(values, lanes, axis=1, mode="promise_in_bounds")


def pick_lanes(states, index):
    field = jnp.right_shift(index, 8)
    lanes = jnp.bitwise_and(jnp.right_shift(index, 1), LANES - 2) + field
    is_odd = jnp.bitwise_and(index, 1) == 1
    is_late = jnp.bitwise_and(index, 2) == 2
    picks = [take_lanes(state, lanes) for state in states]
    return jnp.where(
        is_odd, jnp.where(is_late, picks[3], picks[1]), jnp.where(is_late, picks[2], picks[0])
    )


def group_place(sizes, band, group):
    return jnp.where(band == 0, group, sizes[2] - 1 - group)


def beside_rows(table_ref, sizes, band, group, is_after):
    devices = sizes[2]
    near = group + 1 if is_after else jnp.maximum(group - 1, 0)
    over = near == devices
    place = jnp.where(over, jnp.where(band == 0, 0, devices - 1), group_place(sizes, band, near))
    near_band = jnp.where(over, 1 - band, band)
    last = jnp.where(band == 0, 0, 1) if is_after else jnp.where(band == 0, 1, 0)
    return near_band * devices + place, last


def beside_index(table_ref, sizes, band, group, is_after):
    place, last = beside_rows(table_ref, sizes, band, group, is_after)
    return jnp.bitwise_and(table_ref[place, pl.ds(last, 1), :], 65535)


def beside_observation(table_ref, sizes, band, group, is_after):
    place, last = beside_rows(table_ref, sizes, band, group, is_after)
    value = jnp.right_shift(table_ref[place, pl.ds(last, 1), :], 16)
    scales = table_ref[place, 2:3, :]
    scale = jnp.where(last == 1, jnp.right_shift(scales, 16), jnp.bitwise_and(scales, 65535))
    return value.astype(F32) * F32(1.0 / VALUE_LEVELS), scale.astype(F32) * F32(1.0 / SCALE_LEVELS)


def parts_matrix(from_parts=False):
    shape = (4 * LANES, 4 * LANES)
    rows = lax.broadcasted_iota(jnp.int32, shape, 0)
    columns = lax.broadcasted_iota(jnp.int32, shape, 1)
    column, plain = (rows, columns) if from_parts else (columns, rows)
    lane = jnp.bitwise_and(column, LANES - 1)
    wanted = (
        jnp.bitwise_and(lane, 1) * (2 * LANES)
        + jnp.right_shift(lane, 1) * 4
        + jnp.right_shift(column, 7)
    )
    return jnp.where(plain == wanted, F32(1.0), F32(0.0)).astype(BF16)


def stage_states(load, row_of, count, members, matrix, q_ref, start):
    left = jnp.concatenate(
        [
            jnp.concatenate([load(row_of(k), 2 * half + field) for k in range(count)], axis=0)
            for field in range(2)
            for half in range(2)
        ],
        axis=1,
    )
    first = left.astype(BF16)
    left = left - first.astype(F32)
    second = left.astype(BF16)
    third = (left - second.astype(F32)).astype(BF16)
    size = count * members
    split = jnp.dot(
        jnp.concatenate([first, second, third], axis=0), matrix, preferred_element_type=F32
    )
    split = split[:size] + (split[size : 2 * size] + split[2 * size :])
    for part in range(4):
        values = split[:, part * LANES : (part + 1) * LANES]
        q_ref[part, pl.ds(start, count)] = values.reshape(count, members, LANES)


def stage_winds(east, north, north_sign, matrix, w_ref, row_of):
    count, members = east.shape[0], w_ref.shape[2]
    for side, (wind, sign) in enumerate(((east, F32(-0.25)), (north, north_sign))):
        both = jnp.concatenate([wind, wind], axis=1)
        split = jnp.dot(both, matrix, preferred_element_type=F32) * sign
        for k in range(count):
            for part in range(4):
                lanes = split[k : k + 1, part * LANES : (part + 1) * LANES]
                w_ref[4 * side + part, row_of(k)] = jnp.broadcast_to(lanes, (members, LANES))


def rk_passes(q_ref, stage_refs, w_ref, count, block):
    a_ref, b_ref, c_ref = stage_refs

    def finish_one(part, at, half, here):
        a_ref[part, at] = here + half

    def finish_two(part, at, half, here):
        b_ref[part, at] = q_ref[part, at] + half

    def finish_three(part, at, half, here):
        moved = half + half
        c_ref[part, at] = q_ref[part, at] + moved
        a_ref[part, at] = (a_ref[part, at] + moved) + (here + here)

    def finish_four(part, at, half, here):
        q_ref[part, at] = (a_ref[part, at] + half) * F32(1.0 / 3.0)

    for stage, finish in (
        (q_ref, finish_one),
        (a_ref, finish_two),
        (b_ref, finish_three),
        (c_ref, finish_four),
    ):

        def turn(index, _):
            base = PAD + index * block

            def load(k):
                return [stage[part, base + k - 1] for part in range(4)]

            before, here = load(0), load(1)
            for k in range(1, block + 1):
                after = load(k + 1)
                place = index * block + k - 1
                along = (
                    here[1] - pltpu.roll(here[3], 2, 1),
                    here[2] - here[0],
                    here[3] - here[1],
                    pltpu.roll(here[0], LANES - 2, 1) - here[2],
                )
                for part in range(4):
                    across = after[part] - before[part]
                    half = w_ref[part, place] * along[part] + w_ref[4 + part, place] * across
                    finish(part, base + k - 1, half, here[part])
                before, here = here, after
            return 0

        turns = -(-count // block)
        if turns == 1:
            turn(0, 0)
        else:
            lax.fori_loop(0, turns, turn, 0)


def encode(value):
    level = jnp.round(jnp.log(1.0 + jnp.abs(value) * F32(1.0 / FINEST)) * F32(STEEPNESS))
    return jnp.where(value < 0.0, -level, level)


def decode(code):
    size = (jnp.exp(jnp.abs(code) * F32(1.0 / STEEPNESS)) - 1.0) * F32(FINEST)
    return jnp.where(code < 0.0, -size, size)


def pack_pair(low, high):
    return jnp.concatenate([low, high], axis=0).astype(jnp.int32).astype(jnp.int16)


def tell_kernel(
    sizes,
    own_ref,
    east_ref,
    north_ref,
    index_ref,
    value_ref,
    scale_ref,
    sent_ref,
    told_ref,
    edge_ref,
    winds_ref,
    ints_ref,
    floats_ref,
    copied,
):
    rows, members, devices = sizes
    own_rows = rows // devices
    band = lax.axis_index("lat")
    wind_halo = -(-HALO // CHUNK) * CHUNK
    begin = jnp.where(band == 0, rows - HALO, 0)
    pairs = (
        (own_ref.at[pl.ds(begin, HALO)], edge_ref),
        (east_ref, winds_ref.at[0]),
        (north_ref, winds_ref.at[1]),
        (index_ref, ints_ref),
        (value_ref, floats_ref.at[0]),
        (scale_ref, floats_ref.at[1]),
    )
    copies = [
        pltpu.make_async_copy(source, target, copied.at[turn])
        for turn, (source, target) in enumerate(pairs)
    ]
    for copy in copies:
        copy.start()
    for copy in copies[1:]:
        copy.wait()
    winds = []
    for side in range(2):
        wind = winds_ref[side].astype(F32) * F32(WIND_LEVELS)
        wind = jnp.where(band == 0, wind[rows - wind_halo :], wind[:wind_halo])
        winds += [wind[:, :LANES], wind[:, LANES:]]
    winds = jnp.round(jnp.concatenate(winds, axis=0)).astype(jnp.int32).astype(jnp.int16)
    sent_ref[HALO:] = winds.reshape(-1, sent_ref.shape[1], LANES)
    values = jnp.round(floats_ref[0] * F32(VALUE_LEVELS)).astype(jnp.int32)
    scales = jnp.round(floats_ref[1] * F32(SCALE_LEVELS)).astype(jnp.int32)
    pairs = ints_ref[...] + values * 65536
    ends = [row[end : end + 1] for row in (pairs, scales) for end in (0, own_rows - 1)]
    told = jnp.concatenate(ends[:2] + [ends[2] + ends[3] * 65536, jnp.zeros_like(ends[0])], axis=0)
    told_ref[...] = jnp.broadcast_to(told[None], told_ref.shape)
    copies[0].wait()
    edge = jnp.round(edge_ref[...] * F32(STATE_LEVELS))
    sent_ref[:HALO] = edge.astype(jnp.int32).astype(jnp.int16)


def forecast_kernel(
    sizes,
    own_ref,
    halo_ref,
    east_ref,
    north_ref,
    out_ref,
    edges_ref,
    edge_ref,
    w_ref,
    q_ref,
    *stage_refs,
):
    rows, members, devices = sizes
    own_rows = rows // devices
    band = lax.axis_index("lat")
    matrix = parts_matrix()
    north_sign = jnp.where(band == 0, F32(-0.25), F32(0.25))
    wind_halo = -(-HALO // CHUNK) * CHUNK
    pair = 2 * members

    zero_rows = jnp.zeros((4, PAD, members, LANES), F32)
    for ref in (q_ref, *stage_refs):
        ref[:, :PAD] = zero_rows
    stage_winds(
        east_ref[...],
        north_ref[...],
        north_sign,
        matrix,
        w_ref,
        lambda k: jnp.where(band == 0, k, rows - 1 - k),
    )
    edge_ref[...] = halo_ref[:HALO].astype(jnp.int32).astype(F32) * F32(1.0 / STATE_LEVELS)
    halo_winds = halo_ref[HALO:].astype(jnp.int32).astype(F32).reshape(4 * wind_halo, LANES)
    halo_winds = (halo_winds * F32(1.0 / WIND_LEVELS)).astype(BF16)
    halo_winds = [halo_winds[k * wind_halo : (k + 1) * wind_halo] for k in range(4)]
    stage_winds(
        jnp.concatenate(halo_winds[:2], axis=1),
        jnp.concatenate(halo_winds[2:], axis=1),
        north_sign,
        matrix,
        w_ref,
        lambda k: rows + jnp.where(band == 0, k, wind_halo - 1 - k),
    )

    def row_of(k):
        row = min(k, HALO - 1)
        return jnp.where(band == 0, row, HALO - 1 - row)

    def load(row, lane):
        return edge_ref[row, pl.ds(lane, members, stride=4), :]

    stage_states(load, row_of, wind_halo, members, matrix, q_ref, PAD + rows)

    def load_own(row, lane):
        return own_ref[row, pl.ds(lane, members, stride=4), :]

    def own_row(k):
        return jnp.where(band == 0, k, rows - 1 - k)

    stage_states(load_own, own_row, rows, members, matrix, q_ref, PAD)

    for step in range(STEPS):
        count = rows + HALO - 1 - 4 * step
        rk_passes(q_ref, stage_refs, w_ref, count, -(-count // TURNS))

    def state(row):
        return [q_ref[part, PAD + row] for part in range(4)]

    def emit(group, _):
        first = group * own_rows
        place = group_place(sizes, band, group)
        for j in range(0, own_rows, 2):
            low, high = state(first + j), state(first + j + 1)
            for part in range(4):
                start = (part * own_rows + j) * members
                out_ref[place, pl.ds(start, pair), :] = pack_pair(
                    encode(low[part]), encode(high[part])
                )
        for side, row in enumerate((jnp.maximum(first - 1, 0), first + own_rows)):
            for part, values in enumerate(state(row)):
                edges_ref[place, 4 * side + part] = values
        return 0

    lax.fori_loop(0, devices, emit, 0, unroll=4)


def observe_kernel(sizes, edges_ref, coded_ref, table_ref, out_ref):
    rows, members, devices = sizes
    band = lax.axis_index("lat")
    coded_rows = coded_ref.shape[1]
    out_ref[:, :coded_rows] = coded_ref[...]

    def emit(group, _):
        place = group_place(sizes, band, group)
        values = []
        for side in range(2):
            index = beside_index(table_ref, sizes, band, group, side == 1)
            index = jnp.broadcast_to(index, (members, LANES))
            states = [edges_ref[place, 4 * side + part] for part in range(4)]
            values.append(encode(pick_lanes(states, index)))
        out_ref[place, pl.ds(coded_rows, 2 * members), :] = pack_pair(*values)
        return 0

    lax.fori_loop(0, devices, emit, 0, unroll=4)


def split_value(value):
    high = value.astype(BF16)
    return high, (value - high.astype(F32)).astype(BF16)


def product(left, right):
    (left_high, left_low), (right_high, right_low) = left, right
    size = right_high.shape[1]
    both = jnp.dot(
        jnp.concatenate([left_high, left_low], axis=1),
        jnp.concatenate(
            [
                jnp.concatenate([right_high, right_low], axis=1),
                jnp.concatenate([right_high, jnp.zeros_like(right_low)], axis=1),
            ],
            axis=0,
        ),
        preferred_element_type=F32,
    )
    return both[:, :size] + both[:, size:]


def analysis_kernel(
    sizes,
    got_ref,
    table_ref,
    index_ref,
    value_ref,
    scale_ref,
    out_ref,
    states_ref,
    center_ref,
    high_ref,
    low_ref,
    *iterates,
):
    rows, members, devices = sizes
    own_rows = rows // devices
    total = members * devices
    band = lax.axis_index("lat")
    group = group_place(sizes, band, lax.axis_index("mem"))
    pair = 2 * members
    beside_start = 4 * own_rows * members

    def pair_at(start):
        both = decode(got_ref[:, pl.ds(start, pair), :].astype(jnp.int32).astype(F32))
        both = both.reshape(devices, 2, members, LANES)
        return both[:, 0].reshape(total, LANES), both[:, 1].reshape(total, LANES)

    def info(ref, j):
        return ref[pl.ds(jnp.where(band == 0, j, own_rows - 1 - j), 1), :]

    picked_rows = [None] * (own_rows + 2)
    picked_rows[0], picked_rows[own_rows + 1] = pair_at(beside_start)
    for j in range(0, own_rows, 2):
        parts = [pair_at((part * own_rows + j) * members) for part in range(4)]
        for k in range(2):
            for part in range(4):
                states_ref[4 * (j + k) + part] = parts[part][k]
            index = jnp.broadcast_to(info(index_ref, j + k), (total, LANES)).astype(jnp.int32)
            picked_rows[j + k + 1] = pick_lanes([part[k] for part in parts], index)

    grams = []
    couplings = []
    for j in range(-1, own_rows + 1):
        if 0 <= j < own_rows:
            value, scale = info(value_ref, j), info(scale_ref, j)
        else:
            value, scale = beside_observation(table_ref, sizes, band, group, j == own_rows)
        if j == -1:
            scale = jnp.where(group == 0, 0.0, scale)
        picked = picked_rows[j + 1]
        average = jnp.mean(picked, axis=0, keepdims=True)
        spread = ((picked - average) * scale / math.sqrt(total - 1)).astype(BF16)
        innovation = jnp.broadcast_to((value - average) * scale, (16, LANES)).astype(BF16)
        contract = (((1,), (1,)), ((), ()))
        grams.append(lax.dot_general(spread, spread, contract, preferred_element_type=F32))
        couplings.append(
            lax.dot_general(innovation, spread, contract, preferred_element_type=F32)
        )

    row_ids = lax.broadcasted_iota(jnp.int32, (total, total), 0)
    column_ids = lax.broadcasted_iota(jnp.int32, (total, total), 1)
    diagonal = row_ids == column_ids
    identity = jnp.where(diagonal, F32(1.0), F32(0.0))

    def put(refs, j, value):
        refs[0][j], refs[1][j] = split_value(value)

    upper_refs, lower_refs = iterates[:2], iterates[2:]
    traces = []
    for j in range(own_rows):
        system = identity + 3.0 * grams[j + 1] + grams[j] + grams[j + 2]
        trace = jnp.sum(
            jnp.sum(jnp.where(diagonal, system, 0.0), axis=0, keepdims=True),
            axis=1,
            keepdims=True,
        )
        traces.append(trace)
        scaled = system / trace
        factor = 1.5 * identity - 0.5 * scaled
        put(upper_refs, j, product(split_value(scaled), split_value(factor)))
        put(lower_refs, j, factor)

    def factor_of(j):
        lower, upper = lower_refs, upper_refs
        lower, upper = (lower[0][j], lower[1][j]), (upper[0][j], upper[1][j])
        return lower, upper, split_value(1.5 * identity - 0.5 * product(lower, upper))

    per_turn = -(-4 * own_rows // (ITERS - 2))

    def newton(turn, _):
        for k in range(per_turn):
            entry = jnp.minimum(turn * per_turn + k, 4 * own_rows - 1)
            state = states_ref[entry]
            center = jnp.mean(state, axis=0, keepdims=True)
            center_ref[entry] = jnp.broadcast_to(center, (8, LANES))
            high_ref[entry], low_ref[entry] = split_value(state - center)
        parts = [factor_of(j) for j in range(own_rows)]
        for j in range(own_rows):
            lower, upper, factor = parts[j]
            put(upper_refs, j, product(upper, factor))
            put(lower_refs, j, product(factor, lower))
        return 0

    lax.fori_loop(0, ITERS - 2, newton, 0, unroll=5)

    def joined(ref, j):
        return jnp.concatenate([ref[4 * j + part] for part in range(4)], axis=1)

    parts = [factor_of(j) for j in range(own_rows)]
    roots = [
        split_value(product(parts[j][2], parts[j][0]) / jnp.sqrt(traces[j]))
        for j in range(own_rows)
    ]
    half_steps = []
    for j in range(own_rows):
        coupling = 3.0 * couplings[j + 1] + couplings[j] + couplings[j + 2]
        half_steps.append(product(split_value(coupling), roots[j]))
    spreads = [
        jnp.dot(roots[j][0], joined(high_ref, j), preferred_element_type=F32)
        for j in range(own_rows)
    ]
    results = []
    for j in range(own_rows):
        mean_weight = product(split_value(half_steps[j]), roots[j]) / math.sqrt(total - 1)
        high, low = split_value(mean_weight[:8])
        moved = jnp.dot(
            jnp.concatenate([high, low], axis=0), joined(high_ref, j), preferred_element_type=F32
        )
        rest = jnp.dot(
            jnp.concatenate([high, low], axis=0), joined(low_ref, j), preferred_element_type=F32
        )
        center = joined(center_ref, j)[:1]
        results.append(spreads[j] + (center + (moved[:1] + moved[8:9]) + rest[:1]))
    for j in range(0, own_rows, 2):
        for part in range(4):
            both = [
                results[k][:, part * LANES : (part + 1) * LANES].reshape(devices, members, LANES)
                for k in (j, j + 1)
            ]
            out_ref[:, pl.ds((part * own_rows + j) * members, pair), :] = jnp.concatenate(
                both, axis=1
            ).astype(BF16)


def unpack_kernel(sizes, got_ref, out_ref, rows_ref, copied):
    rows, members, devices = sizes
    own_rows = rows // devices
    band = lax.axis_index("lat")
    matrix = parts_matrix(from_parts=True)
    share = devices // 2
    copies = []
    for start in range(0, devices, share):
        parts = jnp.concatenate(
            [
                got_ref[
                    start : start + share,
                    part * own_rows * members : (part + 1) * own_rows * members,
                ].reshape(share * own_rows * members, LANES)
                for part in range(4)
            ],
            axis=1,
        )
        joined = jnp.dot(parts, matrix, preferred_element_type=F32)
        for k in range(share * own_rows):
            row = start * own_rows + k
            flipped = (start + k // own_rows) * own_rows + own_rows - 1 - k % own_rows
            row = jnp.where(band == 0, row, flipped)
            values = joined[k * members : (k + 1) * members]
            for field in range(2):
                for half in range(2):
                    first = (2 * field + half) * LANES
                    rows_ref[row, pl.ds(2 * half + field, members, stride=4), :] = values[
                        :, first : first + LANES
                    ]
        part_rows = pl.ds(start * own_rows, share * own_rows)
        copies.append(
            pltpu.make_async_copy(
                rows_ref.at[part_rows], out_ref.at[part_rows], copied.at[start // share]
            )
        )
        copies[-1].start()
    for copy in copies:
        copy.wait()


def per_device_pair(background, wind_east, wind_north, obs_index, obs_value, obs_scale):
    rows, members, fields, width = background.shape
    devices = lax.axis_size("mem")
    bands = lax.axis_size("lat")
    own_rows = rows // devices
    total = members * devices
    sizes = (rows, members, devices)
    vmem = pl.BlockSpec(memory_space=pltpu.VMEM)
    params = pltpu.CompilerParams(vmem_limit_bytes=40 * 1024 * 1024)
    whole = pltpu.CompilerParams(vmem_limit_bytes=127 * 512 * 1024)

    def cost(microseconds):
        return pl.CostEstimate(
            flops=0, bytes_accessed=int(microseconds * 3_000_000), transcendentals=0
        )

    grouped = members * fields * 2
    own = background.reshape(rows, members, fields, 2, LANES)
    own = own.transpose(0, 1, 3, 2, 4).reshape(rows, grouped, LANES)

    wind_halo = -(-HALO // CHUNK) * CHUNK
    hbm = pl.BlockSpec(memory_space=pltpu.HBM)
    dma = pltpu.SemaphoreType.DMA
    observations = [
        array.reshape(own_rows, NOBS) for array in (obs_index, obs_value, obs_scale)
    ]
    edge_rows = pltpu.VMEM((HALO, grouped, LANES), F32)
    sent, told = pl.pallas_call(
        functools.partial(tell_kernel, sizes),
        out_shape=(
            jax.ShapeDtypeStruct((HALO + 4 * wind_halo // grouped, grouped, LANES), jnp.int16),
            jax.ShapeDtypeStruct((bands * devices, 4, LANES), jnp.int32),
        ),
        in_specs=[hbm] * 6,
        out_specs=(vmem, vmem),
        scratch_shapes=[
            edge_rows,
            pltpu.VMEM((2, rows, width), BF16),
            pltpu.VMEM((own_rows, LANES), jnp.int32),
            pltpu.VMEM((2, own_rows, LANES), F32),
            dma((6,)),
        ],
        compiler_params=whole,
        cost_estimate=cost(1),
        name="tell",
    )(own, wind_east, wind_north, *observations)
    halo = lax.ppermute(sent, "lat", [(0, 1), (1, 0)])
    table = lax.all_to_all(told, ("lat", "mem"), split_axis=0, concat_axis=0, tiled=True)
    per_target = (4 * own_rows + 2) * members
    wind_rows = pltpu.VMEM((8, rows + wind_halo, members, LANES), F32)
    field_rows = pltpu.VMEM((4, PAD + rows + wind_halo, members, LANES), F32)
    coded, edges = pl.pallas_call(
        functools.partial(forecast_kernel, sizes),
        out_shape=(
            jax.ShapeDtypeStruct((devices, 4 * own_rows * members, LANES), jnp.int16),
            jax.ShapeDtypeStruct((devices, 8, members, LANES), F32),
        ),
        in_specs=[vmem] * 4,
        out_specs=(vmem, vmem),
        scratch_shapes=[edge_rows, wind_rows] + [field_rows] * 4,
        compiler_params=params,
        cost_estimate=cost(12),
        name="forecast",
    )(own, halo, wind_east, wind_north)
    packed = pl.pallas_call(
        functools.partial(observe_kernel, sizes),
        out_shape=jax.ShapeDtypeStruct((devices, per_target, LANES), jnp.int16),
        in_specs=[vmem] * 3,
        out_specs=vmem,
        compiler_params=params,
        cost_estimate=cost(1),
        name="observe",
    )(edges, coded, table)
    got = lax.all_to_all(packed, "mem", split_axis=0, concat_axis=0, tiled=True)
    iterate = pltpu.VMEM((own_rows, total, total), BF16)
    back = pl.pallas_call(
        functools.partial(analysis_kernel, sizes),
        out_shape=jax.ShapeDtypeStruct((devices, 4 * own_rows * members, LANES), BF16),
        in_specs=[vmem] * 5,
        out_specs=vmem,
        scratch_shapes=[
            pltpu.VMEM((4 * own_rows, total, LANES), F32),
            pltpu.VMEM((4 * own_rows, 8, LANES), F32),
            pltpu.VMEM((4 * own_rows, total, LANES), BF16),
            pltpu.VMEM((4 * own_rows, total, LANES), BF16),
        ]
        + [iterate] * 4,
        compiler_params=params,
        cost_estimate=cost(12),
        name="analysis",
    )(got, table, *observations)
    returned = lax.all_to_all(back, "mem", split_axis=0, concat_axis=0, tiled=True)
    result = pl.pallas_call(
        functools.partial(unpack_kernel, sizes),
        out_shape=jax.ShapeDtypeStruct((rows, grouped, LANES), F32),
        in_specs=[vmem],
        out_specs=hbm,
        scratch_shapes=[pltpu.VMEM((rows, grouped, LANES), F32), dma((2,))],
        compiler_params=params,
        cost_estimate=cost(2),
        name="unpack",
    )(returned)
    result = result.reshape(rows, members, 2, fields, LANES).transpose(0, 1, 3, 2, 4)
    return result.reshape(rows, members, fields, width)


def per_device(background, wind_east, wind_north, obs_index, obs_value, obs_scale):
    rows, members, fields, width = background.shape
    devices = lax.axis_size("mem")
    fits = (
        lax.axis_size("lat") == 2
        and members == 8
        and members * devices == LANES
        and fields == 2
        and width == 2 * LANES == PW
        and obs_index.shape[2:] == (1, LANES)
        and rows % (4 * CHUNK) == 0
        and 4 * STEPS % (rows // devices) == 0
        and (rows // devices) % 2 == 0
        and rows >= 8 * STEPS
    )
    run = per_device_pair if fits else per_device_any
    return run(background, wind_east, wind_north, obs_index, obs_value, obs_scale)


def solution(mesh):
    in_specs = (
        P("lat", "mem", None, None),
        P("lat", None),
        P("lat", None),
        P("lat", "mem", None, None),
        P("lat", "mem", None, None),
        P("lat", "mem", None, None),
    )
    out_specs = P("lat", "mem", None, None)
    return jax.shard_map(
        per_device, mesh=mesh, in_specs=in_specs, out_specs=out_specs, check_vma=False
    )
```
